128 devices in a mesh: crow: 8 (over y, core), ccol: 16 (over x, z).
Axes of the slice: x: 4, y: 4, z: 4, core: 2. Of those that a mesh axis runs over, the one named last changes fastest.
Arguments:
- modes: bfloat16 [262144, 512], P(('crow', 'ccol')), may hold values from -6 to 6
- col_basis: bfloat16 [64, 262144], P(None, ('crow', 'ccol')), may hold values from -0.375 to 0.375
- row_basis: bfloat16 [64, 262144], P(None, ('crow', 'ccol')), may hold values from -0.1875 to 0.1875
- near_blocks: bfloat16 [262144, 2304], P(('crow', 'ccol')), may hold values from -0.125 to 0.125
- block_rows: int32 [16384], P(('crow', 'ccol')), may hold values from 0 to 127
- block_owner: int32 [16384, 1], P(('crow', 'ccol')), may hold values from 0 to 127; in each aligned block of 128 rows (0 to 127, 128 to 255, ...) at most 2 rows name the same one
- block_slot: int32 [16384], P(('crow', 'ccol')), may hold values from 0 to 7
- cores: bfloat16 [16384, 4096], P(('crow', 'ccol')), may hold values from -0.75 to 0.75
Outputs:
- pressure: bfloat16 [262144, 512], P(('crow', 'ccol'))
The draws below stay inside these ranges and needn't reach their ends.
Inputs may be any that keep to these rules, and one draw needn't show every extreme that they name: `block_owner`: among the blocks of one device (rows b * 128 to (b + 1) * 128 - 1), at most 2 name the same device; some device reaches 2 for some owner in every draw.
All inputs are finite; a program needn't handle non-finite values.
Results may differ from the reference program's by a relative error of at most 0.0049.
Values may be sent and summed in bfloat16 or wider, within the bound.
No kernel may reach another device: no remote copies, remote signals or barrier semaphores. Data moves between devices by JAX's collectives and lax.ppermute only.
A program may use at most 192 MiB of HBM per device.

```python
import math
import jax
import jax.numpy as jnp
import numpy as np
from jax import lax

M = 512
K = 64
CS = 256
NH = 4
CL_DEV = 8
BLK_DEV = 128
NEAR = 9
CAP = 2
NCL = 1024
NPAN = 262144
TOT_BLK = 16384
GROUP = 128
N_CCOL = 16
DEVICES = 128


def set_ends(result, stream_key, least, largest):
    index_at = [jax.random.randint(jax.random.fold_in(stream_key, axis), (), 0, length) for axis, length in enumerate(result.shape)]
    longest = result.shape.index(max(result.shape))
    next_to = index_at[:longest] + [(index_at[longest] + 1) % result.shape[longest]] + index_at[longest + 1:]
    return result.at[tuple(index_at)].set(least).at[tuple(next_to)].set(largest)


def level_of(own_key, shape, split, least, high):
    def one(dim, blocks):
        heights = jax.random.uniform(jax.random.fold_in(jax.random.fold_in(own_key, 6), dim), (blocks,), jnp.float32, least / len(split), high / len(split))
        return jnp.repeat(jnp.exp(heights), shape[dim] // blocks).reshape((-1,) + (1,) * (len(shape) - dim - 1))

    loudness = one(*split[0])
    for cut in split[1:]:
        loudness = loudness * one(*cut)
    return loudness


def deal_out(rng, own, number, rows, number_of, top, limit, lean):
    sequence = jax.random.permutation(rng, number_of)
    crowded, usual = portions_of(number_of, rows * top, limit, lean, True), portions_of(number_of, rows * top, limit, lean, False)
    places = jnp.arange(number_of)

    def named(tallies, offset_by):
        used = int((tallies > 0).sum())
        fixed = max(1, used // 4)
        moved = fixed + (places - fixed + offset_by * (used - fixed)) % max(1, number_of - fixed)
        return jnp.zeros((number_of,), jnp.int32).at[sequence[jnp.where(places < fixed, places, moved)]].set(jnp.asarray(tallies, jnp.int32))

    tallies = jnp.where(number % 4 == 0, named(crowded, number // 4), named(usual, number - number // 4 - 1))
    mixed = jax.random.permutation(jax.random.fold_in(own, 3), number_of)
    source_of, sink = mixed[0:number_of // 2 * 2:2], mixed[1:number_of // 2 * 2:2]
    room = jnp.minimum(tallies[source_of] - 1, limit - tallies[sink]) // 2
    room = jnp.where((source_of == sequence[0]) | (sink == sequence[0]) | (tallies[sink] == 0), 0, jnp.maximum(room, 0))
    moved = jax.random.randint(jax.random.fold_in(own, 4), (number_of // 2,), 0, 1 << 20) % (room + 1)
    tallies = tallies.at[source_of].add(-moved).at[sink].add(moved)
    labels = jnp.searchsorted(jnp.cumsum(tallies), jnp.arange(rows * top), side="right").astype(jnp.int32)
    grid = labels.reshape(top, rows).T
    grid = grid[jax.random.permutation(jax.random.fold_in(own, 1), rows)]
    offset_by = jax.random.randint(jax.random.fold_in(own, 2), (rows, 1), 0, top)
    return jnp.take_along_axis(grid, (jnp.arange(top)[None, :] + offset_by) % top, axis=1)


def portions_of(amount, total, bound, slope, full):
    portions = [(1 << 20) // math.isqrt(rank ** slope) + 1 for rank in range(1, amount + 1)]
    largest = bound if full else min(bound, max(-(-total // amount), total * portions[0] // sum(portions)))
    least = 1 if total - largest >= amount - 1 else 0
    holding, rest = [largest] + [least] * (amount - 1), total - largest - least * (amount - 1)
    while rest > 0:
        free = [i for i in range(1, amount) if holding[i] < largest] or [i for i in range(1, amount) if holding[i] < bound]
        pool, left = sum([portions[i] for i in free]), rest
        for i in free:
            more = min(bound - holding[i], max(1, left * portions[i] // pool), rest)
            holding[i] = holding[i] + more
            rest = rest - more
    return np.array(holding)


def bell_draw(own_key, dims, deviation, most, shards=(), held_as=jnp.bfloat16):
    result = jax.random.normal(own_key, dims, jnp.float32) * deviation
    if len(shards) > 0:
        result = level_of(own_key, dims, shards, -0.22, 0.18) * result
    return jnp.clip(result, min=-most, max=most).astype(held_as)


def setup_inputs(seed: int = 0) -> dict:
    streams_of = jax.random.split(jax.random.key(seed), 9)
    modes = bell_draw(streams_of[0], (NPAN, M), 1.0, 6.0, ((0, 128),))
    col_basis = bell_draw(streams_of[1], (K, NPAN), CS ** -0.5, 0.375, ((1, 128),))
    row_basis = bell_draw(streams_of[2], (K, NPAN), (16 * K) ** -0.5, 0.1875, ((1, 128),))
    near_blocks = bell_draw(streams_of[3], (NPAN, NEAR * CS), (NEAR * CS) ** -0.5, 0.125, ((0, 128),))
    block_rows = set_ends(jax.random.randint(streams_of[4], (TOT_BLK,), 0, GROUP), jax.random.fold_in(streams_of[4], 1), 0, GROUP - 1).astype(jnp.int32)
    block_owner_keys = jax.random.split(jax.random.fold_in(streams_of[5], 1), TOT_BLK // BLK_DEV)
    block_owner_turns = jax.random.permutation(jax.random.fold_in(streams_of[5], 3), TOT_BLK // BLK_DEV)
    block_owner = jax.vmap(lambda own, number: deal_out(jax.random.fold_in(streams_of[5], 2), own, number, BLK_DEV, DEVICES, 1, CAP, 2))(block_owner_keys, block_owner_turns).reshape((TOT_BLK, 1))
    block_slot = set_ends(jax.random.randint(streams_of[6], (TOT_BLK,), 0, CL_DEV), jax.random.fold_in(streams_of[6], 1), 0, CL_DEV - 1).astype(jnp.int32)
    cores = bell_draw(streams_of[7], (TOT_BLK, K * K), K ** -0.5, 0.75, ((0, 128),))
    return dict(modes=modes, col_basis=col_basis, row_basis=row_basis, near_blocks=near_blocks, block_rows=block_rows, block_owner=block_owner, block_slot=block_slot, cores=cores)


def reference(modes, col_basis, row_basis, near_blocks, block_rows, block_owner, block_slot, cores):
    mode_tiles = modes.reshape(NCL, CS, M).astype(jnp.float32)
    basis_v = col_basis.reshape(K, NCL, CS).astype(jnp.float32)
    compressed = jnp.einsum("kcs,csm->ckm", basis_v, mode_tiles).astype(jnp.bfloat16)
    device_of = jnp.arange(TOT_BLK, dtype=jnp.int32) // BLK_DEV
    row_global = ((device_of // N_CCOL) * GROUP + block_rows).astype(jnp.int32)
    col_global = (block_owner[:, 0] * CL_DEV + block_slot).astype(jnp.int32)

    def add_group(carry, index):
        start = (index * BLK_DEV).astype(jnp.int32)
        rows = lax.dynamic_slice_in_dim(row_global, start, BLK_DEV)
        columns = lax.dynamic_slice_in_dim(col_global, start, BLK_DEV)
        matrices = lax.dynamic_slice_in_dim(cores, start, BLK_DEV).reshape(BLK_DEV, K, K).astype(jnp.float32)
        picked = jnp.take(compressed, columns, axis=0).astype(jnp.float32)
        block_terms = jnp.einsum("bkj,bjm->bkm", matrices, picked)
        return carry.at[rows].add(block_terms), None

    far_sum = lax.scan(add_group, jnp.zeros((NCL, K, M), jnp.float32), jnp.arange(DEVICES, dtype=jnp.int32))[0]
    far_rounded = far_sum.astype(jnp.bfloat16)
    basis_u = row_basis.reshape(K, NCL, CS).astype(jnp.float32)
    far_part = jnp.einsum("krp,rkm->rpm", basis_u, far_rounded.astype(jnp.float32))
    padded = jnp.pad(modes, ((NH * CS, NH * CS), (0, 0))).reshape(NCL + 2 * NH, CS, M)
    near_view = near_blocks.reshape(NCL, CS, NEAR, CS)
    near_sum = jnp.zeros((NCL, CS, M), jnp.float32)
    for offset in range(NEAR):
        near_sum = near_sum + jnp.einsum("rpq,rqm->rpm", near_view[:, :, offset, :].astype(jnp.float32), padded[offset:offset + NCL].astype(jnp.float32))
    return (near_sum + far_part).astype(jnp.bfloat16).reshape(NPAN, M)
```

```python
import functools

import jax
import jax.numpy as jnp
from jax import lax
from jax.experimental import pallas as pl
from jax.experimental.pallas import tpu as pltpu
from jax.sharding import PartitionSpec as P

CS = 256
NH = 4
NEAR = 9
CAP = 2
MIB = 1 << 20
VMEM = pltpu.VMEM
SMEM = pltpu.SMEM


def whole(space=VMEM):
    return pl.BlockSpec(memory_space=space)


def compress_kernel(basis_ref, modes_ref, out_ref):
    out_ref[0] = jnp.dot(
        basis_ref[...], modes_ref[...], preferred_element_type=jnp.float32
    ).astype(jnp.bfloat16)


def compress(col_basis, modes):
    rank, panels = col_basis.shape
    cols = modes.shape[1]
    count = panels // CS
    return pl.pallas_call(
        compress_kernel,
        grid=(count,),
        in_specs=[
            pl.BlockSpec((rank, CS), lambda r: (0, r)),
            pl.BlockSpec((CS, cols), lambda r: (r, 0)),
        ],
        out_specs=pl.BlockSpec((1, rank, cols), lambda r: (r, 0, 0)),
        out_shape=jax.ShapeDtypeStruct((count, rank, cols), jnp.bfloat16),
        cost_estimate=pl.CostEstimate(
            flops=2 * rank * panels * cols, bytes_accessed=3 * MIB, transcendentals=0
        ),
        name="compress",
    )(col_basis, modes)


def dispatch_kernel(
    cols, slots, cl_dev, rows_ref, owners_ref, slot_ref, cores_ref, out_ref, count_ref, meta_ref
):
    blocks, rows, _ = cores_ref.shape
    out_ref[...] = jnp.zeros_like(out_ref)
    meta_ref[...] = jnp.zeros_like(meta_ref)
    lane = lax.broadcasted_iota(jnp.int32, (1, 128), 1)
    for j in range(cols):
        count_ref[j] = 0

    def place(b, carry):
        owner = owners_ref[b]
        column = owner % cols
        at = count_ref[column]
        count_ref[column] = at + 1
        out_ref[column, pl.ds(pl.multiple_of(at * rows, rows), rows), :] = cores_ref[b]
        cluster = (owner // cols) * cl_dev + slot_ref[b]
        entry = (
            jnp.where(lane == at, cluster, 0)
            + jnp.where(lane == slots + at, rows_ref[b], 0)
            + jnp.where(lane == 2 * slots, 1, 0)
        )
        meta_ref[pl.ds(column, 1), :] += entry.astype(jnp.float32)
        return carry

    lax.fori_loop(0, blocks, place, 0)
    for j in range(cols):
        out_ref[j, slots * rows :, :] = jnp.broadcast_to(
            meta_ref[j : j + 1, :], (16, 128)
        ).astype(jnp.bfloat16)


def dispatch(block_rows, owners, block_slot, cores, cols, slots, cl_dev):
    blocks, rows, _ = cores.shape
    return pl.pallas_call(
        functools.partial(dispatch_kernel, cols, slots, cl_dev),
        in_specs=[whole(SMEM), whole(SMEM), whole(SMEM), whole()],
        out_specs=whole(),
        out_shape=jax.ShapeDtypeStruct((cols, slots * rows + 16, 128), jnp.bfloat16),
        scratch_shapes=[SMEM((cols,), jnp.int32), VMEM((cols, 128), jnp.float32)],
        compiler_params=pltpu.CompilerParams(vmem_limit_bytes=16 * MIB),
        cost_estimate=pl.CostEstimate(flops=4 * MIB, bytes_accessed=3 * MIB, transcendentals=0),
        name="dispatch",
    )(block_rows, owners, block_slot, cores)


UNROLL = 4


def far_kernel(slots, rows, comp_ref, sent_ref, out_ref, meta_ref, smem_ref, list_ref, total_ref, sem):
    sources = sent_ref.shape[0]

    @pl.when(pl.program_id(0) == 0)
    def _():
        meta = sent_ref[:, slots * rows : slots * rows + 16, :].astype(jnp.float32)
        meta_ref[...] = jnp.max(meta, axis=1).astype(jnp.int32)
        copy = pltpu.make_async_copy(meta_ref, smem_ref, sem)
        copy.start()
        copy.wait()

        def source(i, total):
            def entry(p, total):
                list_ref[total] = ((i * slots + p) << 16) + (smem_ref[i, p] << 8) + smem_ref[i, slots + p]
                return total + 1

            return lax.fori_loop(0, smem_ref[i, 2 * slots], entry, total)

        total = lax.fori_loop(0, sources, source, 0)
        total_ref[0] = total
        for i in range(UNROLL):
            list_ref[total + i] = 0

    out_ref[...] = jnp.zeros_like(out_ref)
    total = total_ref[0]

    def group(g, carry):
        terms = []
        for i in range(UNROLL):
            at = g * UNROLL + i
            entry = list_ref[at]
            place = entry >> 16
            core = sent_ref[place // slots, pl.ds(pl.multiple_of((place % slots) * rows, rows), rows), :]
            core = jnp.where(at < total, core, jnp.zeros_like(core))
            half = core.shape[1] // 2
            core = jnp.concatenate([core[:, :half], core[:, half:]], axis=0)
            comp = comp_ref[(entry >> 8) & 255]
            terms.append((entry & 255, jnp.dot(core, comp, preferred_element_type=jnp.float32)))
        for row, term in terms:
            out_ref[row] += term
        return carry

    lax.fori_loop(0, (total + UNROLL - 1) // UNROLL, group, 0)


def far_field(comp, sent, slots, rows, group_rows):
    clusters, rank, cols = comp.shape
    sources = sent.shape[0]
    width = cols // 2
    return pl.pallas_call(
        functools.partial(far_kernel, slots, rows),
        grid=(cols // width,),
        in_specs=[
            pl.BlockSpec((clusters, rank, width), lambda m: (0, 0, m)),
            pl.BlockSpec(sent.shape, lambda m: (0, 0, 0)),
        ],
        out_specs=pl.BlockSpec((group_rows, rank, width), lambda m: (0, 0, m)),
        out_shape=jax.ShapeDtypeStruct((group_rows, rank, cols), jnp.float32),
        scratch_shapes=[
            VMEM((sources, 128), jnp.int32),
            SMEM((sources, 128), jnp.int32),
            SMEM((sources * slots + UNROLL,), jnp.int32),
            SMEM((1,), jnp.int32),
            pltpu.SemaphoreType.DMA,
        ],
        compiler_params=pltpu.CompilerParams(vmem_limit_bytes=40 * MIB),
        cost_estimate=pl.CostEstimate(
            flops=2 * 128 * rank * rank * cols * 8, bytes_accessed=24 * MIB, transcendentals=0
        ),
        name="far_field",
    )(comp, sent)


def near_kernel(near_ref, before_ref, modes_ref, after_ref, out_ref, ext_ref):
    r = pl.program_id(0)
    halo, panels = before_ref.shape[0], modes_ref.shape[0]

    @pl.when(r == 0)
    def _():
        ext_ref[:halo] = before_ref[...]
        ext_ref[halo : halo + panels] = modes_ref[...]
        ext_ref[halo + panels :] = after_ref[...]

    window = ext_ref[pl.ds(pl.multiple_of(r * CS, CS), NEAR * CS), :]
    out_ref[...] = jnp.dot(near_ref[...], window, preferred_element_type=jnp.float32)


def near_field(near_blocks, before, modes, after):
    panels, band = near_blocks.shape
    cols = modes.shape[1]
    halo = before.shape[0]
    return pl.pallas_call(
        near_kernel,
        grid=(panels // CS,),
        in_specs=[pl.BlockSpec((CS, band), lambda r: (r, 0))] + [whole()] * 3,
        out_specs=pl.BlockSpec((CS, cols), lambda r: (r, 0)),
        out_shape=jax.ShapeDtypeStruct((panels, cols), jnp.float32),
        scratch_shapes=[VMEM((panels + 2 * halo, cols), jnp.bfloat16)],
        compiler_params=pltpu.CompilerParams(vmem_limit_bytes=32 * MIB),
        cost_estimate=pl.CostEstimate(
            flops=2 * panels * band * cols, bytes_accessed=18 * MIB, transcendentals=0
        ),
        name="near_field",
    )(near_blocks, before, modes, after)


def expand_kernel(near_ref, basis_ref, far_ref, out_ref):
    rank = basis_ref.shape[0]
    half = rank // 2
    want = lax.broadcasted_iota(jnp.int32, (rank, rank), 0)
    have = lax.broadcasted_iota(jnp.int32, (rank, rank), 1)
    order = jnp.where(want < half, 2 * want, 2 * (want - half) + 1)
    select = jnp.where(order == have, 1.0, 0.0).astype(jnp.bfloat16)
    basis = jnp.dot(select, basis_ref[...], preferred_element_type=jnp.float32).astype(jnp.bfloat16)
    far = lax.dot_general(
        basis, far_ref[0], (((0,), (0,)), ((), ())), preferred_element_type=jnp.float32
    )
    out_ref[...] = (near_ref[...] + far).astype(jnp.bfloat16)


def expand(near, row_basis, far):
    panels, cols = near.shape
    rank = row_basis.shape[0]
    return pl.pallas_call(
        expand_kernel,
        grid=(panels // CS,),
        in_specs=[
            pl.BlockSpec((CS, cols), lambda r: (r, 0)),
            pl.BlockSpec((rank, CS), lambda r: (0, r)),
            pl.BlockSpec((1, rank, cols), lambda r: (r, 0, 0)),
        ],
        out_specs=pl.BlockSpec((CS, cols), lambda r: (r, 0)),
        out_shape=jax.ShapeDtypeStruct((panels, cols), jnp.bfloat16),
        cost_estimate=pl.CostEstimate(
            flops=2 * panels * rank * cols, bytes_accessed=7 * MIB, transcendentals=0
        ),
        name="expand",
    )(near, row_basis, far)


def per_device(modes, col_basis, row_basis, near_blocks, block_rows, block_owner, block_slot, cores):
    row_devices, col_devices = lax.axis_size("crow"), lax.axis_size("ccol")
    devices = row_devices * col_devices
    cluster_count = modes.shape[0] // CS
    rank = col_basis.shape[0]
    blocks = cores.shape[0]
    slots = CAP * row_devices

    up = [(i, i + 1) for i in range(devices - 1)]
    down = [(j, i) for i, j in up]
    before = lax.ppermute(modes[-NH * CS :], ("crow", "ccol"), up)
    after = lax.ppermute(modes[: NH * CS], ("crow", "ccol"), down)

    compressed = compress(col_basis, modes)
    gathered = lax.all_gather(compressed, "crow", axis=0, tiled=True)

    lines = rank * rank // 128
    sent = dispatch(
        block_rows, block_owner[:, 0], block_slot, cores.reshape(blocks, lines, 128),
        col_devices, slots, cluster_count,
    )
    sent = lax.all_to_all(sent, "ccol", split_axis=0, concat_axis=0, tiled=True)
    partial = far_field(gathered, sent, slots, lines, col_devices * cluster_count)
    far = lax.psum_scatter(partial, "ccol", scatter_dimension=0, tiled=True).astype(jnp.bfloat16)
    near = near_field(near_blocks, before, modes, after)
    return expand(near, row_basis, far)


def solution(mesh):
    both = ("crow", "ccol")
    in_specs = (
        P(both, None),
        P(None, both),
        P(None, both),
        P(both, None),
        P(both),
        P(both, None),
        P(both),
        P(both, None),
    )
    return jax.shard_map(
        per_device, mesh=mesh, in_specs=in_specs, out_specs=P(both, None), check_vma=False
    )
```

```python
import functools

import jax
import jax.numpy as jnp
from jax import lax
from jax.experimental import pallas as pl
from jax.experimental.pallas import tpu as pltpu
from jax.sharding import PartitionSpec as P

CS = 256
NH = 4
NEAR = 9
CAP = 2
MIB = 1 << 20
VMEM = pltpu.VMEM
SMEM = pltpu.SMEM


def whole(space=VMEM):
    return pl.BlockSpec(memory_space=space)


COMPRESS = 4


def compress_kernel(basis_ref, modes_ref, out_ref):
    for i in range(COMPRESS):
        out_ref[i] = jnp.dot(
            basis_ref[:, i * CS : (i + 1) * CS],
            modes_ref[i * CS : (i + 1) * CS, :],
            preferred_element_type=jnp.float32,
        ).astype(jnp.bfloat16)


def compress(col_basis, modes):
    rank, panels = col_basis.shape
    cols = modes.shape[1]
    count = panels // CS
    return pl.pallas_call(
        compress_kernel,
        grid=(count // COMPRESS,),
        in_specs=[
            pl.BlockSpec((rank, COMPRESS * CS), lambda r: (0, r)),
            pl.BlockSpec((COMPRESS * CS, cols), lambda r: (r, 0)),
        ],
        out_specs=pl.BlockSpec((COMPRESS, rank, cols), lambda r: (r, 0, 0)),
        out_shape=jax.ShapeDtypeStruct((count, rank, cols), jnp.bfloat16),
        cost_estimate=pl.CostEstimate(
            flops=2 * rank * panels * cols, bytes_accessed=3 * MIB, transcendentals=0
        ),
        name="compress",
    )(col_basis, modes)


def dispatch_kernel(
    cols, slots, cl_dev, rows_ref, owners_ref, slot_ref, cores_ref, out_ref, count_ref, meta_ref
):
    blocks, rows, _ = cores_ref.shape
    out_ref[...] = jnp.zeros_like(out_ref)
    meta_ref[...] = jnp.zeros_like(meta_ref)
    lane = lax.broadcasted_iota(jnp.int32, (1, 128), 1)
    for j in range(cols):
        count_ref[j] = 0

    def place(b, carry):
        owner = owners_ref[b]
        column = owner % cols
        at = count_ref[column]
        count_ref[column] = at + 1
        out_ref[column, pl.ds(pl.multiple_of(at * rows, rows), rows), :] = cores_ref[b]
        cluster = (owner // cols) * cl_dev + slot_ref[b]
        entry = (
            jnp.where(lane == at, cluster, 0)
            + jnp.where(lane == slots + at, rows_ref[b], 0)
            + jnp.where(lane == 2 * slots, 1, 0)
        )
        meta_ref[pl.ds(column, 1), :] += entry.astype(jnp.float32)
        return carry

    lax.fori_loop(0, blocks, place, 0)
    for j in range(cols):
        out_ref[j, slots * rows :, :] = jnp.broadcast_to(
            meta_ref[j : j + 1, :], (16, 128)
        ).astype(jnp.bfloat16)


def dispatch(block_rows, owners, block_slot, cores, cols, slots, cl_dev):
    blocks, rows, _ = cores.shape
    return pl.pallas_call(
        functools.partial(dispatch_kernel, cols, slots, cl_dev),
        in_specs=[whole(SMEM), whole(SMEM), whole(SMEM), whole()],
        out_specs=whole(),
        out_shape=jax.ShapeDtypeStruct((cols, slots * rows + 16, 128), jnp.bfloat16),
        scratch_shapes=[SMEM((cols,), jnp.int32), VMEM((cols, 128), jnp.float32)],
        compiler_params=pltpu.CompilerParams(vmem_limit_bytes=16 * MIB),
        cost_estimate=pl.CostEstimate(flops=4 * MIB, bytes_accessed=3 * MIB, transcendentals=0),
        name="dispatch",
    )(block_rows, owners, block_slot, cores)


UNROLL = 8


def far_kernel(
    slots, rows, x_first, comp_ref, sent_ref, far_ref, next_ref, last_ref, next_sum_ref, last_sum_ref, own_ref,
    acc_ref, meta_ref, smem_ref, list_ref, sem,
):
    sources = sent_ref.shape[0]
    group_rows = acc_ref.shape[0]
    part = group_rows // 4
    me = lax.axis_index("ccol")
    here_x, here_z = me // 4, me % 4

    acc_ref[...] = jnp.zeros_like(acc_ref)
    meta = sent_ref[:, slots * rows : slots * rows + 16, :].astype(jnp.float32)
    meta_ref[...] = jnp.max(meta, axis=1).astype(jnp.int32)
    copy = pltpu.make_async_copy(meta_ref, smem_ref, sem)
    copy.start()
    copy.wait()

    def source(i, total):
        def entry(p, total):
            row = smem_ref[i, slots + p]
            to_x = (row // part - here_x + 4) % 4
            to_z = (row // (part // 4) % 4 - here_z + 4) % 4
            first, second = (to_x, to_z) if x_first else (to_z, to_x)
            at = first * part + second * (part // 4) + row % (part // 4)
            list_ref[total] = ((i * slots + p) << 16) + (smem_ref[i, p] << 8) + at
            return total + 1

        return lax.fori_loop(0, smem_ref[i, 2 * slots], entry, total)

    total = lax.fori_loop(0, sources, source, 0)
    for i in range(UNROLL):
        list_ref[total + i] = 0

    def group(g, carry):
        terms = []
        for i in range(UNROLL):
            at = g * UNROLL + i
            entry = list_ref[at]
            place = entry >> 16
            core = sent_ref[place // slots, pl.ds(pl.multiple_of((place % slots) * rows, rows), rows), :]
            core = jnp.where(at < total, core, jnp.zeros_like(core))
            half = core.shape[1] // 2
            core = jnp.concatenate([core[:, :half], core[:, half:]], axis=0)
            comp = comp_ref[(entry >> 8) & 255]
            terms.append((entry & 255, jnp.dot(core, comp, preferred_element_type=jnp.float32)))
        for row, term in terms:
            acc_ref[row] += term
        return carry

    lax.fori_loop(0, (total + UNROLL - 1) // UNROLL, group, 0)
    half = part // 2
    own_ref[...] = acc_ref[:part]
    next_sum_ref[...] = acc_ref[part : part + half]
    next_ref[...] = acc_ref[part + half : 2 * part].astype(jnp.bfloat16)
    far_ref[...] = acc_ref[2 * part : 3 * part].astype(jnp.bfloat16)
    last_ref[...] = acc_ref[3 * part : 3 * part + half].astype(jnp.bfloat16)
    last_sum_ref[...] = acc_ref[3 * part + half :]


def far_field(comp, sent, slots, rows, group_rows, x_first):
    clusters, rank, cols = comp.shape
    sources = sent.shape[0]
    width = cols // 2
    chunk = 0 if x_first else 1
    part = group_rows // 4
    kinds = [
        (part, jnp.bfloat16),
        (part // 2, jnp.bfloat16),
        (part // 2, jnp.bfloat16),
        (part // 2, jnp.float32),
        (part // 2, jnp.float32),
        (part, jnp.float32),
    ]
    return pl.pallas_call(
        functools.partial(far_kernel, slots, rows, x_first),
        grid=(1,),
        in_specs=[
            pl.BlockSpec((clusters, rank, width), lambda m: (0, 0, chunk)),
            pl.BlockSpec(sent.shape, lambda m: (0, 0, 0)),
        ],
        out_specs=[pl.BlockSpec((n, rank, width), lambda m: (0, 0, 0)) for n, _ in kinds],
        out_shape=[jax.ShapeDtypeStruct((n, rank, width), kind) for n, kind in kinds],
        scratch_shapes=[
            VMEM((group_rows, rank, width), jnp.float32),
            VMEM((sources, 128), jnp.int32),
            SMEM((sources, 128), jnp.int32),
            SMEM((sources * slots + UNROLL,), jnp.int32),
            pltpu.SemaphoreType.DMA,
        ],
        compiler_params=pltpu.CompilerParams(vmem_limit_bytes=40 * MIB),
        cost_estimate=pl.CostEstimate(
            flops=2 * 128 * rank * rank * width * 8, bytes_accessed=12 * MIB, transcendentals=0
        ),
        name="far_x" if x_first else "far_z",
    )(comp, sent)


def ring(axis_is_x, step):
    def to(i):
        x, z = i // 4, i % 4
        return ((x + step) % 4) * 4 + z if axis_is_x else x * 4 + (z + step) % 4

    return [(i, to(i)) for i in range(16)]


def f32(value):
    return value.astype(jnp.float32)


def reduce_parts(parts, x_first):
    far, following, last, following_sum, last_sum, own = parts
    half = far.shape[0] // 2
    to_next = functools.partial(lax.ppermute, axis_name="ccol", perm=ring(x_first, 1))
    to_last = functools.partial(lax.ppermute, axis_name="ccol", perm=ring(x_first, -1))
    far_up = to_next(far[:half])
    far_down = to_last(far[half:])
    own_b = f32(to_next(following))
    own_a = f32(to_last(last))
    up = f32(to_next((following_sum + f32(far_up)).astype(jnp.bfloat16)))
    down = f32(to_last((last_sum + f32(far_down)).astype(jnp.bfloat16)))
    first = own[:half] + own_a + up
    second = own[half:] + own_b + down
    quarter = half // 2
    here, following, far, last = first[:quarter], first[quarter:], second[:quarter], second[quarter:]

    half = quarter // 2
    to_next = functools.partial(lax.ppermute, axis_name="ccol", perm=ring(not x_first, 1))
    to_last = functools.partial(lax.ppermute, axis_name="ccol", perm=ring(not x_first, -1))
    far = far.astype(jnp.bfloat16)
    far_up = f32(to_next(far[:half]))
    far_down = f32(to_last(far[half:]))
    following = jnp.concatenate([following[:half] + far_up, following[half:]])
    last = jnp.concatenate([last[:half], last[half:] + far_down])
    up = f32(to_next(following.astype(jnp.bfloat16)))
    down = f32(to_last(last.astype(jnp.bfloat16)))
    return (here + up + down).astype(jnp.bfloat16)


def near_kernel(near_ref, before_ref, modes_ref, after_ref, basis_ref, out_ref, turned_ref, ext_ref):
    r = pl.program_id(0)
    halo, panels = before_ref.shape[0], modes_ref.shape[0]
    rank = basis_ref.shape[0]

    @pl.when(r == 0)
    def _():
        ext_ref[:halo] = before_ref[...]
        ext_ref[halo : halo + panels] = modes_ref[...]
        ext_ref[halo + panels :] = after_ref[...]

    window = ext_ref[pl.ds(pl.multiple_of(r * CS, CS), NEAR * CS), :]
    out_ref[...] = jnp.dot(near_ref[...], window, preferred_element_type=jnp.float32)
    have = lax.broadcasted_iota(jnp.int32, (rank, rank), 0)
    want = lax.broadcasted_iota(jnp.int32, (rank, rank), 1)
    order = jnp.where(want < rank // 2, 2 * want, 2 * want - rank + 1)
    select = jnp.where(order == have, 1.0, 0.0).astype(jnp.bfloat16)
    turned_ref[...] = lax.dot_general(
        basis_ref[...], select, (((0,), (0,)), ((), ())), preferred_element_type=jnp.float32
    ).astype(jnp.bfloat16)


def near_field(near_blocks, before, modes, after, row_basis):
    panels, band = near_blocks.shape
    cols = modes.shape[1]
    halo = before.shape[0]
    rank = row_basis.shape[0]
    return pl.pallas_call(
        near_kernel,
        grid=(panels // CS,),
        in_specs=[pl.BlockSpec((CS, band), lambda r: (r, 0))]
        + [whole()] * 3
        + [pl.BlockSpec((rank, CS), lambda r: (0, r))],
        out_specs=[
            pl.BlockSpec((CS, cols), lambda r: (r, 0)),
            pl.BlockSpec((CS, rank), lambda r: (r, 0)),
        ],
        out_shape=[
            jax.ShapeDtypeStruct((panels, cols), jnp.float32),
            jax.ShapeDtypeStruct((panels, rank), jnp.bfloat16),
        ],
        scratch_shapes=[VMEM((panels + 2 * halo, cols), jnp.bfloat16)],
        compiler_params=pltpu.CompilerParams(vmem_limit_bytes=32 * MIB),
        cost_estimate=pl.CostEstimate(
            flops=2 * panels * band * cols, bytes_accessed=18 * MIB, transcendentals=0
        ),
        name="near_field",
    )(near_blocks, before, modes, after, row_basis)


EXPAND = 2


def expand_kernel(near_ref, basis_ref, left_ref, right_ref, out_ref):
    width = left_ref.shape[2]
    for i in range(EXPAND):
        rows = pl.ds(i * CS, CS)
        for half, far_ref in enumerate((left_ref, right_ref)):
            cols = pl.ds(half * width, width)
            far = jnp.dot(basis_ref[rows, :], far_ref[i], preferred_element_type=jnp.float32)
            out_ref[rows, cols] = (near_ref[rows, cols] + far).astype(jnp.bfloat16)


def expand(near, basis, left, right):
    panels, cols = near.shape
    rank = basis.shape[1]
    width = cols // 2
    return pl.pallas_call(
        expand_kernel,
        grid=(panels // CS // EXPAND,),
        in_specs=[
            pl.BlockSpec((EXPAND * CS, cols), lambda r: (r, 0)),
            pl.BlockSpec((EXPAND * CS, rank), lambda r: (r, 0)),
            pl.BlockSpec((EXPAND, rank, width), lambda r: (r, 0, 0)),
            pl.BlockSpec((EXPAND, rank, width), lambda r: (r, 0, 0)),
        ],
        out_specs=pl.BlockSpec((EXPAND * CS, cols), lambda r: (r, 0)),
        out_shape=jax.ShapeDtypeStruct((panels, cols), jnp.bfloat16),
        compiler_params=pltpu.CompilerParams(vmem_limit_bytes=24 * MIB),
        cost_estimate=pl.CostEstimate(
            flops=2 * panels * rank * cols, bytes_accessed=7 * MIB, transcendentals=0
        ),
        name="expand",
    )(near, basis, left, right)


def per_device(modes, col_basis, row_basis, near_blocks, block_rows, block_owner, block_slot, cores):
    row_devices, col_devices = lax.axis_size("crow"), lax.axis_size("ccol")
    devices = row_devices * col_devices
    cluster_count = modes.shape[0] // CS
    rank = col_basis.shape[0]
    blocks = cores.shape[0]
    slots = CAP * row_devices

    compressed = compress(col_basis, modes)
    gathered = lax.all_gather(compressed, "crow", axis=0, tiled=True)

    edges, _ = lax.optimization_barrier((modes, compressed))
    up = [(i, i + 1) for i in range(devices - 1)]
    down = [(j, i) for i, j in up]
    before = lax.ppermute(edges[-NH * CS :], ("crow", "ccol"), up)
    after = lax.ppermute(edges[: NH * CS], ("crow", "ccol"), down)

    lines = rank * rank // 128
    sent = dispatch(
        block_rows, block_owner[:, 0], block_slot, cores.reshape(blocks, lines, 128),
        col_devices, slots, cluster_count,
    )
    sent = lax.all_to_all(sent, "ccol", split_axis=0, concat_axis=0, tiled=True)
    gathered, sent, before, after = lax.optimization_barrier((gathered, sent, before, after))
    group_rows = col_devices * cluster_count
    left = far_field(gathered, sent, slots, lines, group_rows, True)
    right = far_field(gathered, sent, slots, lines, group_rows, False)
    near, basis = near_field(near_blocks, before, modes, after, row_basis)
    return expand(near, basis, reduce_parts(left, True), reduce_parts(right, False))


def solution(mesh):
    both = ("crow", "ccol")
    in_specs = (
        P(both, None),
        P(None, both),
        P(None, both),
        P(both, None),
        P(both),
        P(both, None),
        P(both),
        P(both, None),
    )
    return jax.shard_map(
        per_device, mesh=mesh, in_specs=in_specs, out_specs=P(both, None), check_vma=False
    )
```

```python
import functools

import jax
import jax.numpy as jnp
from jax import lax
from jax.experimental import pallas as pl
from jax.experimental.pallas import tpu as pltpu
from jax.sharding import PartitionSpec as P

CS = 256
NH = 4
NEAR = 9
CAP = 2
MIB = 1 << 20
VMEM = pltpu.VMEM
SMEM = pltpu.SMEM


def whole(space=VMEM):
    return pl.BlockSpec(memory_space=space)


COMPRESS = 4


def compress_kernel(basis_ref, modes_ref, out_ref):
    for i in range(COMPRESS):
        out_ref[i] = jnp.dot(
            basis_ref[:, i * CS : (i + 1) * CS],
            modes_ref[i * CS : (i + 1) * CS, :],
            preferred_element_type=jnp.float32,
        ).astype(jnp.bfloat16)


def compress(col_basis, modes):
    rank, panels = col_basis.shape
    cols = modes.shape[1]
    count = panels // CS
    return pl.pallas_call(
        compress_kernel,
        grid=(count // COMPRESS,),
        in_specs=[
            pl.BlockSpec((rank, COMPRESS * CS), lambda r: (0, r)),
            pl.BlockSpec((COMPRESS * CS, cols), lambda r: (r, 0)),
        ],
        out_specs=pl.BlockSpec((COMPRESS, rank, cols), lambda r: (r, 0, 0)),
        out_shape=jax.ShapeDtypeStruct((count, rank, cols), jnp.bfloat16),
        cost_estimate=pl.CostEstimate(
            flops=2 * rank * panels * cols, bytes_accessed=3 * MIB, transcendentals=0
        ),
        name="compress",
    )(col_basis, modes)


def dispatch_kernel(
    cols, slots, cl_dev, rows_ref, owners_ref, slot_ref, cores_ref, out_ref, count_ref, meta_ref
):
    blocks, rows, _ = cores_ref.shape
    out_ref[...] = jnp.zeros_like(out_ref)
    meta_ref[...] = jnp.zeros_like(meta_ref)
    lane = lax.broadcasted_iota(jnp.int32, (1, 128), 1)
    for j in range(cols):
        count_ref[j] = 0

    def place(b, carry):
        owner = owners_ref[b]
        column = owner % cols
        at = count_ref[column]
        count_ref[column] = at + 1
        out_ref[column, pl.ds(pl.multiple_of(at * rows, rows), rows), :] = cores_ref[b]
        cluster = (owner // cols) * cl_dev + slot_ref[b]
        entry = (
            jnp.where(lane == at, cluster, 0)
            + jnp.where(lane == slots + at, rows_ref[b], 0)
            + jnp.where(lane == 2 * slots, 1, 0)
        )
        meta_ref[pl.ds(column, 1), :] += entry.astype(jnp.float32)
        return carry

    lax.fori_loop(0, blocks, place, 0)
    for j in range(cols):
        out_ref[j, slots * rows :, :] = jnp.broadcast_to(
            meta_ref[j : j + 1, :], (16, 128)
        ).astype(jnp.bfloat16)


def dispatch(block_rows, owners, block_slot, cores, cols, slots, cl_dev):
    blocks, rows, _ = cores.shape
    return pl.pallas_call(
        functools.partial(dispatch_kernel, cols, slots, cl_dev),
        in_specs=[whole(SMEM), whole(SMEM), whole(SMEM), whole()],
        out_specs=whole(),
        out_shape=jax.ShapeDtypeStruct((cols, slots * rows + 16, 128), jnp.bfloat16),
        scratch_shapes=[SMEM((cols,), jnp.int32), VMEM((cols, 128), jnp.float32)],
        compiler_params=pltpu.CompilerParams(vmem_limit_bytes=16 * MIB),
        cost_estimate=pl.CostEstimate(flops=4 * MIB, bytes_accessed=3 * MIB, transcendentals=0),
        name="dispatch",
    )(block_rows, owners, block_slot, cores)


UNROLL = 8


def far_kernel(
    slots, rows, x_first, comp_ref, sent_ref, far_ref, next_ref, last_ref, next_sum_ref, last_sum_ref, own_ref,
    acc_ref, meta_ref, smem_ref, list_ref, sem,
):
    sources = sent_ref.shape[0]
    group_rows = acc_ref.shape[0]
    part = group_rows // 4
    me = lax.axis_index("ccol")
    here_x, here_z = me // 4, me % 4

    acc_ref[...] = jnp.zeros_like(acc_ref)
    meta = sent_ref[:, slots * rows : slots * rows + 16, :].astype(jnp.float32)
    meta_ref[...] = jnp.max(meta, axis=1).astype(jnp.int32)
    copy = pltpu.make_async_copy(meta_ref, smem_ref, sem)
    copy.start()
    copy.wait()

    def source(i, total):
        def entry(p, total):
            row = smem_ref[i, slots + p]
            to_x = (row // part - here_x + 4) % 4
            to_z = (row // (part // 4) % 4 - here_z + 4) % 4
            first, second = (to_x, to_z) if x_first else (to_z, to_x)
            at = first * part + second * (part // 4) + row % (part // 4)
            list_ref[total] = ((i * slots + p) << 16) + (smem_ref[i, p] << 8) + at
            return total + 1

        return lax.fori_loop(0, smem_ref[i, 2 * slots], entry, total)

    total = lax.fori_loop(0, sources, source, 0)
    for i in range(UNROLL):
        list_ref[total + i] = 0

    def group(g, carry):
        terms = []
        for i in range(UNROLL):
            at = g * UNROLL + i
            entry = list_ref[at]
            place = entry >> 16
            core = sent_ref[place // slots, pl.ds(pl.multiple_of((place % slots) * rows, rows), rows), :]
            core = jnp.where(at < total, core, jnp.zeros_like(core))
            half = core.shape[1] // 2
            core = jnp.concatenate([core[:, :half], core[:, half:]], axis=0)
            comp = comp_ref[(entry >> 8) & 255]
            terms.append((entry & 255, jnp.dot(core, comp, preferred_element_type=jnp.float32)))
        for row, term in terms:
            acc_ref[row] += term
        return carry

    lax.fori_loop(0, (total + UNROLL - 1) // UNROLL, group, 0)
    half = part // 2
    own_ref[...] = acc_ref[:part]
    next_sum_ref[...] = acc_ref[part : part + half]
    next_ref[...] = acc_ref[part + half : 2 * part].astype(jnp.bfloat16)
    far_ref[...] = acc_ref[2 * part : 3 * part].astype(jnp.bfloat16)
    last_ref[...] = acc_ref[3 * part : 3 * part + half].astype(jnp.bfloat16)
    last_sum_ref[...] = acc_ref[3 * part + half :]


def far_field(comp, sent, slots, rows, group_rows, x_first):
    clusters, rank, cols = comp.shape
    sources = sent.shape[0]
    width = cols // 2
    chunk = 0 if x_first else 1
    part = group_rows // 4
    kinds = [
        (part, jnp.bfloat16),
        (part // 2, jnp.bfloat16),
        (part // 2, jnp.bfloat16),
        (part // 2, jnp.float32),
        (part // 2, jnp.float32),
        (part, jnp.float32),
    ]
    return pl.pallas_call(
        functools.partial(far_kernel, slots, rows, x_first),
        grid=(1,),
        in_specs=[
            pl.BlockSpec((clusters, rank, width), lambda m: (0, 0, chunk)),
            pl.BlockSpec(sent.shape, lambda m: (0, 0, 0)),
        ],
        out_specs=[pl.BlockSpec((n, rank, width), lambda m: (0, 0, 0)) for n, _ in kinds],
        out_shape=[jax.ShapeDtypeStruct((n, rank, width), kind) for n, kind in kinds],
        scratch_shapes=[
            VMEM((group_rows, rank, width), jnp.float32),
            VMEM((sources, 128), jnp.int32),
            SMEM((sources, 128), jnp.int32),
            SMEM((sources * slots + UNROLL,), jnp.int32),
            pltpu.SemaphoreType.DMA,
        ],
        compiler_params=pltpu.CompilerParams(vmem_limit_bytes=40 * MIB),
        cost_estimate=pl.CostEstimate(
            flops=2 * 128 * rank * rank * width * 8, bytes_accessed=12 * MIB, transcendentals=0
        ),
        name="far_x" if x_first else "far_z",
    )(comp, sent)


def ring(axis_is_x, step):
    def to(i):
        x, z = i // 4, i % 4
        return ((x + step) % 4) * 4 + z if axis_is_x else x * 4 + (z + step) % 4

    return [(i, to(i)) for i in range(16)]


def f32(value):
    return value.astype(jnp.float32)


def first_stage(parts, x_first):
    far, following, last, following_sum, last_sum, own = parts
    half = far.shape[0] // 2
    to_next = functools.partial(lax.ppermute, axis_name="ccol", perm=ring(x_first, 1))
    to_last = functools.partial(lax.ppermute, axis_name="ccol", perm=ring(x_first, -1))
    far_up = to_next(far[:half])
    far_down = to_last(far[half:])
    own_b = to_next(following)
    own_a = to_last(last)
    up = to_next((following_sum + f32(far_up)).astype(jnp.bfloat16))
    down = to_last((last_sum + f32(far_down)).astype(jnp.bfloat16))
    return own, own_a, own_b, up, down


def second_stage(arrived, x_first):
    own, own_a, own_b, up, down = arrived
    half = own_a.shape[0]
    first = own[:half] + f32(own_a) + f32(up)
    second = own[half:] + f32(own_b) + f32(down)
    quarter = half // 2
    here, following, far, last = first[:quarter], first[quarter:], second[:quarter], second[quarter:]

    half = quarter // 2
    to_next = functools.partial(lax.ppermute, axis_name="ccol", perm=ring(not x_first, 1))
    to_last = functools.partial(lax.ppermute, axis_name="ccol", perm=ring(not x_first, -1))
    far = far.astype(jnp.bfloat16)
    far_up = f32(to_next(far[:half]))
    far_down = f32(to_last(far[half:]))
    following = jnp.concatenate([following[:half] + far_up, following[half:]])
    last = jnp.concatenate([last[:half], last[half:] + far_down])
    up = f32(to_next(following.astype(jnp.bfloat16)))
    down = f32(to_last(last.astype(jnp.bfloat16)))
    return (here + up + down).astype(jnp.bfloat16)


def near_kernel(near_ref, before_ref, modes_ref, after_ref, basis_ref, out_ref, turned_ref, ext_ref):
    r = pl.program_id(0)
    halo, panels = before_ref.shape[0], modes_ref.shape[0]
    rank = basis_ref.shape[0]

    @pl.when(r == 0)
    def _():
        ext_ref[:halo] = before_ref[...]
        ext_ref[halo : halo + panels] = modes_ref[...]
        ext_ref[halo + panels :] = after_ref[...]

    window = ext_ref[pl.ds(pl.multiple_of(r * CS, CS), NEAR * CS), :]
    out_ref[...] = jnp.dot(near_ref[...], window, preferred_element_type=jnp.float32)
    have = lax.broadcasted_iota(jnp.int32, (rank, rank), 0)
    want = lax.broadcasted_iota(jnp.int32, (rank, rank), 1)
    order = jnp.where(want < rank // 2, 2 * want, 2 * want - rank + 1)
    select = jnp.where(order == have, 1.0, 0.0).astype(jnp.bfloat16)
    turned_ref[...] = lax.dot_general(
        basis_ref[...], select, (((0,), (0,)), ((), ())), preferred_element_type=jnp.float32
    ).astype(jnp.bfloat16)


def near_field(near_blocks, before, modes, after, row_basis):
    panels, band = near_blocks.shape
    cols = modes.shape[1]
    halo = before.shape[0]
    rank = row_basis.shape[0]
    return pl.pallas_call(
        near_kernel,
        grid=(panels // CS,),
        in_specs=[pl.BlockSpec((CS, band), lambda r: (r, 0))]
        + [whole()] * 3
        + [pl.BlockSpec((rank, CS), lambda r: (0, r))],
        out_specs=[
            pl.BlockSpec((CS, cols), lambda r: (r, 0)),
            pl.BlockSpec((CS, rank), lambda r: (r, 0)),
        ],
        out_shape=[
            jax.ShapeDtypeStruct((panels, cols), jnp.float32),
            jax.ShapeDtypeStruct((panels, rank), jnp.bfloat16),
        ],
        scratch_shapes=[VMEM((panels + 2 * halo, cols), jnp.bfloat16)],
        compiler_params=pltpu.CompilerParams(vmem_limit_bytes=32 * MIB),
        cost_estimate=pl.CostEstimate(
            flops=2 * panels * band * cols, bytes_accessed=18 * MIB, transcendentals=0
        ),
        name="near_field",
    )(near_blocks, before, modes, after, row_basis)


EXPAND = 2


def expand_kernel(near_ref, basis_ref, left_ref, right_ref, out_ref):
    width = left_ref.shape[2]
    for i in range(EXPAND):
        rows = pl.ds(i * CS, CS)
        for half, far_ref in enumerate((left_ref, right_ref)):
            cols = pl.ds(half * width, width)
            far = jnp.dot(basis_ref[rows, :], far_ref[i], preferred_element_type=jnp.float32)
            out_ref[rows, cols] = (near_ref[rows, cols] + far).astype(jnp.bfloat16)


def expand(near, basis, left, right):
    panels, cols = near.shape
    rank = basis.shape[1]
    width = cols // 2
    return pl.pallas_call(
        expand_kernel,
        grid=(panels // CS // EXPAND,),
        in_specs=[
            pl.BlockSpec((EXPAND * CS, cols), lambda r: (r, 0)),
            pl.BlockSpec((EXPAND * CS, rank), lambda r: (r, 0)),
            pl.BlockSpec((EXPAND, rank, width), lambda r: (r, 0, 0)),
            pl.BlockSpec((EXPAND, rank, width), lambda r: (r, 0, 0)),
        ],
        out_specs=pl.BlockSpec((EXPAND * CS, cols), lambda r: (r, 0)),
        out_shape=jax.ShapeDtypeStruct((panels, cols), jnp.bfloat16),
        compiler_params=pltpu.CompilerParams(vmem_limit_bytes=24 * MIB),
        cost_estimate=pl.CostEstimate(
            flops=2 * panels * rank * cols, bytes_accessed=7 * MIB, transcendentals=0
        ),
        name="expand",
    )(near, basis, left, right)


def per_device(modes, col_basis, row_basis, near_blocks, block_rows, block_owner, block_slot, cores):
    row_devices, col_devices = lax.axis_size("crow"), lax.axis_size("ccol")
    devices = row_devices * col_devices
    cluster_count = modes.shape[0] // CS
    rank = col_basis.shape[0]
    blocks = cores.shape[0]
    slots = CAP * row_devices

    compressed = compress(col_basis, modes)
    gathered = lax.all_gather(compressed, "crow", axis=0, tiled=True)

    lines = rank * rank // 128
    sent = dispatch(
        block_rows, block_owner[:, 0], block_slot, cores.reshape(blocks, lines, 128),
        col_devices, slots, cluster_count,
    )
    sent = lax.all_to_all(sent, "ccol", split_axis=0, concat_axis=0, tiled=True)

    edges, sent = lax.optimization_barrier((modes, sent))
    up = [(i, i + 1) for i in range(devices - 1)]
    down = [(j, i) for i, j in up]
    before = lax.ppermute(edges[-NH * CS :], ("crow", "ccol"), up)
    after = lax.ppermute(edges[: NH * CS], ("crow", "ccol"), down)

    group_rows = col_devices * cluster_count
    left = list(far_field(gathered, sent, slots, lines, group_rows, True))
    gathered, sent, left[0] = lax.optimization_barrier((gathered, sent, left[0]))
    right = list(far_field(gathered, sent, slots, lines, group_rows, False))
    right[0], before, after = lax.optimization_barrier((right[0], before, after))
    near, basis = near_field(near_blocks, before, modes, after, row_basis)
    left = first_stage(left, True)
    right = first_stage(right, False)
    left, near, basis = lax.optimization_barrier((left, near, basis))
    return expand(near, basis, second_stage(left, True), second_stage(right, False))


def solution(mesh):
    both = ("crow", "ccol")
    in_specs = (
        P(both, None),
        P(None, both),
        P(None, both),
        P(both, None),
        P(both),
        P(both, None),
        P(both),
        P(both, None),
    )
    return jax.shard_map(
        per_device, mesh=mesh, in_specs=in_specs, out_specs=P(both, None), check_vma=False
    )
```

```python
import functools

import jax
import jax.numpy as jnp
from jax import lax
from jax.experimental import pallas as pl
from jax.experimental.pallas import tpu as pltpu
from jax.sharding import PartitionSpec as P

CS = 256
NH = 4
NEAR = 9
CAP = 2
MIB = 1 << 20
VMEM = pltpu.VMEM
SMEM = pltpu.SMEM


def whole(space=VMEM):
    return pl.BlockSpec(memory_space=space)


COMPRESS = 4


def compress_kernel(basis_ref, modes_ref, out_ref, low_ref, high_ref):
    step = pl.program_id(0)

    @pl.when(step == 0)
    def _():
        low_ref[...] = modes_ref[: NH * CS, :]

    @pl.when(step == pl.num_programs(0) - 1)
    def _():
        high_ref[...] = modes_ref[(COMPRESS - NH) * CS :, :]

    for i in range(COMPRESS):
        out_ref[i] = jnp.dot(
            basis_ref[:, i * CS : (i + 1) * CS],
            modes_ref[i * CS : (i + 1) * CS, :],
            preferred_element_type=jnp.float32,
        ).astype(jnp.bfloat16)


def compress(col_basis, modes):
    rank, panels = col_basis.shape
    cols = modes.shape[1]
    count = panels // CS
    return pl.pallas_call(
        compress_kernel,
        grid=(count // COMPRESS,),
        in_specs=[
            pl.BlockSpec((rank, COMPRESS * CS), lambda r: (0, r)),
            pl.BlockSpec((COMPRESS * CS, cols), lambda r: (r, 0)),
        ],
        out_specs=[
            pl.BlockSpec((COMPRESS, rank, cols), lambda r: (r, 0, 0)),
            pl.BlockSpec((NH * CS, cols), lambda r: (0, 0)),
            pl.BlockSpec((NH * CS, cols), lambda r: (0, 0)),
        ],
        out_shape=[
            jax.ShapeDtypeStruct((count, rank, cols), jnp.bfloat16),
            jax.ShapeDtypeStruct((NH * CS, cols), jnp.bfloat16),
            jax.ShapeDtypeStruct((NH * CS, cols), jnp.bfloat16),
        ],
        compiler_params=pltpu.CompilerParams(vmem_limit_bytes=58 * MIB),
        cost_estimate=pl.CostEstimate(
            flops=2 * rank * panels * cols, bytes_accessed=3 * MIB, transcendentals=0
        ),
        name="compress",
    )(col_basis, modes)


def dispatch_kernel(
    cols, slots, cl_dev, rows_ref, owners_ref, slot_ref, cores_ref, out_ref, count_ref, meta_ref
):
    blocks, rows, _ = cores_ref.shape
    out_ref[...] = jnp.zeros_like(out_ref)
    meta_ref[...] = jnp.zeros_like(meta_ref)
    lane = lax.broadcasted_iota(jnp.int32, (1, 128), 1)
    for j in range(cols):
        count_ref[j] = 0

    def place(b, carry):
        owner = owners_ref[b]
        column = owner % cols
        at = count_ref[column]
        count_ref[column] = at + 1
        out_ref[column, pl.ds(pl.multiple_of(at * rows, rows), rows), :] = cores_ref[b]
        cluster = (owner // cols) * cl_dev + slot_ref[b]
        entry = (
            jnp.where(lane == at, cluster, 0)
            + jnp.where(lane == slots + at, rows_ref[b], 0)
            + jnp.where(lane == 2 * slots, 1, 0)
        )
        meta_ref[pl.ds(column, 1), :] += entry.astype(jnp.float32)
        return carry

    lax.fori_loop(0, blocks, place, 0)
    for j in range(cols):
        out_ref[j, slots * rows :, :] = jnp.broadcast_to(
            meta_ref[j : j + 1, :], (16, 128)
        ).astype(jnp.bfloat16)


def dispatch(block_rows, owners, block_slot, cores, cols, slots, cl_dev):
    blocks, rows, _ = cores.shape
    return pl.pallas_call(
        functools.partial(dispatch_kernel, cols, slots, cl_dev),
        in_specs=[whole(SMEM), whole(SMEM), whole(SMEM), whole()],
        out_specs=whole(),
        out_shape=jax.ShapeDtypeStruct((cols, slots * rows + 16, 128), jnp.bfloat16),
        scratch_shapes=[SMEM((cols,), jnp.int32), VMEM((cols, 128), jnp.float32)],
        compiler_params=pltpu.CompilerParams(vmem_limit_bytes=16 * MIB),
        cost_estimate=pl.CostEstimate(flops=4 * MIB, bytes_accessed=3 * MIB, transcendentals=0),
        name="dispatch",
    )(block_rows, owners, block_slot, cores)


UNROLL = 8


def far_kernel(
    slots, rows, x_first, comp_ref, sent_ref, up_ref, down_ref, next_ref, last_ref, own_ref,
    acc_ref, meta_ref, smem_ref, list_ref, sem,
):
    sources = sent_ref.shape[0]
    group_rows = acc_ref.shape[0]
    part = group_rows // 4
    me = lax.axis_index("ccol")
    here_x, here_z = me // 4, me % 4

    acc_ref[...] = jnp.zeros_like(acc_ref)
    meta = sent_ref[:, slots * rows : slots * rows + 16, :].astype(jnp.float32)
    meta_ref[...] = jnp.max(meta, axis=1).astype(jnp.int32)
    copy = pltpu.make_async_copy(meta_ref, smem_ref, sem)
    copy.start()
    copy.wait()

    def source(i, total):
        def entry(p, total):
            row = smem_ref[i, slots + p]
            to_x = (row // part - here_x + 4) % 4
            to_z = (row // (part // 4) % 4 - here_z + 4) % 4
            first, second = (to_x, to_z) if x_first else (to_z, to_x)
            at = first * part + second * (part // 4) + row % (part // 4)
            list_ref[total] = ((i * slots + p) << 16) + (smem_ref[i, p] << 8) + at
            return total + 1

        return lax.fori_loop(0, smem_ref[i, 2 * slots], entry, total)

    total = lax.fori_loop(0, sources, source, 0)
    for i in range(UNROLL):
        list_ref[total + i] = 0

    def group(g, carry):
        terms = []
        for i in range(UNROLL):
            at = g * UNROLL + i
            entry = list_ref[at]
            place = entry >> 16
            core = sent_ref[place // slots, pl.ds(pl.multiple_of((place % slots) * rows, rows), rows), :]
            core = jnp.where(at < total, core, jnp.zeros_like(core))
            half = core.shape[1] // 2
            core = jnp.concatenate([core[:, :half], core[:, half:]], axis=0)
            comp = comp_ref[(entry >> 8) & 255]
            terms.append((entry & 255, jnp.dot(core, comp, preferred_element_type=jnp.float32)))
        for row, term in terms:
            acc_ref[row] += term
        return carry

    lax.fori_loop(0, (total + UNROLL - 1) // UNROLL, group, 0)
    half = part // 2
    own_ref[...] = acc_ref[:part]
    next_ref[...] = acc_ref[part : part + half]
    up_ref[half:] = acc_ref[part + half : 2 * part].astype(jnp.bfloat16)
    up_ref[:half] = acc_ref[2 * part : 2 * part + half].astype(jnp.bfloat16)
    down_ref[half:] = acc_ref[2 * part + half : 3 * part].astype(jnp.bfloat16)
    down_ref[:half] = acc_ref[3 * part : 3 * part + half].astype(jnp.bfloat16)
    last_ref[...] = acc_ref[3 * part + half :]


def far_field(comp, sent, slots, rows, group_rows, x_first):
    clusters, rank, cols = comp.shape
    sources = sent.shape[0]
    width = cols // 2
    chunk = 0 if x_first else 1
    part = group_rows // 4
    kinds = [
        (part, jnp.bfloat16),
        (part, jnp.bfloat16),
        (part // 2, jnp.float32),
        (part // 2, jnp.float32),
        (part, jnp.float32),
    ]
    return pl.pallas_call(
        functools.partial(far_kernel, slots, rows, x_first),
        grid=(1,),
        in_specs=[
            pl.BlockSpec((clusters, rank, width), lambda m: (0, 0, chunk)),
            pl.BlockSpec(sent.shape, lambda m: (0, 0, 0)),
        ],
        out_specs=[pl.BlockSpec((n, rank, width), lambda m: (0, 0, 0)) for n, _ in kinds],
        out_shape=[jax.ShapeDtypeStruct((n, rank, width), kind) for n, kind in kinds],
        scratch_shapes=[
            VMEM((group_rows, rank, width), jnp.float32),
            VMEM((sources, 128), jnp.int32),
            SMEM((sources, 128), jnp.int32),
            SMEM((sources * slots + UNROLL,), jnp.int32),
            pltpu.SemaphoreType.DMA,
        ],
        compiler_params=pltpu.CompilerParams(vmem_limit_bytes=58 * MIB),
        cost_estimate=pl.CostEstimate(
            flops=2 * 128 * rank * rank * width * 8, bytes_accessed=12 * MIB, transcendentals=0
        ),
        name="far_x" if x_first else "far_z",
    )(comp, sent)


def ring(axis_is_x, step):
    def to(i):
        x, z = i // 4, i % 4
        return ((x + step) % 4) * 4 + z if axis_is_x else x * 4 + (z + step) % 4

    return [(i, to(i)) for i in range(16)]


def f32(value):
    return value.astype(jnp.float32)


def both_ways(up, down, along_x):
    return lax.ppermute(up, "ccol", ring(along_x, 1)), lax.ppermute(down, "ccol", ring(along_x, -1))


SMALL = pl.CostEstimate(flops=0, bytes_accessed=0, transcendentals=0)


def pass_kernel(following_ref, last_ref, up_ref, down_ref, up_out_ref, down_out_ref):
    half = following_ref.shape[0]
    up_out_ref[...] = (following_ref[...] + f32(up_ref[:half])).astype(jnp.bfloat16)
    down_out_ref[...] = (last_ref[...] + f32(down_ref[half:])).astype(jnp.bfloat16)


def passed_on(following, last, up, down):
    shape = jax.ShapeDtypeStruct(following.shape, jnp.bfloat16)
    return pl.pallas_call(
        pass_kernel,
        in_specs=[whole()] * 4,
        out_specs=[whole()] * 2,
        out_shape=[shape] * 2,
        compiler_params=pltpu.CompilerParams(vmem_limit_bytes=24 * MIB),
        cost_estimate=SMALL,
        name="passed_on",
    )(following, last, up, down)


def ring_sum(place, own, up_ref, down_ref, up_rest_ref, down_rest_ref):
    half = up_rest_ref.shape[0]
    if place < half:
        return own + f32(down_ref[place]) + f32(up_rest_ref[place])
    return own + f32(up_ref[place]) + f32(down_rest_ref[place - half])


def turn_kernel(own_ref, *refs):
    arrived, (up_ref, down_ref, next_ref, last_ref, here_ref) = refs[:4], refs[4:]
    part = here_ref.shape[0]
    half = part // 2
    for place in range(4 * part):
        value = ring_sum(place, own_ref[place], *arrived)
        kind, at = place // part, place % part
        if kind == 0:
            here_ref[at] = value
        elif kind == 1 and at < half:
            next_ref[at] = value
        elif kind == 1:
            up_ref[at] = value.astype(jnp.bfloat16)
        elif kind == 2 and at < half:
            up_ref[at] = value.astype(jnp.bfloat16)
        elif kind == 2:
            down_ref[at] = value.astype(jnp.bfloat16)
        elif at < half:
            down_ref[at] = value.astype(jnp.bfloat16)
        else:
            last_ref[at - half] = value


def turn(own, up, down, up_rest, down_rest):
    rows, rank, width = own.shape
    part = rows // 4
    kinds = [
        (part, jnp.bfloat16),
        (part, jnp.bfloat16),
        (part // 2, jnp.float32),
        (part // 2, jnp.float32),
        (part, jnp.float32),
    ]
    return pl.pallas_call(
        turn_kernel,
        in_specs=[whole()] * 5,
        out_specs=[whole()] * 5,
        out_shape=[jax.ShapeDtypeStruct((n, rank, width), kind) for n, kind in kinds],
        compiler_params=pltpu.CompilerParams(vmem_limit_bytes=24 * MIB),
        cost_estimate=SMALL,
        name="turn",
    )(own, up, down, up_rest, down_rest)


def second_stage(parts, along_x):
    up, down, following, last, own = parts
    up, down = both_ways(up, down, along_x)
    return own, up, down, *both_ways(*passed_on(following, last, up, down), along_x)


def near_kernel(near_ref, before_ref, modes_ref, after_ref, basis_ref, out_ref, turned_ref, ext_ref):
    r = pl.program_id(0)
    halo, panels = before_ref.shape[0], modes_ref.shape[0]
    rank = basis_ref.shape[0]

    @pl.when(r == 0)
    def _():
        ext_ref[:halo] = before_ref[...]
        ext_ref[halo : halo + panels] = modes_ref[...]
        ext_ref[halo + panels :] = after_ref[...]

    window = ext_ref[pl.ds(pl.multiple_of(r * CS, CS), NEAR * CS), :]
    out_ref[...] = jnp.dot(near_ref[...], window, preferred_element_type=jnp.float32)
    have = lax.broadcasted_iota(jnp.int32, (rank, rank), 0)
    want = lax.broadcasted_iota(jnp.int32, (rank, rank), 1)
    order = jnp.where(want < rank // 2, 2 * want, 2 * want - rank + 1)
    select = jnp.where(order == have, 1.0, 0.0).astype(jnp.bfloat16)
    turned_ref[...] = lax.dot_general(
        basis_ref[...], select, (((0,), (0,)), ((), ())), preferred_element_type=jnp.float32
    ).astype(jnp.bfloat16)


def near_field(near_blocks, before, modes, after, row_basis):
    panels, band = near_blocks.shape
    cols = modes.shape[1]
    halo = before.shape[0]
    rank = row_basis.shape[0]
    return pl.pallas_call(
        near_kernel,
        grid=(panels // CS,),
        in_specs=[pl.BlockSpec((CS, band), lambda r: (r, 0))]
        + [whole()] * 3
        + [pl.BlockSpec((rank, CS), lambda r: (0, r))],
        out_specs=[
            pl.BlockSpec((CS, cols), lambda r: (r, 0)),
            pl.BlockSpec((CS, rank), lambda r: (r, 0)),
        ],
        out_shape=[
            jax.ShapeDtypeStruct((panels, cols), jnp.float32),
            jax.ShapeDtypeStruct((panels, rank), jnp.bfloat16),
        ],
        scratch_shapes=[VMEM((panels + 2 * halo, cols), jnp.bfloat16)],
        compiler_params=pltpu.CompilerParams(vmem_limit_bytes=58 * MIB),
        cost_estimate=pl.CostEstimate(
            flops=16 * panels * band * cols, bytes_accessed=18 * MIB, transcendentals=0
        ),
        name="near_field",
    )(near_blocks, before, modes, after, row_basis)


EXPAND = 2


def expand_kernel(near_ref, basis_ref, *refs):
    halves, out_ref = (refs[:5], refs[5:10]), refs[10]
    clusters, _, width = halves[0][0].shape
    step = pl.program_id(0)
    for group in range(clusters // EXPAND):

        @pl.when(step == group)
        def _():
            for i in range(EXPAND):
                rows = pl.ds(i * CS, CS)
                for side, half in enumerate(halves):
                    place = group * EXPAND + i
                    far = ring_sum(place, half[0][place], *half[1:]).astype(jnp.bfloat16)
                    cols = pl.ds(side * width, width)
                    value = jnp.dot(basis_ref[rows, :], far, preferred_element_type=jnp.float32)
                    out_ref[rows, cols] = (near_ref[rows, cols] + value).astype(jnp.bfloat16)


def expand(near, basis, left, right):
    panels, cols = near.shape
    rank = basis.shape[1]
    return pl.pallas_call(
        expand_kernel,
        grid=(panels // CS // EXPAND,),
        in_specs=[
            pl.BlockSpec((EXPAND * CS, cols), lambda r: (r, 0)),
            pl.BlockSpec((EXPAND * CS, rank), lambda r: (r, 0)),
        ]
        + [pl.BlockSpec(v.shape, lambda r: (0, 0, 0)) for v in (*left, *right)],
        out_specs=pl.BlockSpec((EXPAND * CS, cols), lambda r: (r, 0)),
        out_shape=jax.ShapeDtypeStruct((panels, cols), jnp.bfloat16),
        compiler_params=pltpu.CompilerParams(vmem_limit_bytes=24 * MIB),
        cost_estimate=pl.CostEstimate(
            flops=2 * panels * rank * cols, bytes_accessed=7 * MIB, transcendentals=0
        ),
        name="expand",
    )(near, basis, *left, *right)


def per_device(modes, col_basis, row_basis, near_blocks, block_rows, block_owner, block_slot, cores):
    row_devices, col_devices = lax.axis_size("crow"), lax.axis_size("ccol")
    devices = row_devices * col_devices
    cluster_count = modes.shape[0] // CS
    rank = col_basis.shape[0]
    blocks = cores.shape[0]
    slots = CAP * row_devices

    compressed, low, high = compress(col_basis, modes)
    gathered = lax.all_gather(compressed, "crow", axis=0, tiled=True)

    lines = rank * rank // 128
    sent = dispatch(
        block_rows, block_owner[:, 0], block_slot, cores.reshape(blocks, lines, 128),
        col_devices, slots, cluster_count,
    )
    sent = lax.all_to_all(sent, "ccol", split_axis=0, concat_axis=0, tiled=True)

    low, high, sent = lax.optimization_barrier((low, high, sent))
    up = [(i, i + 1) for i in range(devices - 1)]
    down = [(j, i) for i, j in up]
    before = lax.ppermute(high, ("crow", "ccol"), up)
    after = lax.ppermute(low, ("crow", "ccol"), down)

    group_rows = col_devices * cluster_count
    left = list(far_field(gathered, sent, slots, lines, group_rows, True))
    gathered, sent, left[0] = lax.optimization_barrier((gathered, sent, left[0]))
    right = list(far_field(gathered, sent, slots, lines, group_rows, False))
    right[0], before, after = lax.optimization_barrier((right[0], before, after))

    left_up, left_down = both_ways(left[0], left[1], True)
    right_up, right_down = both_ways(right[0], right[1], False)
    left_up, left_down, before, after = lax.optimization_barrier((left_up, left_down, before, after))
    left_rest = both_ways(*passed_on(left[2], left[3], left_up, left_down), True)
    near, basis = near_field(near_blocks, before, modes, after, row_basis)
    right_up, right_down, near, basis = lax.optimization_barrier((right_up, right_down, near, basis))
    right_rest = passed_on(right[2], right[3], right_up, right_down)
    left_rest, _ = lax.optimization_barrier((left_rest, right_rest))
    right_rest = both_ways(*right_rest, False)
    left = second_stage(turn(left[4], left_up, left_down, *left_rest), False)
    left, right_rest = lax.optimization_barrier((left, right_rest))
    right = second_stage(turn(right[4], right_up, right_down, *right_rest), True)
    return expand(near, basis, left, right)


def solution(mesh):
    both = ("crow", "ccol")
    in_specs = (
        P(both, None),
        P(None, both),
        P(None, both),
        P(both, None),
        P(both),
        P(both, None),
        P(both),
        P(both, None),
    )
    return jax.shard_map(
        per_device, mesh=mesh, in_specs=in_specs, out_specs=P(both, None), check_vma=False
    )
```

```python
import functools

import jax
import jax.numpy as jnp
from jax import lax
from jax.experimental import pallas as pl
from jax.experimental.pallas import tpu as pltpu
from jax.sharding import PartitionSpec as P

CS = 256
NH = 4
NEAR = 9
CAP = 2
MIB = 1 << 20
VMEM = pltpu.VMEM
SMEM = pltpu.SMEM


def whole(space=VMEM):
    return pl.BlockSpec(memory_space=space)


COMPRESS = 4


def compress_kernel(basis_ref, modes_ref, out_ref, low_ref, high_ref):
    step = pl.program_id(0)

    @pl.when(step == 0)
    def _():
        low_ref[...] = modes_ref[: NH * CS, :]

    @pl.when(step == pl.num_programs(0) - 1)
    def _():
        high_ref[...] = modes_ref[(COMPRESS - NH) * CS :, :]

    for i in range(COMPRESS):
        out_ref[i] = jnp.dot(
            basis_ref[:, i * CS : (i + 1) * CS],
            modes_ref[i * CS : (i + 1) * CS, :],
            preferred_element_type=jnp.float32,
        ).astype(jnp.bfloat16)


def compress(col_basis, modes):
    rank, panels = col_basis.shape
    cols = modes.shape[1]
    count = panels // CS
    return pl.pallas_call(
        compress_kernel,
        grid=(count // COMPRESS,),
        in_specs=[
            pl.BlockSpec((rank, COMPRESS * CS), lambda r: (0, r)),
            pl.BlockSpec((COMPRESS * CS, cols), lambda r: (r, 0)),
        ],
        out_specs=[
            pl.BlockSpec((COMPRESS, rank, cols), lambda r: (r, 0, 0)),
            pl.BlockSpec((NH * CS, cols), lambda r: (0, 0)),
            pl.BlockSpec((NH * CS, cols), lambda r: (0, 0)),
        ],
        out_shape=[
            jax.ShapeDtypeStruct((count, rank, cols), jnp.bfloat16),
            jax.ShapeDtypeStruct((NH * CS, cols), jnp.bfloat16),
            jax.ShapeDtypeStruct((NH * CS, cols), jnp.bfloat16),
        ],
        compiler_params=pltpu.CompilerParams(vmem_limit_bytes=58 * MIB),
        cost_estimate=pl.CostEstimate(
            flops=2 * rank * panels * cols, bytes_accessed=3 * MIB, transcendentals=0
        ),
        name="compress",
    )(col_basis, modes)


def dispatch_kernel(
    cols, slots, cl_dev, rows_ref, owners_ref, slot_ref, cores_ref, out_ref, count_ref, meta_ref
):
    blocks, rows, _ = cores_ref.shape
    out_ref[...] = jnp.zeros_like(out_ref)
    meta_ref[...] = jnp.zeros_like(meta_ref)
    lane = lax.broadcasted_iota(jnp.int32, (1, 128), 1)
    for j in range(cols):
        count_ref[j] = 0

    def place(b, carry):
        owner = owners_ref[b]
        column = owner % cols
        at = count_ref[column]
        count_ref[column] = at + 1
        out_ref[column, pl.ds(pl.multiple_of(at * rows, rows), rows), :] = cores_ref[b]
        cluster = (owner // cols) * cl_dev + slot_ref[b]
        entry = (
            jnp.where(lane == at, cluster, 0)
            + jnp.where(lane == slots + at, rows_ref[b], 0)
            + jnp.where(lane == 2 * slots, 1, 0)
        )
        meta_ref[pl.ds(column, 1), :] += entry.astype(jnp.float32)
        return carry

    lax.fori_loop(0, blocks, place, 0)
    for j in range(cols):
        out_ref[j, slots * rows :, :] = jnp.broadcast_to(
            meta_ref[j : j + 1, :], (16, 128)
        ).astype(jnp.bfloat16)


def dispatch(block_rows, owners, block_slot, cores, cols, slots, cl_dev):
    blocks, rows, _ = cores.shape
    return pl.pallas_call(
        functools.partial(dispatch_kernel, cols, slots, cl_dev),
        in_specs=[whole(SMEM), whole(SMEM), whole(SMEM), whole()],
        out_specs=whole(),
        out_shape=jax.ShapeDtypeStruct((cols, slots * rows + 16, 128), jnp.bfloat16),
        scratch_shapes=[SMEM((cols,), jnp.int32), VMEM((cols, 128), jnp.float32)],
        compiler_params=pltpu.CompilerParams(vmem_limit_bytes=16 * MIB),
        cost_estimate=pl.CostEstimate(flops=4 * MIB, bytes_accessed=3 * MIB, transcendentals=0),
        name="dispatch",
    )(block_rows, owners, block_slot, cores)


UNROLL = 8


def far_kernel(
    slots, rows, x_first, comp_ref, sent_ref, up_ref, down_ref, next_ref, last_ref, own_ref,
    acc_ref, meta_ref, smem_ref, list_ref, sem,
):
    sources = sent_ref.shape[0]
    group_rows = acc_ref.shape[0]
    part = group_rows // 4
    me = lax.axis_index("ccol")
    here_x, here_z = me // 4, me % 4

    acc_ref[...] = jnp.zeros_like(acc_ref)
    meta = sent_ref[:, slots * rows : slots * rows + 16, :].astype(jnp.float32)
    meta_ref[...] = jnp.max(meta, axis=1).astype(jnp.int32)
    copy = pltpu.make_async_copy(meta_ref, smem_ref, sem)
    copy.start()
    copy.wait()

    def source(i, total):
        def entry(p, total):
            row = smem_ref[i, slots + p]
            to_x = (row // part - here_x + 4) % 4
            to_z = (row // (part // 4) % 4 - here_z + 4) % 4
            first, second = (to_x, to_z) if x_first else (to_z, to_x)
            at = first * part + second * (part // 4) + row % (part // 4)
            list_ref[total] = ((i * slots + p) << 16) + (smem_ref[i, p] << 8) + at
            return total + 1

        return lax.fori_loop(0, smem_ref[i, 2 * slots], entry, total)

    total = lax.fori_loop(0, sources, source, 0)
    for i in range(UNROLL):
        list_ref[total + i] = 0

    def group(g, carry):
        terms = []
        for i in range(UNROLL):
            at = g * UNROLL + i
            entry = list_ref[at]
            place = entry >> 16
            core = sent_ref[place // slots, pl.ds(pl.multiple_of((place % slots) * rows, rows), rows), :]
            core = jnp.where(at < total, core, jnp.zeros_like(core))
            half = core.shape[1] // 2
            core = jnp.concatenate([core[:, :half], core[:, half:]], axis=0)
            comp = comp_ref[(entry >> 8) & 255]
            terms.append((entry & 255, jnp.dot(core, comp, preferred_element_type=jnp.float32)))
        for row, term in terms:
            acc_ref[row] += term
        return carry

    lax.fori_loop(0, (total + UNROLL - 1) // UNROLL, group, 0)
    half = part // 2
    own_ref[...] = acc_ref[:part]
    next_ref[...] = acc_ref[part : part + half]
    up_ref[half:] = acc_ref[part + half : 2 * part].astype(jnp.bfloat16)
    up_ref[:half] = acc_ref[2 * part : 2 * part + half].astype(jnp.bfloat16)
    down_ref[half:] = acc_ref[2 * part + half : 3 * part].astype(jnp.bfloat16)
    down_ref[:half] = acc_ref[3 * part : 3 * part + half].astype(jnp.bfloat16)
    last_ref[...] = acc_ref[3 * part + half :]


def far_field(comp, sent, slots, rows, group_rows, x_first):
    clusters, rank, cols = comp.shape
    sources = sent.shape[0]
    width = cols // 2
    chunk = 0 if x_first else 1
    part = group_rows // 4
    kinds = [
        (part, jnp.bfloat16),
        (part, jnp.bfloat16),
        (part // 2, jnp.float32),
        (part // 2, jnp.float32),
        (part, jnp.float32),
    ]
    return pl.pallas_call(
        functools.partial(far_kernel, slots, rows, x_first),
        grid=(1,),
        in_specs=[
            pl.BlockSpec((clusters, rank, width), lambda m: (0, 0, chunk)),
            pl.BlockSpec(sent.shape, lambda m: (0, 0, 0)),
        ],
        out_specs=[pl.BlockSpec((n, rank, width), lambda m: (0, 0, 0)) for n, _ in kinds],
        out_shape=[jax.ShapeDtypeStruct((n, rank, width), kind) for n, kind in kinds],
        scratch_shapes=[
            VMEM((group_rows, rank, width), jnp.float32),
            VMEM((sources, 128), jnp.int32),
            SMEM((sources, 128), jnp.int32),
            SMEM((sources * slots + UNROLL,), jnp.int32),
            pltpu.SemaphoreType.DMA,
        ],
        compiler_params=pltpu.CompilerParams(vmem_limit_bytes=40 * MIB),
        cost_estimate=pl.CostEstimate(
            flops=2 * 128 * rank * rank * width * 8, bytes_accessed=12 * MIB, transcendentals=0
        ),
        name="far_x" if x_first else "far_z",
    )(comp, sent)


def ring(axis_is_x, step):
    def to(i):
        x, z = i // 4, i % 4
        return ((x + step) % 4) * 4 + z if axis_is_x else x * 4 + (z + step) % 4

    return [(i, to(i)) for i in range(16)]


def f32(value):
    return value.astype(jnp.float32)


def both_ways(up, down, along_x):
    return lax.ppermute(up, "ccol", ring(along_x, 1)), lax.ppermute(down, "ccol", ring(along_x, -1))


SMALL = pl.CostEstimate(flops=0, bytes_accessed=0, transcendentals=0)


def pass_kernel(following_ref, last_ref, up_ref, down_ref, up_out_ref, down_out_ref):
    half = following_ref.shape[0]
    up_out_ref[...] = (following_ref[...] + f32(up_ref[:half])).astype(jnp.bfloat16)
    down_out_ref[...] = (last_ref[...] + f32(down_ref[half:])).astype(jnp.bfloat16)


def passed_on(following, last, up, down):
    shape = jax.ShapeDtypeStruct(following.shape, jnp.bfloat16)
    return pl.pallas_call(
        pass_kernel,
        in_specs=[whole()] * 4,
        out_specs=[whole()] * 2,
        out_shape=[shape] * 2,
        compiler_params=pltpu.CompilerParams(vmem_limit_bytes=24 * MIB),
        cost_estimate=SMALL,
        name="passed_on",
    )(following, last, up, down)


def ring_sum(place, own, up_ref, down_ref, up_rest_ref, down_rest_ref):
    half = up_rest_ref.shape[0]
    if place < half:
        return own + f32(down_ref[place]) + f32(up_rest_ref[place])
    return own + f32(up_ref[place]) + f32(down_rest_ref[place - half])


def turn_kernel(own_ref, *refs):
    arrived, (up_ref, down_ref, next_ref, last_ref, here_ref) = refs[:4], refs[4:]
    part = here_ref.shape[0]
    half = part // 2
    for place in range(4 * part):
        value = ring_sum(place, own_ref[place], *arrived)
        kind, at = place // part, place % part
        if kind == 0:
            here_ref[at] = value
        elif kind == 1 and at < half:
            next_ref[at] = value
        elif kind == 1:
            up_ref[at] = value.astype(jnp.bfloat16)
        elif kind == 2 and at < half:
            up_ref[at] = value.astype(jnp.bfloat16)
        elif kind == 2:
            down_ref[at] = value.astype(jnp.bfloat16)
        elif at < half:
            down_ref[at] = value.astype(jnp.bfloat16)
        else:
            last_ref[at - half] = value


def turn(own, up, down, up_rest, down_rest):
    rows, rank, width = own.shape
    part = rows // 4
    kinds = [
        (part, jnp.bfloat16),
        (part, jnp.bfloat16),
        (part // 2, jnp.float32),
        (part // 2, jnp.float32),
        (part, jnp.float32),
    ]
    return pl.pallas_call(
        turn_kernel,
        in_specs=[whole()] * 5,
        out_specs=[whole()] * 5,
        out_shape=[jax.ShapeDtypeStruct((n, rank, width), kind) for n, kind in kinds],
        compiler_params=pltpu.CompilerParams(vmem_limit_bytes=24 * MIB),
        cost_estimate=SMALL,
        name="turn",
    )(own, up, down, up_rest, down_rest)


def near_kernel(near_ref, before_ref, modes_ref, after_ref, basis_ref, out_ref, turned_ref, ext_ref):
    r = pl.program_id(0)
    halo, panels = before_ref.shape[0], modes_ref.shape[0]
    rank = basis_ref.shape[0]

    @pl.when(r == 0)
    def _():
        ext_ref[:halo] = before_ref[...]
        ext_ref[halo : halo + panels] = modes_ref[...]
        ext_ref[halo + panels :] = after_ref[...]

    window = ext_ref[pl.ds(pl.multiple_of(r * CS, CS), NEAR * CS), :]
    out_ref[...] = jnp.dot(near_ref[...], window, preferred_element_type=jnp.float32)
    have = lax.broadcasted_iota(jnp.int32, (rank, rank), 0)
    want = lax.broadcasted_iota(jnp.int32, (rank, rank), 1)
    order = jnp.where(want < rank // 2, 2 * want, 2 * want - rank + 1)
    select = jnp.where(order == have, 1.0, 0.0).astype(jnp.bfloat16)
    turned_ref[...] = lax.dot_general(
        basis_ref[...], select, (((0,), (0,)), ((), ())), preferred_element_type=jnp.float32
    ).astype(jnp.bfloat16)


def near_field(near_blocks, before, modes, after, row_basis):
    panels, band = near_blocks.shape
    cols = modes.shape[1]
    halo = before.shape[0]
    rank = row_basis.shape[0]
    return pl.pallas_call(
        near_kernel,
        grid=(panels // CS,),
        in_specs=[pl.BlockSpec((CS, band), lambda r: (r, 0))]
        + [whole()] * 3
        + [pl.BlockSpec((rank, CS), lambda r: (0, r))],
        out_specs=[
            pl.BlockSpec((CS, cols), lambda r: (r, 0)),
            pl.BlockSpec((CS, rank), lambda r: (r, 0)),
        ],
        out_shape=[
            jax.ShapeDtypeStruct((panels, cols), jnp.float32),
            jax.ShapeDtypeStruct((panels, rank), jnp.bfloat16),
        ],
        scratch_shapes=[VMEM((panels + 2 * halo, cols), jnp.bfloat16)],
        compiler_params=pltpu.CompilerParams(vmem_limit_bytes=32 * MIB),
        cost_estimate=pl.CostEstimate(
            flops=16 * panels * band * cols, bytes_accessed=18 * MIB, transcendentals=0
        ),
        name="near_field",
    )(near_blocks, before, modes, after, row_basis)


EXPAND = 2


def expand_kernel(near_ref, basis_ref, *refs):
    halves, out_ref = (refs[:5], refs[5:10]), refs[10]
    clusters, _, width = halves[0][0].shape
    step = pl.program_id(0)
    for group in range(clusters // EXPAND):

        @pl.when(step == group)
        def _():
            for i in range(EXPAND):
                rows = pl.ds(i * CS, CS)
                for side, half in enumerate(halves):
                    place = group * EXPAND + i
                    far = ring_sum(place, half[0][place], *half[1:]).astype(jnp.bfloat16)
                    cols = pl.ds(side * width, width)
                    value = jnp.dot(basis_ref[rows, :], far, preferred_element_type=jnp.float32)
                    out_ref[rows, cols] = (near_ref[rows, cols] + value).astype(jnp.bfloat16)


def expand(near, basis, left, right):
    panels, cols = near.shape
    rank = basis.shape[1]
    return pl.pallas_call(
        expand_kernel,
        grid=(panels // CS // EXPAND,),
        in_specs=[
            pl.BlockSpec((EXPAND * CS, cols), lambda r: (r, 0)),
            pl.BlockSpec((EXPAND * CS, rank), lambda r: (r, 0)),
        ]
        + [pl.BlockSpec(v.shape, lambda r: (0, 0, 0)) for v in (*left, *right)],
        out_specs=pl.BlockSpec((EXPAND * CS, cols), lambda r: (r, 0)),
        out_shape=jax.ShapeDtypeStruct((panels, cols), jnp.bfloat16),
        compiler_params=pltpu.CompilerParams(vmem_limit_bytes=24 * MIB),
        cost_estimate=pl.CostEstimate(
            flops=2 * panels * rank * cols, bytes_accessed=7 * MIB, transcendentals=0
        ),
        name="expand",
    )(near, basis, *left, *right)


def per_device(modes, col_basis, row_basis, near_blocks, block_rows, block_owner, block_slot, cores):
    row_devices, col_devices = lax.axis_size("crow"), lax.axis_size("ccol")
    devices = row_devices * col_devices
    cluster_count = modes.shape[0] // CS
    rank = col_basis.shape[0]
    blocks = cores.shape[0]
    slots = CAP * row_devices

    compressed, low, high = compress(col_basis, modes)
    gathered = lax.all_gather(compressed, "crow", axis=0, tiled=True)

    lines = rank * rank // 128
    sent = dispatch(
        block_rows, block_owner[:, 0], block_slot, cores.reshape(blocks, lines, 128),
        col_devices, slots, cluster_count,
    )
    sent = lax.all_to_all(sent, "ccol", split_axis=0, concat_axis=0, tiled=True)

    low, high, sent = lax.optimization_barrier((low, high, sent))
    up = [(i, i + 1) for i in range(devices - 1)]
    down = [(j, i) for i, j in up]
    before = lax.ppermute(high, ("crow", "ccol"), up)
    after = lax.ppermute(low, ("crow", "ccol"), down)

    group_rows = col_devices * cluster_count
    left = list(far_field(gathered, sent, slots, lines, group_rows, True))
    gathered, sent, left[0] = lax.optimization_barrier((gathered, sent, left[0]))
    right = list(far_field(gathered, sent, slots, lines, group_rows, False))
    right[0], before, after = lax.optimization_barrier((right[0], before, after))

    left_up, left_down = both_ways(left[0], left[1], True)
    right_up, right_down = both_ways(right[0], right[1], False)
    left_up, left_down, before, after = lax.optimization_barrier((left_up, left_down, before, after))
    left_rest = both_ways(*passed_on(left[2], left[3], left_up, left_down), True)
    near, basis = near_field(near_blocks, before, modes, after, row_basis)
    right_up, right_down, near, basis = lax.optimization_barrier((right_up, right_down, near, basis))
    right_rest = passed_on(right[2], right[3], right_up, right_down)
    left_rest, _ = lax.optimization_barrier((left_rest, right_rest))
    right_rest = both_ways(*right_rest, False)
    left = turn(left[4], left_up, left_down, *left_rest)
    left_up, left_down = both_ways(left[0], left[1], False)
    right = turn(right[4], right_up, right_down, *right_rest)
    right_up, right_down = both_ways(right[0], right[1], True)
    (left_up, left_down), _ = lax.optimization_barrier(((left_up, left_down), right))
    left_rest = both_ways(*passed_on(left[2], left[3], left_up, left_down), False)
    right_rest = both_ways(*passed_on(right[2], right[3], right_up, right_down), True)
    left = (left[4], left_up, left_down, *left_rest)
    right = (right[4], right_up, right_down, *right_rest)
    return expand(near, basis, left, right)


def solution(mesh):
    both = ("crow", "ccol")
    in_specs = (
        P(both, None),
        P(None, both),
        P(None, both),
        P(both, None),
        P(both),
        P(both, None),
        P(both),
        P(both, None),
    )
    return jax.shard_map(
        per_device, mesh=mesh, in_specs=in_specs, out_specs=P(both, None), check_vma=False
    )
```

```python
import functools

import jax
import jax.numpy as jnp
from jax import lax
from jax.experimental import pallas as pl
from jax.experimental.pallas import tpu as pltpu
from jax.sharding import PartitionSpec as P

CS = 256
NH = 4
NEAR = 9
CAP = 2
MIB = 1 << 20
VMEM = pltpu.VMEM
SMEM = pltpu.SMEM


def whole(space=VMEM):
    return pl.BlockSpec(memory_space=space)


COMPRESS = 4


def compress_kernel(basis_ref, modes_ref, out_ref, low_ref, high_ref):
    step = pl.program_id(0)

    @pl.when(step == 0)
    def _():
        low_ref[...] = modes_ref[: NH * CS, :]

    @pl.when(step == pl.num_programs(0) - 1)
    def _():
        high_ref[...] = modes_ref[(COMPRESS - NH) * CS :, :]

    for i in range(COMPRESS):
        out_ref[i] = jnp.dot(
            basis_ref[:, i * CS : (i + 1) * CS],
            modes_ref[i * CS : (i + 1) * CS, :],
            preferred_element_type=jnp.float32,
        ).astype(jnp.bfloat16)


def compress(col_basis, modes):
    rank, panels = col_basis.shape
    cols = modes.shape[1]
    count = panels // CS
    return pl.pallas_call(
        compress_kernel,
        grid=(count // COMPRESS,),
        in_specs=[
            pl.BlockSpec((rank, COMPRESS * CS), lambda r: (0, r)),
            pl.BlockSpec((COMPRESS * CS, cols), lambda r: (r, 0)),
        ],
        out_specs=[
            pl.BlockSpec((COMPRESS, rank, cols), lambda r: (r, 0, 0)),
            pl.BlockSpec((NH * CS, cols), lambda r: (0, 0)),
            pl.BlockSpec((NH * CS, cols), lambda r: (0, 0)),
        ],
        out_shape=[
            jax.ShapeDtypeStruct((count, rank, cols), jnp.bfloat16),
            jax.ShapeDtypeStruct((NH * CS, cols), jnp.bfloat16),
            jax.ShapeDtypeStruct((NH * CS, cols), jnp.bfloat16),
        ],
        compiler_params=pltpu.CompilerParams(vmem_limit_bytes=58 * MIB),
        cost_estimate=pl.CostEstimate(
            flops=2 * rank * panels * cols, bytes_accessed=3 * MIB, transcendentals=0
        ),
        name="compress",
    )(col_basis, modes)


def dispatch_kernel(
    cols, slots, cl_dev, rows_ref, owners_ref, slot_ref, cores_ref, out_ref, count_ref, meta_ref
):
    blocks, rows, _ = cores_ref.shape
    out_ref[...] = jnp.zeros_like(out_ref)
    meta_ref[...] = jnp.zeros_like(meta_ref)
    lane = lax.broadcasted_iota(jnp.int32, (1, 128), 1)
    for j in range(cols):
        count_ref[j] = 0

    def place(b, carry):
        owner = owners_ref[b]
        column = owner % cols
        at = count_ref[column]
        count_ref[column] = at + 1
        out_ref[column, pl.ds(pl.multiple_of(at * rows, rows), rows), :] = cores_ref[b]
        cluster = (owner // cols) * cl_dev + slot_ref[b]
        entry = (
            jnp.where(lane == at, cluster, 0)
            + jnp.where(lane == slots + at, rows_ref[b], 0)
            + jnp.where(lane == 2 * slots, 1, 0)
        )
        meta_ref[pl.ds(column, 1), :] += entry.astype(jnp.float32)
        return carry

    lax.fori_loop(0, blocks, place, 0)
    for j in range(cols):
        out_ref[j, slots * rows :, :] = jnp.broadcast_to(
            meta_ref[j : j + 1, :], (16, 128)
        ).astype(jnp.bfloat16)


def dispatch(block_rows, owners, block_slot, cores, cols, slots, cl_dev):
    blocks, rows, _ = cores.shape
    return pl.pallas_call(
        functools.partial(dispatch_kernel, cols, slots, cl_dev),
        in_specs=[whole(SMEM), whole(SMEM), whole(SMEM), whole()],
        out_specs=whole(),
        out_shape=jax.ShapeDtypeStruct((cols, slots * rows + 16, 128), jnp.bfloat16),
        scratch_shapes=[SMEM((cols,), jnp.int32), VMEM((cols, 128), jnp.float32)],
        compiler_params=pltpu.CompilerParams(vmem_limit_bytes=16 * MIB),
        cost_estimate=pl.CostEstimate(flops=4 * MIB, bytes_accessed=3 * MIB, transcendentals=0),
        name="dispatch",
    )(block_rows, owners, block_slot, cores)


UNROLL = 32


def far_kernel(slots, rows, comp_ref, sent_ref, *refs):
    outs, (left_ref, right_ref, meta_ref, smem_ref, list_ref, sem) = (refs[:5], refs[5:10]), refs[10:]
    sources = sent_ref.shape[0]
    group_rows, _, width = left_ref.shape
    part = group_rows // 4
    row_part = part // 4
    me = lax.axis_index("ccol")
    here_x, here_z = me // 4, me % 4

    meta = sent_ref[:, slots * rows : slots * rows + 16, :].astype(jnp.float32)
    meta = jnp.max(meta, axis=1).astype(jnp.int32)
    lane = lax.broadcasted_iota(jnp.int32, meta.shape, 1)
    row = pltpu.roll(meta, 128 - slots, axis=1) & (group_rows - 1)
    to_x = (row // part - here_x) & 3
    to_z = (row // row_part - here_z) & 3
    rest = row & (row_part - 1)
    left = to_x * part + to_z * row_part + rest
    right = to_z * part + to_x * row_part + rest
    place = lax.broadcasted_iota(jnp.int32, meta.shape, 0) * slots + lane
    words = (place << 22) + (meta << 14) + (left << 7) + right
    meta_ref[...] = jnp.where(lane < slots, words, meta)
    copy = pltpu.make_async_copy(meta_ref, smem_ref, sem)
    copy.start()
    left_ref[...] = jnp.zeros_like(left_ref)
    right_ref[...] = jnp.zeros_like(right_ref)
    copy.wait()

    total = 0
    for i in range(sources):
        for p in range(slots):
            list_ref[total + p] = smem_ref[i, p]
        total = total + smem_ref[i, 2 * slots]
    for i in range(UNROLL):
        list_ref[total + i] = 0

    def group(g, carry):
        for i in range(UNROLL):
            at = g * UNROLL + i
            entry = list_ref[at]
            place = entry >> 22
            core = sent_ref[place // slots, pl.ds(pl.multiple_of((place % slots) * rows, rows), rows), :]
            core = jnp.where(at < total, core, jnp.zeros_like(core))
            half = core.shape[1] // 2
            core = jnp.concatenate([core[:, :half], core[:, half:]], axis=0)
            comp = comp_ref[(entry >> 14) & 255]
            left_ref[(entry >> 7) & 127] += jnp.dot(core, comp[:, :width], preferred_element_type=jnp.float32)
            right_ref[entry & 127] += jnp.dot(core, comp[:, width:], preferred_element_type=jnp.float32)
        return carry

    lax.fori_loop(0, (total + UNROLL - 1) // UNROLL, group, 0)
    half = part // 2
    for acc_ref, (up_ref, down_ref, next_ref, last_ref, own_ref) in zip((left_ref, right_ref), outs):
        own_ref[...] = acc_ref[:part]
        next_ref[...] = acc_ref[part : part + half]
        up_ref[half:] = acc_ref[part + half : 2 * part].astype(jnp.bfloat16)
        up_ref[:half] = acc_ref[2 * part : 2 * part + half].astype(jnp.bfloat16)
        down_ref[half:] = acc_ref[2 * part + half : 3 * part].astype(jnp.bfloat16)
        down_ref[:half] = acc_ref[3 * part : 3 * part + half].astype(jnp.bfloat16)
        last_ref[...] = acc_ref[3 * part + half :]


def far_field(comp, sent, slots, rows, group_rows):
    _, rank, cols = comp.shape
    sources = sent.shape[0]
    width = cols // 2
    part = group_rows // 4
    kinds = [
        (part, jnp.bfloat16),
        (part, jnp.bfloat16),
        (part // 2, jnp.float32),
        (part // 2, jnp.float32),
        (part, jnp.float32),
    ] * 2
    parts = pl.pallas_call(
        functools.partial(far_kernel, slots, rows),
        in_specs=[whole()] * 2,
        out_specs=[whole()] * len(kinds),
        out_shape=[jax.ShapeDtypeStruct((n, rank, width), kind) for n, kind in kinds],
        scratch_shapes=[
            VMEM((group_rows, rank, width), jnp.float32),
            VMEM((group_rows, rank, width), jnp.float32),
            VMEM((sources, 128), jnp.int32),
            SMEM((sources, 128), jnp.int32),
            SMEM((sources * slots + UNROLL + slots,), jnp.int32),
            pltpu.SemaphoreType.DMA,
        ],
        compiler_params=pltpu.CompilerParams(vmem_limit_bytes=40 * MIB),
        cost_estimate=pl.CostEstimate(
            flops=2 * 128 * rank * rank * cols * 8, bytes_accessed=24 * MIB, transcendentals=0
        ),
        name="far_field",
    )(comp, sent)
    return parts[:5], parts[5:]


def ring(axis_is_x, step):
    def to(i):
        x, z = i // 4, i % 4
        return ((x + step) % 4) * 4 + z if axis_is_x else x * 4 + (z + step) % 4

    return [(i, to(i)) for i in range(16)]


def f32(value):
    return value.astype(jnp.float32)


def both_ways(up, down, along_x):
    return lax.ppermute(up, "ccol", ring(along_x, 1)), lax.ppermute(down, "ccol", ring(along_x, -1))


SMALL = pl.CostEstimate(flops=0, bytes_accessed=0, transcendentals=0)


def pass_kernel(following_ref, last_ref, up_ref, down_ref, up_out_ref, down_out_ref):
    half = following_ref.shape[0]
    up_out_ref[...] = (following_ref[...] + f32(up_ref[:half])).astype(jnp.bfloat16)
    down_out_ref[...] = (last_ref[...] + f32(down_ref[half:])).astype(jnp.bfloat16)


def passed_on(following, last, up, down):
    shape = jax.ShapeDtypeStruct(following.shape, jnp.bfloat16)
    return pl.pallas_call(
        pass_kernel,
        in_specs=[whole()] * 4,
        out_specs=[whole()] * 2,
        out_shape=[shape] * 2,
        compiler_params=pltpu.CompilerParams(vmem_limit_bytes=24 * MIB),
        cost_estimate=SMALL,
        name="passed_on",
    )(following, last, up, down)


def ring_sum(place, own, up_ref, down_ref, up_rest_ref, down_rest_ref):
    half = up_rest_ref.shape[0]
    if place < half:
        return own + f32(down_ref[place]) + f32(up_rest_ref[place])
    return own + f32(up_ref[place]) + f32(down_rest_ref[place - half])


def turn_kernel(own_ref, *refs):
    arrived, (up_ref, down_ref, next_ref, last_ref, here_ref) = refs[:4], refs[4:]
    part = here_ref.shape[0]
    half = part // 2
    for place in range(4 * part):
        value = ring_sum(place, own_ref[place], *arrived)
        kind, at = place // part, place % part
        if kind == 0:
            here_ref[at] = value
        elif kind == 1 and at < half:
            next_ref[at] = value
        elif kind == 1:
            up_ref[at] = value.astype(jnp.bfloat16)
        elif kind == 2 and at < half:
            up_ref[at] = value.astype(jnp.bfloat16)
        elif kind == 2:
            down_ref[at] = value.astype(jnp.bfloat16)
        elif at < half:
            down_ref[at] = value.astype(jnp.bfloat16)
        else:
            last_ref[at - half] = value


def turn(own, up, down, up_rest, down_rest):
    rows, rank, width = own.shape
    part = rows // 4
    kinds = [
        (part, jnp.bfloat16),
        (part, jnp.bfloat16),
        (part // 2, jnp.float32),
        (part // 2, jnp.float32),
        (part, jnp.float32),
    ]
    return pl.pallas_call(
        turn_kernel,
        in_specs=[whole()] * 5,
        out_specs=[whole()] * 5,
        out_shape=[jax.ShapeDtypeStruct((n, rank, width), kind) for n, kind in kinds],
        compiler_params=pltpu.CompilerParams(vmem_limit_bytes=24 * MIB),
        cost_estimate=SMALL,
        name="turn",
    )(own, up, down, up_rest, down_rest)


def near_kernel(near_ref, before_ref, modes_ref, after_ref, basis_ref, out_ref, turned_ref, ext_ref):
    r = pl.program_id(0)
    halo, panels = before_ref.shape[0], modes_ref.shape[0]
    rank = basis_ref.shape[0]

    @pl.when(r == 0)
    def _():
        ext_ref[:halo] = before_ref[...]
        ext_ref[halo : halo + panels] = modes_ref[...]
        ext_ref[halo + panels :] = after_ref[...]

    window = ext_ref[pl.ds(pl.multiple_of(r * CS, CS), NEAR * CS), :]
    out_ref[...] = jnp.dot(near_ref[...], window, preferred_element_type=jnp.float32)
    have = lax.broadcasted_iota(jnp.int32, (rank, rank), 0)
    want = lax.broadcasted_iota(jnp.int32, (rank, rank), 1)
    order = jnp.where(want < rank // 2, 2 * want, 2 * want - rank + 1)
    select = jnp.where(order == have, 1.0, 0.0).astype(jnp.bfloat16)
    turned_ref[...] = lax.dot_general(
        basis_ref[...], select, (((0,), (0,)), ((), ())), preferred_element_type=jnp.float32
    ).astype(jnp.bfloat16)


def near_field(near_blocks, before, modes, after, row_basis):
    panels, band = near_blocks.shape
    cols = modes.shape[1]
    halo = before.shape[0]
    rank = row_basis.shape[0]
    return pl.pallas_call(
        near_kernel,
        grid=(panels // CS,),
        in_specs=[pl.BlockSpec((CS, band), lambda r: (r, 0))]
        + [whole()] * 3
        + [pl.BlockSpec((rank, CS), lambda r: (0, r))],
        out_specs=[
            pl.BlockSpec((CS, cols), lambda r: (r, 0)),
            pl.BlockSpec((CS, rank), lambda r: (r, 0)),
        ],
        out_shape=[
            jax.ShapeDtypeStruct((panels, cols), jnp.float32),
            jax.ShapeDtypeStruct((panels, rank), jnp.bfloat16),
        ],
        scratch_shapes=[VMEM((panels + 2 * halo, cols), jnp.bfloat16)],
        compiler_params=pltpu.CompilerParams(vmem_limit_bytes=32 * MIB),
        cost_estimate=pl.CostEstimate(
            flops=16 * panels * band * cols, bytes_accessed=18 * MIB, transcendentals=0
        ),
        name="near_field",
    )(near_blocks, before, modes, after, row_basis)


EXPAND = 2


def expand_kernel(near_ref, basis_ref, *refs):
    halves, out_ref = (refs[:5], refs[5:10]), refs[10]
    clusters, _, width = halves[0][0].shape
    step = pl.program_id(0)
    for group in range(clusters // EXPAND):

        @pl.when(step == group)
        def _():
            for i in range(EXPAND):
                rows = pl.ds(i * CS, CS)
                for side, half in enumerate(halves):
                    place = group * EXPAND + i
                    far = ring_sum(place, half[0][place], *half[1:]).astype(jnp.bfloat16)
                    cols = pl.ds(side * width, width)
                    value = jnp.dot(basis_ref[rows, :], far, preferred_element_type=jnp.float32)
                    out_ref[rows, cols] = (near_ref[rows, cols] + value).astype(jnp.bfloat16)


def expand(near, basis, left, right):
    panels, cols = near.shape
    rank = basis.shape[1]
    return pl.pallas_call(
        expand_kernel,
        grid=(panels // CS // EXPAND,),
        in_specs=[
            pl.BlockSpec((EXPAND * CS, cols), lambda r: (r, 0)),
            pl.BlockSpec((EXPAND * CS, rank), lambda r: (r, 0)),
        ]
        + [pl.BlockSpec(v.shape, lambda r: (0, 0, 0)) for v in (*left, *right)],
        out_specs=pl.BlockSpec((EXPAND * CS, cols), lambda r: (r, 0)),
        out_shape=jax.ShapeDtypeStruct((panels, cols), jnp.bfloat16),
        compiler_params=pltpu.CompilerParams(vmem_limit_bytes=24 * MIB),
        cost_estimate=pl.CostEstimate(
            flops=2 * panels * rank * cols, bytes_accessed=7 * MIB, transcendentals=0
        ),
        name="expand",
    )(near, basis, *left, *right)


def per_device(modes, col_basis, row_basis, near_blocks, block_rows, block_owner, block_slot, cores):
    row_devices, col_devices = lax.axis_size("crow"), lax.axis_size("ccol")
    devices = row_devices * col_devices
    cluster_count = modes.shape[0] // CS
    rank = col_basis.shape[0]
    blocks = cores.shape[0]
    slots = CAP * row_devices

    compressed, low, high = compress(col_basis, modes)
    gathered = lax.all_gather(compressed, "crow", axis=0, tiled=True)

    lines = rank * rank // 128
    sent = dispatch(
        block_rows, block_owner[:, 0], block_slot, cores.reshape(blocks, lines, 128),
        col_devices, slots, cluster_count,
    )
    sent = lax.all_to_all(sent, "ccol", split_axis=0, concat_axis=0, tiled=True)

    low, high, sent = lax.optimization_barrier((low, high, sent))
    up = [(i, i + 1) for i in range(devices - 1)]
    down = [(j, i) for i, j in up]
    before = lax.ppermute(high, ("crow", "ccol"), up)
    after = lax.ppermute(low, ("crow", "ccol"), down)

    left, right = far_field(gathered, sent, slots, lines, col_devices * cluster_count)
    for along_x in (True, False):
        left_up, left_down = both_ways(left[0], left[1], along_x)
        right_up, right_down = both_ways(right[0], right[1], not along_x)
        if along_x:
            (before, after), _ = lax.optimization_barrier(((before, after), left[0]))
            near, basis = near_field(near_blocks, before, modes, after, row_basis)
            (left_up, left_down), _ = lax.optimization_barrier(((left_up, left_down), near))
        left_rest = passed_on(left[2], left[3], left_up, left_down)
        right_rest = passed_on(right[2], right[3], right_up, right_down)
        left_rest = both_ways(*left_rest, along_x)
        right_rest = both_ways(*right_rest, not along_x)
        left = (left[4], left_up, left_down, *left_rest)
        right = (right[4], right_up, right_down, *right_rest)
        if along_x:
            left, right = turn(*left), turn(*right)
    return expand(near, basis, left, right)


def solution(mesh):
    both = ("crow", "ccol")
    in_specs = (
        P(both, None),
        P(None, both),
        P(None, both),
        P(both, None),
        P(both),
        P(both, None),
        P(both),
        P(both, None),
    )
    return jax.shard_map(
        per_device, mesh=mesh, in_specs=in_specs, out_specs=P(both, None), check_vma=False
    )
```

```python
import functools

import jax
import jax.numpy as jnp
from jax import lax
from jax.experimental import pallas as pl
from jax.experimental.pallas import tpu as pltpu
from jax.sharding import PartitionSpec as P

CS = 256
NH = 4
NEAR = 9
CAP = 2
MIB = 1 << 20
VMEM = pltpu.VMEM
SMEM = pltpu.SMEM


def whole(space=VMEM):
    return pl.BlockSpec(memory_space=space)


COMPRESS = 4


def compress_kernel(basis_ref, modes_ref, out_ref, low_ref, high_ref):
    step = pl.program_id(0)

    @pl.when(step == 0)
    def _():
        low_ref[...] = modes_ref[: NH * CS, :]

    @pl.when(step == pl.num_programs(0) - 1)
    def _():
        high_ref[...] = modes_ref[(COMPRESS - NH) * CS :, :]

    for i in range(COMPRESS):
        out_ref[i] = jnp.dot(
            basis_ref[:, i * CS : (i + 1) * CS],
            modes_ref[i * CS : (i + 1) * CS, :],
            preferred_element_type=jnp.float32,
        ).astype(jnp.bfloat16)


def compress(col_basis, modes):
    rank, panels = col_basis.shape
    cols = modes.shape[1]
    count = panels // CS
    return pl.pallas_call(
        compress_kernel,
        grid=(count // COMPRESS,),
        in_specs=[
            pl.BlockSpec((rank, COMPRESS * CS), lambda r: (0, r)),
            pl.BlockSpec((COMPRESS * CS, cols), lambda r: (r, 0)),
        ],
        out_specs=[
            pl.BlockSpec((COMPRESS, rank, cols), lambda r: (r, 0, 0)),
            pl.BlockSpec((NH * CS, cols), lambda r: (0, 0)),
            pl.BlockSpec((NH * CS, cols), lambda r: (0, 0)),
        ],
        out_shape=[
            jax.ShapeDtypeStruct((count, rank, cols), jnp.bfloat16),
            jax.ShapeDtypeStruct((NH * CS, cols), jnp.bfloat16),
            jax.ShapeDtypeStruct((NH * CS, cols), jnp.bfloat16),
        ],
        compiler_params=pltpu.CompilerParams(vmem_limit_bytes=58 * MIB),
        cost_estimate=pl.CostEstimate(
            flops=2 * rank * panels * cols, bytes_accessed=3 * MIB, transcendentals=0
        ),
        name="compress",
    )(col_basis, modes)


def dispatch_kernel(
    cols, slots, cl_dev, rows_ref, owners_ref, slot_ref, cores_ref, out_ref, count_ref, meta_ref
):
    blocks, rows, _ = cores_ref.shape
    out_ref[...] = jnp.zeros_like(out_ref)
    meta_ref[...] = jnp.zeros_like(meta_ref)
    lane = lax.broadcasted_iota(jnp.int32, (1, 128), 1)
    for j in range(cols):
        count_ref[j] = 0

    def place(b, carry):
        owner = owners_ref[b]
        column = owner & (cols - 1)
        at = count_ref[column]
        count_ref[column] = at + 1
        out_ref[column, pl.ds(pl.multiple_of(at * rows, rows), rows), :] = cores_ref[b]
        cluster = (owner >> (cols.bit_length() - 1)) * cl_dev + slot_ref[b]
        entry = (
            jnp.where(lane == at, cluster, 0)
            + jnp.where(lane == slots + at, rows_ref[b], 0)
            + jnp.where(lane == 2 * slots, 1, 0)
        )
        meta_ref[pl.ds(column, 1), :] += entry.astype(jnp.float32)
        return carry

    lax.fori_loop(0, blocks, place, 0, unroll=8)
    for j in range(cols):
        out_ref[j, slots * rows :, :] = jnp.broadcast_to(
            meta_ref[j : j + 1, :], (16, 128)
        ).astype(jnp.bfloat16)


def dispatch(block_rows, owners, block_slot, cores, cols, slots, cl_dev):
    blocks, rows, _ = cores.shape
    return pl.pallas_call(
        functools.partial(dispatch_kernel, cols, slots, cl_dev),
        in_specs=[whole(SMEM), whole(SMEM), whole(SMEM), whole()],
        out_specs=whole(),
        out_shape=jax.ShapeDtypeStruct((cols, slots * rows + 16, 128), jnp.bfloat16),
        scratch_shapes=[SMEM((cols,), jnp.int32), VMEM((cols, 128), jnp.float32)],
        compiler_params=pltpu.CompilerParams(vmem_limit_bytes=16 * MIB),
        cost_estimate=pl.CostEstimate(flops=4 * MIB, bytes_accessed=3 * MIB, transcendentals=0),
        name="dispatch",
    )(block_rows, owners, block_slot, cores)


UNROLL = 32
X_ROWS = 5


def far_kernel(slots, rows, comp_ref, sent_ref, *refs):
    outs, (acc_ref, meta_ref, smem_ref, list_ref, sem) = (refs[:5], refs[5:10]), refs[10:]
    sources = sent_ref.shape[0]
    group_rows = acc_ref.shape[0]
    part = group_rows // 4
    row_part = part // 4
    me = lax.axis_index("ccol")
    here_x, here_z = me // 4, me % 4

    meta = sent_ref[:, slots * rows : slots * rows + 16, :].astype(jnp.float32)
    meta = jnp.max(meta, axis=1).astype(jnp.int32)
    lane = lax.broadcasted_iota(jnp.int32, meta.shape, 1)
    row = pltpu.roll(meta, 128 - slots, axis=1) & (group_rows - 1)
    to_x = (row // part - here_x) & 3
    to_z = (row // row_part - here_z) & 3
    rest = row & (row_part - 1)
    z_rows = row_part - X_ROWS
    x_place = (to_x * 4 + to_z) * X_ROWS + rest
    z_place = 16 * X_ROWS + (to_z * 4 + to_x) * z_rows + rest - X_ROWS
    filed = jnp.where(rest < X_ROWS, x_place, z_place)
    place = lax.broadcasted_iota(jnp.int32, meta.shape, 0) * slots + lane
    words = (place << 14) + (meta << 7) + filed
    meta_ref[...] = jnp.where(lane < slots, words, meta)
    copy = pltpu.make_async_copy(meta_ref, smem_ref, sem)
    copy.start()
    acc_ref[...] = jnp.zeros_like(acc_ref)
    copy.wait()

    total = 0
    for i in range(sources):
        for p in range(slots):
            list_ref[total + p] = smem_ref[i, p]
        total = total + smem_ref[i, 2 * slots]
    for i in range(UNROLL):
        list_ref[total + i] = 0

    def group(g, carry):
        for i in range(UNROLL):
            at = g * UNROLL + i
            entry = list_ref[at]
            place = entry >> 14
            core = sent_ref[place // slots, pl.ds(pl.multiple_of((place % slots) * rows, rows), rows), :]
            core = jnp.where(at < total, core, jnp.zeros_like(core))
            half = core.shape[1] // 2
            core = jnp.concatenate([core[:, :half], core[:, half:]], axis=0)
            comp = comp_ref[(entry >> 7) & 127]
            acc_ref[entry & 127] += jnp.dot(core, comp, preferred_element_type=jnp.float32)
        return carry

    lax.fori_loop(0, (total + UNROLL - 1) // UNROLL, group, 0)
    begin = 0
    for up_ref, down_ref, next_ref, last_ref, own_ref in outs:
        part = own_ref.shape[0]
        half = part // 2
        own, following, far, last, begin = (begin + i * part for i in range(5))
        own_ref[...] = acc_ref[own : own + part]
        next_ref[...] = acc_ref[following : following + half]
        up_ref[half:] = acc_ref[following + half : following + part].astype(jnp.bfloat16)
        up_ref[:half] = acc_ref[far : far + half].astype(jnp.bfloat16)
        down_ref[half:] = acc_ref[far + half : far + part].astype(jnp.bfloat16)
        down_ref[:half] = acc_ref[last : last + half].astype(jnp.bfloat16)
        last_ref[...] = acc_ref[last + half : last + part]


def far_field(comp, sent, slots, rows, group_rows):
    _, rank, cols = comp.shape
    sources = sent.shape[0]
    x_part = X_ROWS * 4
    kinds = [
        (n, kind)
        for part in (x_part, group_rows // 4 - x_part)
        for n, kind in (
            (part, jnp.bfloat16),
            (part, jnp.bfloat16),
            (part // 2, jnp.float32),
            (part // 2, jnp.float32),
            (part, jnp.float32),
        )
    ]
    parts = pl.pallas_call(
        functools.partial(far_kernel, slots, rows),
        in_specs=[whole()] * 2,
        out_specs=[whole()] * len(kinds),
        out_shape=[jax.ShapeDtypeStruct((n, rank, cols), kind) for n, kind in kinds],
        scratch_shapes=[
            VMEM((group_rows, rank, cols), jnp.float32),
            VMEM((sources, 128), jnp.int32),
            SMEM((sources, 128), jnp.int32),
            SMEM((sources * slots + UNROLL + slots,), jnp.int32),
            pltpu.SemaphoreType.DMA,
        ],
        compiler_params=pltpu.CompilerParams(vmem_limit_bytes=40 * MIB),
        cost_estimate=pl.CostEstimate(
            flops=2 * 128 * rank * rank * cols * 8, bytes_accessed=24 * MIB, transcendentals=0
        ),
        name="far_field",
    )(comp, sent)
    return parts[:5], parts[5:]


def ring(axis_is_x, step):
    def to(i):
        x, z = i // 4, i % 4
        return ((x + step) % 4) * 4 + z if axis_is_x else x * 4 + (z + step) % 4

    return [(i, to(i)) for i in range(16)]


def f32(value):
    return value.astype(jnp.float32)


def both_ways(up, down, along_x):
    return lax.ppermute(up, "ccol", ring(along_x, 1)), lax.ppermute(down, "ccol", ring(along_x, -1))


SMALL = pl.CostEstimate(flops=0, bytes_accessed=0, transcendentals=0)


def pass_kernel(following_ref, last_ref, up_ref, down_ref, up_out_ref, down_out_ref):
    half = following_ref.shape[0]
    up_out_ref[...] = (following_ref[...] + f32(up_ref[:half])).astype(jnp.bfloat16)
    down_out_ref[...] = (last_ref[...] + f32(down_ref[half:])).astype(jnp.bfloat16)


def passed_on(following, last, up, down):
    shape = jax.ShapeDtypeStruct(following.shape, jnp.bfloat16)
    return pl.pallas_call(
        pass_kernel,
        in_specs=[whole()] * 4,
        out_specs=[whole()] * 2,
        out_shape=[shape] * 2,
        compiler_params=pltpu.CompilerParams(vmem_limit_bytes=24 * MIB),
        cost_estimate=SMALL,
        name="passed_on",
    )(following, last, up, down)


def turn_kernel(own_ref, up_in_ref, down_in_ref, up_rest_ref, down_rest_ref, up_ref, down_ref, next_ref, last_ref, here_ref):
    part, _, width = next_ref.shape
    half = up_rest_ref.shape[0]

    def total(kind):
        at = kind * part
        rows = pl.ds(at, part)
        if at < half:
            return own_ref[rows] + f32(down_in_ref[rows]) + f32(up_rest_ref[rows])
        return own_ref[rows] + f32(up_in_ref[rows]) + f32(down_rest_ref[pl.ds(at - half, part)])

    here_ref[...] = total(0)
    following, far, last = total(1), total(2), total(3)
    next_ref[...] = following[:, :, :width]
    up_ref[part:] = following[:, :, width:].astype(jnp.bfloat16)
    up_ref[:part] = far[:, :, :width].astype(jnp.bfloat16)
    down_ref[part:] = far[:, :, width:].astype(jnp.bfloat16)
    down_ref[:part] = last[:, :, :width].astype(jnp.bfloat16)
    last_ref[...] = last[:, :, width:]


def turn(own, up, down, up_rest, down_rest):
    rows, rank, cols = own.shape
    part, width = rows // 4, cols // 2
    kinds = [
        (2 * part, width, jnp.bfloat16),
        (2 * part, width, jnp.bfloat16),
        (part, width, jnp.float32),
        (part, width, jnp.float32),
        (part, cols, jnp.float32),
    ]
    return pl.pallas_call(
        turn_kernel,
        in_specs=[whole()] * 5,
        out_specs=[whole()] * 5,
        out_shape=[jax.ShapeDtypeStruct((n, rank, w), kind) for n, w, kind in kinds],
        compiler_params=pltpu.CompilerParams(vmem_limit_bytes=24 * MIB),
        cost_estimate=SMALL,
        name="turn",
    )(own, up, down, up_rest, down_rest)


def near_kernel(near_ref, before_ref, modes_ref, after_ref, basis_ref, out_ref, turned_ref, ext_ref):
    r = pl.program_id(0)
    halo, panels = before_ref.shape[0], modes_ref.shape[0]
    rank = basis_ref.shape[0]

    @pl.when(r == 0)
    def _():
        ext_ref[:halo] = before_ref[...]
        ext_ref[halo : halo + panels] = modes_ref[...]
        ext_ref[halo + panels :] = after_ref[...]

    window = ext_ref[pl.ds(pl.multiple_of(r * CS, CS), NEAR * CS), :]
    out_ref[...] = jnp.dot(near_ref[...], window, preferred_element_type=jnp.float32)
    have = lax.broadcasted_iota(jnp.int32, (rank, rank), 0)
    want = lax.broadcasted_iota(jnp.int32, (rank, rank), 1)
    order = jnp.where(want < rank // 2, 2 * want, 2 * want - rank + 1)
    select = jnp.where(order == have, 1.0, 0.0).astype(jnp.bfloat16)
    turned_ref[...] = lax.dot_general(
        basis_ref[...], select, (((0,), (0,)), ((), ())), preferred_element_type=jnp.float32
    ).astype(jnp.bfloat16)


def near_field(near_blocks, before, modes, after, row_basis):
    panels, band = near_blocks.shape
    cols = modes.shape[1]
    halo = before.shape[0]
    rank = row_basis.shape[0]
    return pl.pallas_call(
        near_kernel,
        grid=(panels // CS,),
        in_specs=[pl.BlockSpec((CS, band), lambda r: (r, 0))]
        + [whole()] * 3
        + [pl.BlockSpec((rank, CS), lambda r: (0, r))],
        out_specs=[
            pl.BlockSpec((CS, cols), lambda r: (r, 0)),
            pl.BlockSpec((CS, rank), lambda r: (r, 0)),
        ],
        out_shape=[
            jax.ShapeDtypeStruct((panels, cols), jnp.float32),
            jax.ShapeDtypeStruct((panels, rank), jnp.bfloat16),
        ],
        scratch_shapes=[VMEM((panels + 2 * halo, cols), jnp.bfloat16)],
        compiler_params=pltpu.CompilerParams(vmem_limit_bytes=32 * MIB),
        cost_estimate=pl.CostEstimate(
            flops=2 * panels * band * cols, bytes_accessed=2 * MIB, transcendentals=0
        ),
        name="near_field",
    )(near_blocks, before, modes, after, row_basis)


EXPAND = 2


def expand_kernel(near_ref, basis_ref, *refs):
    sides, out_ref = (refs[:5], refs[5:10]), refs[10]
    places = [(side, at) for side in sides for at in range(side[0].shape[0])]
    width = sides[0][3].shape[2]
    step = pl.program_id(0)
    for group in range(len(places) // EXPAND):

        @pl.when(step == group)
        def _():
            for i in range(EXPAND):
                rows = pl.ds(i * CS, CS)
                (own_ref, up_ref, down_ref, up_rest_ref, down_rest_ref), at = places[group * EXPAND + i]
                part = own_ref.shape[0]
                own = own_ref[at]
                first = own[:, :width] + f32(down_ref[at]) + f32(up_rest_ref[at])
                second = own[:, width:] + f32(up_ref[part + at]) + f32(down_rest_ref[at])
                for far, cols in ((first, pl.ds(0, width)), (second, pl.ds(width, width))):
                    value = jnp.dot(basis_ref[rows, :], far.astype(jnp.bfloat16), preferred_element_type=jnp.float32)
                    out_ref[rows, cols] = (near_ref[rows, cols] + value).astype(jnp.bfloat16)


def expand(near, basis, left, right):
    panels, cols = near.shape
    rank = basis.shape[1]
    return pl.pallas_call(
        expand_kernel,
        grid=(panels // CS // EXPAND,),
        in_specs=[
            pl.BlockSpec((EXPAND * CS, cols), lambda r: (r, 0)),
            pl.BlockSpec((EXPAND * CS, rank), lambda r: (r, 0)),
        ]
        + [pl.BlockSpec(v.shape, lambda r: (0, 0, 0)) for v in (*left, *right)],
        out_specs=pl.BlockSpec((EXPAND * CS, cols), lambda r: (r, 0)),
        out_shape=jax.ShapeDtypeStruct((panels, cols), jnp.bfloat16),
        compiler_params=pltpu.CompilerParams(vmem_limit_bytes=24 * MIB),
        cost_estimate=pl.CostEstimate(
            flops=2 * panels * rank * cols, bytes_accessed=7 * MIB, transcendentals=0
        ),
        name="expand",
    )(near, basis, *left, *right)


def per_device(modes, col_basis, row_basis, near_blocks, block_rows, block_owner, block_slot, cores):
    row_devices, col_devices = lax.axis_size("crow"), lax.axis_size("ccol")
    devices = row_devices * col_devices
    cluster_count = modes.shape[0] // CS
    rank = col_basis.shape[0]
    blocks = cores.shape[0]
    slots = CAP * row_devices

    compressed, low, high = compress(col_basis, modes)
    gathered = lax.all_gather(compressed, "crow", axis=0, tiled=True)

    lines = rank * rank // 128
    sent = dispatch(
        block_rows, block_owner[:, 0], block_slot, cores.reshape(blocks, lines, 128),
        col_devices, slots, cluster_count,
    )
    sent = lax.all_to_all(sent, "ccol", split_axis=0, concat_axis=0, tiled=True)

    low, high, sent = lax.optimization_barrier((low, high, sent))
    up = [(i, i + 1) for i in range(devices - 1)]
    down = [(j, i) for i, j in up]
    before = lax.ppermute(high, ("crow", "ccol"), up)
    after = lax.ppermute(low, ("crow", "ccol"), down)

    left, right = far_field(gathered, sent, slots, lines, col_devices * cluster_count)
    for along_x in (True, False):
        left_up, left_down = both_ways(left[0], left[1], along_x)
        right_up, right_down = both_ways(right[0], right[1], not along_x)
        if along_x:
            (before, after), _ = lax.optimization_barrier(((before, after), left[0]))
            near, basis = near_field(near_blocks, before, modes, after, row_basis)
            (left_up, left_down), _ = lax.optimization_barrier(((left_up, left_down), near))
        left_rest = passed_on(left[2], left[3], left_up, left_down)
        right_rest = passed_on(right[2], right[3], right_up, right_down)
        left_rest = both_ways(*left_rest, along_x)
        right_rest = both_ways(*right_rest, not along_x)
        left = (left[4], left_up, left_down, *left_rest)
        right = (right[4], right_up, right_down, *right_rest)
        if along_x:
            left, right = turn(*left), turn(*right)
    return expand(near, basis, left, right)


def solution(mesh):
    both = ("crow", "ccol")
    in_specs = (
        P(both, None),
        P(None, both),
        P(None, both),
        P(both, None),
        P(both),
        P(both, None),
        P(both),
        P(both, None),
    )
    return jax.shard_map(
        per_device, mesh=mesh, in_specs=in_specs, out_specs=P(both, None), check_vma=False
    )
```

```python
import functools

import jax
import jax.numpy as jnp
from jax import lax
from jax.experimental import pallas as pl
from jax.experimental.pallas import tpu as pltpu
from jax.sharding import PartitionSpec as P

CS = 256
NH = 4
NEAR = 9
CAP = 2
MIB = 1 << 20
VMEM = pltpu.VMEM
SMEM = pltpu.SMEM


def whole(space=VMEM):
    return pl.BlockSpec(memory_space=space)


COMPRESS = 4


def compress_kernel(basis_ref, modes_ref, out_ref, low_ref, high_ref):
    step = pl.program_id(0)

    @pl.when(step == 0)
    def _():
        low_ref[...] = modes_ref[: NH * CS, :]

    @pl.when(step == pl.num_programs(0) - 1)
    def _():
        high_ref[...] = modes_ref[(COMPRESS - NH) * CS :, :]

    for i in range(COMPRESS):
        out_ref[i] = jnp.dot(
            basis_ref[:, i * CS : (i + 1) * CS],
            modes_ref[i * CS : (i + 1) * CS, :],
            preferred_element_type=jnp.float32,
        ).astype(jnp.bfloat16)


def compress(col_basis, modes):
    rank, panels = col_basis.shape
    cols = modes.shape[1]
    count = panels // CS
    return pl.pallas_call(
        compress_kernel,
        grid=(count // COMPRESS,),
        in_specs=[
            pl.BlockSpec((rank, COMPRESS * CS), lambda r: (0, r)),
            pl.BlockSpec((COMPRESS * CS, cols), lambda r: (r, 0)),
        ],
        out_specs=[
            pl.BlockSpec((COMPRESS, rank, cols), lambda r: (r, 0, 0)),
            pl.BlockSpec((NH * CS, cols), lambda r: (0, 0)),
            pl.BlockSpec((NH * CS, cols), lambda r: (0, 0)),
        ],
        out_shape=[
            jax.ShapeDtypeStruct((count, rank, cols), jnp.bfloat16),
            jax.ShapeDtypeStruct((NH * CS, cols), jnp.bfloat16),
            jax.ShapeDtypeStruct((NH * CS, cols), jnp.bfloat16),
        ],
        compiler_params=pltpu.CompilerParams(vmem_limit_bytes=58 * MIB),
        cost_estimate=pl.CostEstimate(
            flops=2 * rank * panels * cols, bytes_accessed=3 * MIB, transcendentals=0
        ),
        name="compress",
    )(col_basis, modes)


def dispatch_kernel(
    cols, slots, cl_dev, rows_ref, owners_ref, slot_ref, cores_ref, out_ref, count_ref, meta_ref
):
    blocks, rows, _ = cores_ref.shape
    out_ref[...] = jnp.zeros_like(out_ref)
    meta_ref[...] = jnp.zeros_like(meta_ref)
    lane = lax.broadcasted_iota(jnp.int32, (1, 128), 1)
    for j in range(cols):
        count_ref[j] = 0

    def place(b, carry):
        owner = owners_ref[b]
        column = owner & (cols - 1)
        at = count_ref[column]
        count_ref[column] = at + 1
        out_ref[column, pl.ds(pl.multiple_of(at * rows, rows), rows), :] = cores_ref[b]
        cluster = (owner >> (cols.bit_length() - 1)) * cl_dev + slot_ref[b]
        entry = (
            jnp.where(lane == at, cluster, 0)
            + jnp.where(lane == slots + at, rows_ref[b], 0)
            + jnp.where(lane == 2 * slots, 1, 0)
        )
        meta_ref[pl.ds(column, 1), :] += entry.astype(jnp.float32)
        return carry

    lax.fori_loop(0, blocks, place, 0, unroll=8)
    for j in range(cols):
        out_ref[j, slots * rows :, :] = jnp.broadcast_to(
            meta_ref[j : j + 1, :], (16, 128)
        ).astype(jnp.bfloat16)


def dispatch(block_rows, owners, block_slot, cores, cols, slots, cl_dev):
    blocks, rows, _ = cores.shape
    return pl.pallas_call(
        functools.partial(dispatch_kernel, cols, slots, cl_dev),
        in_specs=[whole(SMEM), whole(SMEM), whole(SMEM), whole()],
        out_specs=whole(),
        out_shape=jax.ShapeDtypeStruct((cols, slots * rows + 16, 128), jnp.bfloat16),
        scratch_shapes=[SMEM((cols,), jnp.int32), VMEM((cols, 128), jnp.float32)],
        compiler_params=pltpu.CompilerParams(vmem_limit_bytes=16 * MIB),
        cost_estimate=pl.CostEstimate(flops=4 * MIB, bytes_accessed=3 * MIB, transcendentals=0),
        name="dispatch",
    )(block_rows, owners, block_slot, cores)


UNROLL = 32
X_ROWS = 4


def far_kernel(slots, rows, comp_ref, sent_ref, *refs):
    outs, (acc_ref, meta_ref, smem_ref, list_ref, sem) = (refs[:5], refs[5:10]), refs[10:]
    sources = sent_ref.shape[0]
    group_rows = acc_ref.shape[0]
    part = group_rows // 4
    row_part = part // 4
    me = lax.axis_index("ccol")
    here_x, here_z = me // 4, me % 4

    meta = sent_ref[:, slots * rows : slots * rows + 16, :].astype(jnp.float32)
    meta = jnp.max(meta, axis=1).astype(jnp.int32)
    lane = lax.broadcasted_iota(jnp.int32, meta.shape, 1)
    row = pltpu.roll(meta, 128 - slots, axis=1) & (group_rows - 1)
    to_x = (row // part - here_x) & 3
    to_z = (row // row_part - here_z) & 3
    rest = row & (row_part - 1)
    z_rows = row_part - X_ROWS
    x_place = (to_x * 4 + to_z) * X_ROWS + rest
    z_place = 16 * X_ROWS + (to_z * 4 + to_x) * z_rows + rest - X_ROWS
    filed = jnp.where(rest < X_ROWS, x_place, z_place)
    place = lax.broadcasted_iota(jnp.int32, meta.shape, 0) * slots + lane
    words = (place << 14) + (meta << 7) + filed
    meta_ref[...] = jnp.where(lane < slots, words, meta)
    copy = pltpu.make_async_copy(meta_ref, smem_ref, sem)
    copy.start()
    acc_ref[...] = jnp.zeros_like(acc_ref)
    copy.wait()

    total = 0
    for i in range(sources):
        for p in range(slots):
            list_ref[total + p] = smem_ref[i, p]
        total = total + smem_ref[i, 2 * slots]
    for i in range(UNROLL):
        list_ref[total + i] = 0

    def group(g, carry):
        for i in range(UNROLL):
            at = g * UNROLL + i
            entry = list_ref[at]
            place = entry >> 14
            core = sent_ref[place // slots, pl.ds(pl.multiple_of((place % slots) * rows, rows), rows), :]
            core = jnp.where(at < total, core, jnp.zeros_like(core))
            half = core.shape[1] // 2
            core = jnp.concatenate([core[:, :half], core[:, half:]], axis=0)
            comp = comp_ref[(entry >> 7) & 127]
            acc_ref[entry & 127] += jnp.dot(core, comp, preferred_element_type=jnp.float32)
        return carry

    lax.fori_loop(0, (total + UNROLL - 1) // UNROLL, group, 0)
    begin = 0
    for up_ref, down_ref, next_ref, last_ref, own_ref in outs:
        part = own_ref.shape[0]
        half = part // 2
        own, following, far, last, begin = (begin + i * part for i in range(5))
        own_ref[...] = acc_ref[own : own + part]
        next_ref[...] = acc_ref[following : following + half]
        up_ref[half:] = acc_ref[following + half : following + part].astype(jnp.bfloat16)
        up_ref[:half] = acc_ref[far : far + half].astype(jnp.bfloat16)
        down_ref[half:] = acc_ref[far + half : far + part].astype(jnp.bfloat16)
        down_ref[:half] = acc_ref[last : last + half].astype(jnp.bfloat16)
        last_ref[...] = acc_ref[last + half : last + part]


def far_field(comp, sent, slots, rows, group_rows):
    _, rank, cols = comp.shape
    sources = sent.shape[0]
    x_part = X_ROWS * 4
    kinds = [
        (n, kind)
        for part in (x_part, group_rows // 4 - x_part)
        for n, kind in (
            (part, jnp.bfloat16),
            (part, jnp.bfloat16),
            (part // 2, jnp.float32),
            (part // 2, jnp.float32),
            (part, jnp.float32),
        )
    ]
    parts = pl.pallas_call(
        functools.partial(far_kernel, slots, rows),
        in_specs=[whole()] * 2,
        out_specs=[whole()] * len(kinds),
        out_shape=[jax.ShapeDtypeStruct((n, rank, cols), kind) for n, kind in kinds],
        scratch_shapes=[
            VMEM((group_rows, rank, cols), jnp.float32),
            VMEM((sources, 128), jnp.int32),
            SMEM((sources, 128), jnp.int32),
            SMEM((sources * slots + UNROLL + slots,), jnp.int32),
            pltpu.SemaphoreType.DMA,
        ],
        compiler_params=pltpu.CompilerParams(vmem_limit_bytes=40 * MIB),
        cost_estimate=pl.CostEstimate(
            flops=2 * 128 * rank * rank * cols * 8, bytes_accessed=24 * MIB, transcendentals=0
        ),
        name="far_field",
    )(comp, sent)
    return parts[:5], parts[5:]


def ring(axis_is_x, step):
    def to(i):
        x, z = i // 4, i % 4
        return ((x + step) % 4) * 4 + z if axis_is_x else x * 4 + (z + step) % 4

    return [(i, to(i)) for i in range(16)]


def f32(value):
    return value.astype(jnp.float32)


def both_ways(up, down, along_x):
    return lax.ppermute(up, "ccol", ring(along_x, 1)), lax.ppermute(down, "ccol", ring(along_x, -1))


SMALL = pl.CostEstimate(flops=0, bytes_accessed=0, transcendentals=0)


def pass_kernel(following_ref, last_ref, up_ref, down_ref, up_out_ref, down_out_ref):
    half = following_ref.shape[0]
    up_out_ref[...] = (following_ref[...] + f32(up_ref[:half])).astype(jnp.bfloat16)
    down_out_ref[...] = (last_ref[...] + f32(down_ref[half:])).astype(jnp.bfloat16)


def passed_on(following, last, up, down):
    shape = jax.ShapeDtypeStruct(following.shape, jnp.bfloat16)
    return pl.pallas_call(
        pass_kernel,
        in_specs=[whole()] * 4,
        out_specs=[whole()] * 2,
        out_shape=[shape] * 2,
        compiler_params=pltpu.CompilerParams(vmem_limit_bytes=24 * MIB),
        cost_estimate=SMALL,
        name="passed_on",
    )(following, last, up, down)


def turn_kernel(own_ref, up_in_ref, down_in_ref, up_rest_ref, down_rest_ref, up_ref, down_ref, next_ref, last_ref, here_ref):
    part, _, width = next_ref.shape
    half = up_rest_ref.shape[0]

    def total(kind):
        at = kind * part
        rows = pl.ds(at, part)
        if at < half:
            return own_ref[rows] + f32(down_in_ref[rows]) + f32(up_rest_ref[rows])
        return own_ref[rows] + f32(up_in_ref[rows]) + f32(down_rest_ref[pl.ds(at - half, part)])

    here_ref[...] = total(0)
    following, far, last = total(1), total(2), total(3)
    next_ref[...] = following[:, :, :width]
    up_ref[part:] = following[:, :, width:].astype(jnp.bfloat16)
    up_ref[:part] = far[:, :, :width].astype(jnp.bfloat16)
    down_ref[part:] = far[:, :, width:].astype(jnp.bfloat16)
    down_ref[:part] = last[:, :, :width].astype(jnp.bfloat16)
    last_ref[...] = last[:, :, width:]


def turn(own, up, down, up_rest, down_rest):
    rows, rank, cols = own.shape
    part, width = rows // 4, cols // 2
    kinds = [
        (2 * part, width, jnp.bfloat16),
        (2 * part, width, jnp.bfloat16),
        (part, width, jnp.float32),
        (part, width, jnp.float32),
        (part, cols, jnp.float32),
    ]
    return pl.pallas_call(
        turn_kernel,
        in_specs=[whole()] * 5,
        out_specs=[whole()] * 5,
        out_shape=[jax.ShapeDtypeStruct((n, rank, w), kind) for n, w, kind in kinds],
        compiler_params=pltpu.CompilerParams(vmem_limit_bytes=24 * MIB),
        cost_estimate=SMALL,
        name="turn",
    )(own, up, down, up_rest, down_rest)


def near_kernel(near_ref, before_ref, modes_ref, after_ref, basis_ref, out_ref, turned_ref, ext_ref):
    r = pl.program_id(0)
    halo, panels = before_ref.shape[0], modes_ref.shape[0]
    rank = basis_ref.shape[0]

    @pl.when(r == 0)
    def _():
        ext_ref[:halo] = before_ref[...]
        ext_ref[halo : halo + panels] = modes_ref[...]
        ext_ref[halo + panels :] = after_ref[...]

    window = ext_ref[pl.ds(pl.multiple_of(r * CS, CS), NEAR * CS), :]
    out_ref[...] = jnp.dot(near_ref[...], window, preferred_element_type=jnp.float32)
    have = lax.broadcasted_iota(jnp.int32, (rank, rank), 0)
    want = lax.broadcasted_iota(jnp.int32, (rank, rank), 1)
    order = jnp.where(want < rank // 2, 2 * want, 2 * want - rank + 1)
    select = jnp.where(order == have, 1.0, 0.0).astype(jnp.bfloat16)
    turned_ref[...] = lax.dot_general(
        basis_ref[...], select, (((0,), (0,)), ((), ())), preferred_element_type=jnp.float32
    ).astype(jnp.bfloat16)


def near_field(near_blocks, before, modes, after, row_basis):
    panels, band = near_blocks.shape
    cols = modes.shape[1]
    halo = before.shape[0]
    rank = row_basis.shape[0]
    return pl.pallas_call(
        near_kernel,
        grid=(panels // CS,),
        in_specs=[pl.BlockSpec((CS, band), lambda r: (r, 0))]
        + [whole()] * 3
        + [pl.BlockSpec((rank, CS), lambda r: (0, r))],
        out_specs=[
            pl.BlockSpec((CS, cols), lambda r: (r, 0)),
            pl.BlockSpec((CS, rank), lambda r: (r, 0)),
        ],
        out_shape=[
            jax.ShapeDtypeStruct((panels, cols), jnp.float32),
            jax.ShapeDtypeStruct((panels, rank), jnp.bfloat16),
        ],
        scratch_shapes=[VMEM((panels + 2 * halo, cols), jnp.bfloat16)],
        compiler_params=pltpu.CompilerParams(vmem_limit_bytes=32 * MIB),
        cost_estimate=pl.CostEstimate(
            flops=16 * panels * band * cols, bytes_accessed=16 * MIB, transcendentals=0
        ),
        name="near_field",
    )(near_blocks, before, modes, after, row_basis)


EXPAND = 2


def expand_kernel(near_ref, basis_ref, *refs):
    sides, out_ref = (refs[:5], refs[5:10]), refs[10]
    places = [(side, at) for side in sides for at in range(side[0].shape[0])]
    width = sides[0][3].shape[2]
    step = pl.program_id(0)
    for group in range(len(places) // EXPAND):

        @pl.when(step == group)
        def _():
            for i in range(EXPAND):
                rows = pl.ds(i * CS, CS)
                (own_ref, up_ref, down_ref, up_rest_ref, down_rest_ref), at = places[group * EXPAND + i]
                part = own_ref.shape[0]
                own = own_ref[at]
                first = own[:, :width] + f32(down_ref[at]) + f32(up_rest_ref[at])
                second = own[:, width:] + f32(up_ref[part + at]) + f32(down_rest_ref[at])
                for far, cols in ((first, pl.ds(0, width)), (second, pl.ds(width, width))):
                    value = jnp.dot(basis_ref[rows, :], far.astype(jnp.bfloat16), preferred_element_type=jnp.float32)
                    out_ref[rows, cols] = (near_ref[rows, cols] + value).astype(jnp.bfloat16)


def expand(near, basis, left, right):
    panels, cols = near.shape
    rank = basis.shape[1]
    return pl.pallas_call(
        expand_kernel,
        grid=(panels // CS // EXPAND,),
        in_specs=[
            pl.BlockSpec((EXPAND * CS, cols), lambda r: (r, 0)),
            pl.BlockSpec((EXPAND * CS, rank), lambda r: (r, 0)),
        ]
        + [pl.BlockSpec(v.shape, lambda r: (0, 0, 0)) for v in (*left, *right)],
        out_specs=pl.BlockSpec((EXPAND * CS, cols), lambda r: (r, 0)),
        out_shape=jax.ShapeDtypeStruct((panels, cols), jnp.bfloat16),
        compiler_params=pltpu.CompilerParams(vmem_limit_bytes=24 * MIB),
        cost_estimate=pl.CostEstimate(
            flops=2 * panels * rank * cols, bytes_accessed=7 * MIB, transcendentals=0
        ),
        name="expand",
    )(near, basis, *left, *right)


def per_device(modes, col_basis, row_basis, near_blocks, block_rows, block_owner, block_slot, cores):
    row_devices, col_devices = lax.axis_size("crow"), lax.axis_size("ccol")
    devices = row_devices * col_devices
    cluster_count = modes.shape[0] // CS
    rank = col_basis.shape[0]
    blocks = cores.shape[0]
    slots = CAP * row_devices

    compressed, low, high = compress(col_basis, modes)
    gathered = lax.all_gather(compressed, "crow", axis=0, tiled=True)

    lines = rank * rank // 128
    sent = dispatch(
        block_rows, block_owner[:, 0], block_slot, cores.reshape(blocks, lines, 128),
        col_devices, slots, cluster_count,
    )
    sent = lax.all_to_all(sent, "ccol", split_axis=0, concat_axis=0, tiled=True)

    up = [(i, i + 1) for i in range(devices - 1)]
    down = [(j, i) for i, j in up]
    before = lax.ppermute(high, ("crow", "ccol"), up)
    after = lax.ppermute(low, ("crow", "ccol"), down)
    near, basis = near_field(near_blocks, before, modes, after, row_basis)
    gathered, _ = lax.optimization_barrier((gathered, near))

    left, right = far_field(gathered, sent, slots, lines, col_devices * cluster_count)
    for along_x in (True, False):
        left_up, left_down = both_ways(left[0], left[1], along_x)
        right_up, right_down = both_ways(right[0], right[1], not along_x)
        left_rest = passed_on(left[2], left[3], left_up, left_down)
        right_rest = passed_on(right[2], right[3], right_up, right_down)
        left_rest = both_ways(*left_rest, along_x)
        right_rest = both_ways(*right_rest, not along_x)
        left = (left[4], left_up, left_down, *left_rest)
        right = (right[4], right_up, right_down, *right_rest)
        if along_x:
            left, right = turn(*left), turn(*right)
    return expand(near, basis, left, right)


def solution(mesh):
    both = ("crow", "ccol")
    in_specs = (
        P(both, None),
        P(None, both),
        P(None, both),
        P(both, None),
        P(both),
        P(both, None),
        P(both),
        P(both, None),
    )
    return jax.shard_map(
        per_device, mesh=mesh, in_specs=in_specs, out_specs=P(both, None), check_vma=False
    )
```

```python
import functools

import jax
import jax.numpy as jnp
from jax import lax
from jax.experimental import pallas as pl
from jax.experimental.pallas import tpu as pltpu
from jax.sharding import PartitionSpec as P

CS = 256
NH = 4
NEAR = 9
CAP = 2
MIB = 1 << 20
VMEM = pltpu.VMEM
SMEM = pltpu.SMEM


def whole(space=VMEM):
    return pl.BlockSpec(memory_space=space)


COMPRESS = 4


def compress_kernel(basis_ref, modes_ref, out_ref, low_ref, high_ref):
    step = pl.program_id(0)

    @pl.when(step == 0)
    def _():
        low_ref[...] = modes_ref[: NH * CS, :]

    @pl.when(step == pl.num_programs(0) - 1)
    def _():
        high_ref[...] = modes_ref[(COMPRESS - NH) * CS :, :]

    for i in range(COMPRESS):
        out_ref[i] = jnp.dot(
            basis_ref[:, i * CS : (i + 1) * CS],
            modes_ref[i * CS : (i + 1) * CS, :],
            preferred_element_type=jnp.float32,
        ).astype(jnp.bfloat16)


def compress(col_basis, modes):
    rank, panels = col_basis.shape
    cols = modes.shape[1]
    count = panels // CS
    return pl.pallas_call(
        compress_kernel,
        grid=(count // COMPRESS,),
        in_specs=[
            pl.BlockSpec((rank, COMPRESS * CS), lambda r: (0, r)),
            pl.BlockSpec((COMPRESS * CS, cols), lambda r: (r, 0)),
        ],
        out_specs=[
            pl.BlockSpec((COMPRESS, rank, cols), lambda r: (r, 0, 0)),
            pl.BlockSpec((NH * CS, cols), lambda r: (0, 0)),
            pl.BlockSpec((NH * CS, cols), lambda r: (0, 0)),
        ],
        out_shape=[
            jax.ShapeDtypeStruct((count, rank, cols), jnp.bfloat16),
            jax.ShapeDtypeStruct((NH * CS, cols), jnp.bfloat16),
            jax.ShapeDtypeStruct((NH * CS, cols), jnp.bfloat16),
        ],
        compiler_params=pltpu.CompilerParams(vmem_limit_bytes=58 * MIB),
        cost_estimate=pl.CostEstimate(
            flops=2 * rank * panels * cols, bytes_accessed=3 * MIB, transcendentals=0
        ),
        name="compress",
    )(col_basis, modes)


def dispatch_kernel(
    cols, slots, cl_dev, rows_ref, owners_ref, slot_ref, cores_ref, out_ref, count_ref, meta_ref
):
    blocks, rows, _ = cores_ref.shape
    out_ref[...] = jnp.zeros_like(out_ref)
    meta_ref[...] = jnp.zeros_like(meta_ref)
    lane = lax.broadcasted_iota(jnp.int32, (1, 128), 1)
    for j in range(cols):
        count_ref[j] = 0

    def place(b, carry):
        owner = owners_ref[b]
        column = owner & (cols - 1)
        at = count_ref[column]
        count_ref[column] = at + 1
        out_ref[column, pl.ds(pl.multiple_of(at * rows, rows), rows), :] = cores_ref[b]
        cluster = (owner >> (cols.bit_length() - 1)) * cl_dev + slot_ref[b]
        entry = (
            jnp.where(lane == at, cluster, 0)
            + jnp.where(lane == slots + at, rows_ref[b], 0)
            + jnp.where(lane == 2 * slots, 1, 0)
        )
        meta_ref[pl.ds(column, 1), :] += entry.astype(jnp.float32)
        return carry

    lax.fori_loop(0, blocks, place, 0, unroll=8)
    for j in range(cols):
        out_ref[j, slots * rows :, :] = jnp.broadcast_to(
            meta_ref[j : j + 1, :], (16, 128)
        ).astype(jnp.bfloat16)


def dispatch(block_rows, owners, block_slot, cores, cols, slots, cl_dev):
    blocks, rows, _ = cores.shape
    return pl.pallas_call(
        functools.partial(dispatch_kernel, cols, slots, cl_dev),
        in_specs=[whole(SMEM), whole(SMEM), whole(SMEM), whole()],
        out_specs=whole(),
        out_shape=jax.ShapeDtypeStruct((cols, slots * rows + 16, 128), jnp.bfloat16),
        scratch_shapes=[SMEM((cols,), jnp.int32), VMEM((cols, 128), jnp.float32)],
        compiler_params=pltpu.CompilerParams(vmem_limit_bytes=16 * MIB),
        cost_estimate=pl.CostEstimate(flops=4 * MIB, bytes_accessed=3 * MIB, transcendentals=0),
        name="dispatch",
    )(block_rows, owners, block_slot, cores)


UNROLL = 32
X_ROWS = 4


def far_kernel(slots, rows, here_ref, comp_ref, sent_ref, *refs):
    outs, (acc_ref, meta_ref, smem_ref, list_ref, sem) = (refs[:5], refs[5:10]), refs[10:]
    sources = sent_ref.shape[0]
    group_rows = acc_ref.shape[0]
    part = group_rows // 4
    row_part = part // 4
    me = lax.axis_index("ccol")
    here_x, here_z = me // 4, me % 4

    meta = sent_ref[:, slots * rows : slots * rows + 16, :].astype(jnp.float32)
    meta = jnp.max(meta, axis=1).astype(jnp.int32)
    lane = lax.broadcasted_iota(jnp.int32, meta.shape, 1)
    row = pltpu.roll(meta, 128 - slots, axis=1) & (group_rows - 1)
    to_x = (row // part - here_x) & 3
    to_z = (row // row_part - here_z) & 3
    rest = row & (row_part - 1)
    z_rows = row_part - X_ROWS
    x_place = (to_x * 4 + to_z) * X_ROWS + rest
    z_place = 16 * X_ROWS + (to_z * 4 + to_x) * z_rows + rest - X_ROWS
    filed = jnp.where(rest < X_ROWS, x_place, z_place)
    place = lax.broadcasted_iota(jnp.int32, meta.shape, 0) * slots + lane
    words = (place << 14) + (meta << 7) + filed
    meta_ref[...] = jnp.where(lane < slots, words, meta)
    copy = pltpu.make_async_copy(meta_ref, smem_ref, sem)
    copy.start()
    acc_ref[...] = jnp.zeros_like(acc_ref)
    copy.wait()

    total = 0
    for i in range(sources):
        for p in range(slots):
            list_ref[total + p] = smem_ref[i, p]
        total = total + smem_ref[i, 2 * slots]
    for i in range(UNROLL):
        list_ref[total + i] = 0

    def group(g, carry):
        for i in range(UNROLL):
            at = g * UNROLL + i
            entry = list_ref[at]
            place = entry >> 14
            core = sent_ref[place // slots, pl.ds(pl.multiple_of((place % slots) * rows, rows), rows), :]
            core = jnp.where(at < total, core, jnp.zeros_like(core))
            half = core.shape[1] // 2
            core = jnp.concatenate([core[:, :half], core[:, half:]], axis=0)
            comp = comp_ref[(entry >> 7) & 127]
            acc_ref[entry & 127] += jnp.dot(core, comp, preferred_element_type=jnp.float32)
        return carry

    lax.fori_loop(0, (total + UNROLL - 1) // UNROLL, group, 0)
    begin = 0
    for up_ref, down_ref, next_ref, last_ref, own_ref in outs:
        part = own_ref.shape[0]
        half = part // 2
        own, following, far, last, begin = (begin + i * part for i in range(5))
        own_ref[...] = acc_ref[own : own + part]
        next_ref[...] = acc_ref[following : following + half]
        up_ref[half:] = acc_ref[following + half : following + part].astype(jnp.bfloat16)
        up_ref[:half] = acc_ref[far : far + half].astype(jnp.bfloat16)
        down_ref[half:] = acc_ref[far + half : far + part].astype(jnp.bfloat16)
        down_ref[:half] = acc_ref[last : last + half].astype(jnp.bfloat16)
        last_ref[...] = acc_ref[last + half : last + part]


def far_field(here, comp, sent, slots, rows, group_rows):
    _, rank, cols = comp.shape
    sources = sent.shape[0]
    x_part = X_ROWS * 4
    kinds = [
        (n, kind)
        for part in (x_part, group_rows // 4 - x_part)
        for n, kind in (
            (part, jnp.bfloat16),
            (part, jnp.bfloat16),
            (part // 2, jnp.float32),
            (part // 2, jnp.float32),
            (part, jnp.float32),
        )
    ]
    parts = pl.pallas_call(
        functools.partial(far_kernel, slots, rows),
        in_specs=[whole(pl.ANY)] + [whole()] * 2,
        out_specs=[whole()] * len(kinds),
        out_shape=[jax.ShapeDtypeStruct((n, rank, cols), kind) for n, kind in kinds],
        scratch_shapes=[
            VMEM((group_rows, rank, cols), jnp.float32),
            VMEM((sources, 128), jnp.int32),
            SMEM((sources, 128), jnp.int32),
            SMEM((sources * slots + UNROLL + slots,), jnp.int32),
            pltpu.SemaphoreType.DMA,
        ],
        compiler_params=pltpu.CompilerParams(vmem_limit_bytes=40 * MIB),
        cost_estimate=pl.CostEstimate(
            flops=2 * 128 * rank * rank * cols * 8, bytes_accessed=24 * MIB, transcendentals=0
        ),
        name="far_field",
    )(here, comp, sent)
    return parts[:5], parts[5:]


def ring(axis_is_x, step):
    def to(i):
        x, z = i // 4, i % 4
        return ((x + step) % 4) * 4 + z if axis_is_x else x * 4 + (z + step) % 4

    return [(i, to(i)) for i in range(16)]


def f32(value):
    return value.astype(jnp.float32)


def both_ways(up, down, along_x):
    return lax.ppermute(up, "ccol", ring(along_x, 1)), lax.ppermute(down, "ccol", ring(along_x, -1))


SMALL = pl.CostEstimate(flops=0, bytes_accessed=0, transcendentals=0)


def pass_kernel(following_ref, last_ref, up_ref, down_ref, up_out_ref, down_out_ref):
    half = following_ref.shape[0]
    up_out_ref[...] = (following_ref[...] + f32(up_ref[:half])).astype(jnp.bfloat16)
    down_out_ref[...] = (last_ref[...] + f32(down_ref[half:])).astype(jnp.bfloat16)


def passed_on(following, last, up, down):
    shape = jax.ShapeDtypeStruct(following.shape, jnp.bfloat16)
    return pl.pallas_call(
        pass_kernel,
        in_specs=[whole()] * 4,
        out_specs=[whole()] * 2,
        out_shape=[shape] * 2,
        compiler_params=pltpu.CompilerParams(vmem_limit_bytes=24 * MIB),
        cost_estimate=SMALL,
        name="passed_on",
    )(following, last, up, down)


def turn_kernel(own_ref, up_in_ref, down_in_ref, up_rest_ref, down_rest_ref, up_ref, down_ref, next_ref, last_ref, here_ref):
    part, _, width = next_ref.shape
    half = up_rest_ref.shape[0]

    def total(kind):
        at = kind * part
        rows = pl.ds(at, part)
        if at < half:
            return own_ref[rows] + f32(down_in_ref[rows]) + f32(up_rest_ref[rows])
        return own_ref[rows] + f32(up_in_ref[rows]) + f32(down_rest_ref[pl.ds(at - half, part)])

    here_ref[...] = total(0)
    following, far, last = total(1), total(2), total(3)
    next_ref[...] = following[:, :, :width]
    up_ref[part:] = following[:, :, width:].astype(jnp.bfloat16)
    up_ref[:part] = far[:, :, :width].astype(jnp.bfloat16)
    down_ref[part:] = far[:, :, width:].astype(jnp.bfloat16)
    down_ref[:part] = last[:, :, :width].astype(jnp.bfloat16)
    last_ref[...] = last[:, :, width:]


def turn(own, up, down, up_rest, down_rest):
    rows, rank, cols = own.shape
    part, width = rows // 4, cols // 2
    kinds = [
        (2 * part, width, jnp.bfloat16),
        (2 * part, width, jnp.bfloat16),
        (part, width, jnp.float32),
        (part, width, jnp.float32),
        (part, cols, jnp.float32),
    ]
    return pl.pallas_call(
        turn_kernel,
        in_specs=[whole()] * 5,
        out_specs=[whole()] * 5,
        out_shape=[jax.ShapeDtypeStruct((n, rank, w), kind) for n, w, kind in kinds],
        compiler_params=pltpu.CompilerParams(vmem_limit_bytes=24 * MIB),
        cost_estimate=SMALL,
        name="turn",
    )(own, up, down, up_rest, down_rest)


def near_kernel(near_ref, before_ref, modes_ref, after_ref, basis_ref, out_ref, turned_ref, ext_ref):
    r = pl.program_id(0)
    halo, panels = before_ref.shape[0], modes_ref.shape[0]
    rank = basis_ref.shape[0]

    @pl.when(r == 0)
    def _():
        ext_ref[:halo] = before_ref[...]
        ext_ref[halo : halo + panels] = modes_ref[...]
        ext_ref[halo + panels :] = after_ref[...]

    window = ext_ref[pl.ds(pl.multiple_of(r * CS, CS), NEAR * CS), :]
    out_ref[...] = jnp.dot(near_ref[...], window, preferred_element_type=jnp.float32)
    have = lax.broadcasted_iota(jnp.int32, (rank, rank), 0)
    want = lax.broadcasted_iota(jnp.int32, (rank, rank), 1)
    order = jnp.where(want < rank // 2, 2 * want, 2 * want - rank + 1)
    select = jnp.where(order == have, 1.0, 0.0).astype(jnp.bfloat16)
    turned_ref[...] = lax.dot_general(
        basis_ref[...], select, (((0,), (0,)), ((), ())), preferred_element_type=jnp.float32
    ).astype(jnp.bfloat16)


def near_field(near_blocks, before, modes, after, row_basis):
    panels, band = near_blocks.shape
    cols = modes.shape[1]
    halo = before.shape[0]
    rank = row_basis.shape[0]
    return pl.pallas_call(
        near_kernel,
        grid=(panels // CS,),
        in_specs=[pl.BlockSpec((CS, band), lambda r: (r, 0))]
        + [whole()] * 3
        + [pl.BlockSpec((rank, CS), lambda r: (0, r))],
        out_specs=[
            pl.BlockSpec((CS, cols), lambda r: (r, 0)),
            pl.BlockSpec((CS, rank), lambda r: (r, 0)),
        ],
        out_shape=[
            jax.ShapeDtypeStruct((panels, cols), jnp.float32),
            jax.ShapeDtypeStruct((panels, rank), jnp.bfloat16),
        ],
        scratch_shapes=[VMEM((panels + 2 * halo, cols), jnp.bfloat16)],
        compiler_params=pltpu.CompilerParams(vmem_limit_bytes=32 * MIB),
        cost_estimate=pl.CostEstimate(
            flops=2 * panels * band * cols, bytes_accessed=2 * MIB, transcendentals=0
        ),
        name="near_field",
    )(near_blocks, before, modes, after, row_basis)


def arrival_kernel(before_ref, after_ref, out_ref):
    out_ref[...] = jnp.zeros_like(out_ref)


def arrival(before, after):
    return pl.pallas_call(
        arrival_kernel,
        in_specs=[whole(pl.ANY)] * 2,
        out_specs=whole(),
        out_shape=jax.ShapeDtypeStruct((8, 128), jnp.float32),
        cost_estimate=pl.CostEstimate(flops=40 << 30, bytes_accessed=16 * MIB, transcendentals=0),
        name="arrival",
    )(before, after)


EXPAND = 2


def expand_kernel(near_ref, basis_ref, *refs):
    sides, out_ref = (refs[:5], refs[5:10]), refs[10]
    places = [(side, at) for side in sides for at in range(side[0].shape[0])]
    width = sides[0][3].shape[2]
    step = pl.program_id(0)
    for group in range(len(places) // EXPAND):

        @pl.when(step == group)
        def _():
            for i in range(EXPAND):
                rows = pl.ds(i * CS, CS)
                (own_ref, up_ref, down_ref, up_rest_ref, down_rest_ref), at = places[group * EXPAND + i]
                part = own_ref.shape[0]
                own = own_ref[at]
                first = own[:, :width] + f32(down_ref[at]) + f32(up_rest_ref[at])
                second = own[:, width:] + f32(up_ref[part + at]) + f32(down_rest_ref[at])
                for far, cols in ((first, pl.ds(0, width)), (second, pl.ds(width, width))):
                    value = jnp.dot(basis_ref[rows, :], far.astype(jnp.bfloat16), preferred_element_type=jnp.float32)
                    out_ref[rows, cols] = (near_ref[rows, cols] + value).astype(jnp.bfloat16)


def expand(near, basis, left, right):
    panels, cols = near.shape
    rank = basis.shape[1]
    return pl.pallas_call(
        expand_kernel,
        grid=(panels // CS // EXPAND,),
        in_specs=[
            pl.BlockSpec((EXPAND * CS, cols), lambda r: (r, 0)),
            pl.BlockSpec((EXPAND * CS, rank), lambda r: (r, 0)),
        ]
        + [pl.BlockSpec(v.shape, lambda r: (0, 0, 0)) for v in (*left, *right)],
        out_specs=pl.BlockSpec((EXPAND * CS, cols), lambda r: (r, 0)),
        out_shape=jax.ShapeDtypeStruct((panels, cols), jnp.bfloat16),
        compiler_params=pltpu.CompilerParams(vmem_limit_bytes=24 * MIB),
        cost_estimate=pl.CostEstimate(
            flops=2 * panels * rank * cols, bytes_accessed=7 * MIB, transcendentals=0
        ),
        name="expand",
    )(near, basis, *left, *right)


def per_device(modes, col_basis, row_basis, near_blocks, block_rows, block_owner, block_slot, cores):
    row_devices, col_devices = lax.axis_size("crow"), lax.axis_size("ccol")
    devices = row_devices * col_devices
    cluster_count = modes.shape[0] // CS
    rank = col_basis.shape[0]
    blocks = cores.shape[0]
    slots = CAP * row_devices

    compressed, low, high = compress(col_basis, modes)
    gathered = lax.all_gather(compressed, "crow", axis=0, tiled=True)

    lines = rank * rank // 128
    sent = dispatch(
        block_rows, block_owner[:, 0], block_slot, cores.reshape(blocks, lines, 128),
        col_devices, slots, cluster_count,
    )
    sent = lax.all_to_all(sent, "ccol", split_axis=0, concat_axis=0, tiled=True)

    up = [(i, i + 1) for i in range(devices - 1)]
    down = [(j, i) for i, j in up]
    before = lax.ppermute(high, ("crow", "ccol"), up)
    after = lax.ppermute(low, ("crow", "ccol"), down)
    here = arrival(before, after)
    left, right = far_field(here, gathered, sent, slots, lines, col_devices * cluster_count)
    for along_x in (True, False):
        left_up, left_down = both_ways(left[0], left[1], along_x)
        right_up, right_down = both_ways(right[0], right[1], not along_x)
        if along_x:
            (before, after), _ = lax.optimization_barrier(((before, after), left[0]))
            near, basis = near_field(near_blocks, before, modes, after, row_basis)
            (left_up, left_down), _ = lax.optimization_barrier(((left_up, left_down), near))
        left_rest = passed_on(left[2], left[3], left_up, left_down)
        right_rest = passed_on(right[2], right[3], right_up, right_down)
        left_rest = both_ways(*left_rest, along_x)
        right_rest = both_ways(*right_rest, not along_x)
        left = (left[4], left_up, left_down, *left_rest)
        right = (right[4], right_up, right_down, *right_rest)
        if along_x:
            left, right = turn(*left), turn(*right)
    return expand(near, basis, left, right)


def solution(mesh):
    both = ("crow", "ccol")
    in_specs = (
        P(both, None),
        P(None, both),
        P(None, both),
        P(both, None),
        P(both),
        P(both, None),
        P(both),
        P(both, None),
    )
    return jax.shard_map(
        per_device, mesh=mesh, in_specs=in_specs, out_specs=P(both, None), check_vma=False
    )
```

```python
import functools

import jax
import jax.numpy as jnp
from jax import lax
from jax.experimental import pallas as pl
from jax.experimental.pallas import tpu as pltpu
from jax.sharding import PartitionSpec as P

CS = 256
NH = 4
NEAR = 9
CAP = 2
MIB = 1 << 20
VMEM = pltpu.VMEM
SMEM = pltpu.SMEM


def whole(space=VMEM):
    return pl.BlockSpec(memory_space=space)


COMPRESS = 4


def compress_kernel(basis_ref, modes_ref, out_ref, low_ref, high_ref):
    step = pl.program_id(0)

    @pl.when(step == 0)
    def _():
        low_ref[...] = modes_ref[: NH * CS, :]

    @pl.when(step == pl.num_programs(0) - 1)
    def _():
        high_ref[...] = modes_ref[(COMPRESS - NH) * CS :, :]

    for i in range(COMPRESS):
        out_ref[i] = jnp.dot(
            basis_ref[:, i * CS : (i + 1) * CS],
            modes_ref[i * CS : (i + 1) * CS, :],
            preferred_element_type=jnp.float32,
        ).astype(jnp.bfloat16)


def compress(col_basis, modes):
    rank, panels = col_basis.shape
    cols = modes.shape[1]
    count = panels // CS
    return pl.pallas_call(
        compress_kernel,
        grid=(count // COMPRESS,),
        in_specs=[
            pl.BlockSpec((rank, COMPRESS * CS), lambda r: (0, r)),
            pl.BlockSpec((COMPRESS * CS, cols), lambda r: (r, 0)),
        ],
        out_specs=[
            pl.BlockSpec((COMPRESS, rank, cols), lambda r: (r, 0, 0)),
            pl.BlockSpec((NH * CS, cols), lambda r: (0, 0)),
            pl.BlockSpec((NH * CS, cols), lambda r: (0, 0)),
        ],
        out_shape=[
            jax.ShapeDtypeStruct((count, rank, cols), jnp.bfloat16),
            jax.ShapeDtypeStruct((NH * CS, cols), jnp.bfloat16),
            jax.ShapeDtypeStruct((NH * CS, cols), jnp.bfloat16),
        ],
        compiler_params=pltpu.CompilerParams(vmem_limit_bytes=58 * MIB),
        cost_estimate=pl.CostEstimate(
            flops=2 * rank * panels * cols, bytes_accessed=3 * MIB, transcendentals=0
        ),
        name="compress",
    )(col_basis, modes)


def dispatch_kernel(
    cols, slots, cl_dev, rows_ref, owners_ref, slot_ref, cores_ref, out_ref, count_ref, meta_ref
):
    blocks, rows, _ = cores_ref.shape
    out_ref[...] = jnp.zeros_like(out_ref)
    meta_ref[...] = jnp.zeros_like(meta_ref)
    lane = lax.broadcasted_iota(jnp.int32, (1, 128), 1)
    for j in range(cols):
        count_ref[j] = 0

    def place(b, carry):
        owner = owners_ref[b]
        column = owner & (cols - 1)
        at = count_ref[column]
        count_ref[column] = at + 1
        out_ref[column, pl.ds(pl.multiple_of(at * rows, rows), rows), :] = cores_ref[b]
        cluster = (owner >> (cols.bit_length() - 1)) * cl_dev + slot_ref[b]
        entry = (
            jnp.where(lane == at, cluster, 0)
            + jnp.where(lane == slots + at, rows_ref[b], 0)
            + jnp.where(lane == 2 * slots, 1, 0)
        )
        meta_ref[pl.ds(column, 1), :] += entry.astype(jnp.float32)
        return carry

    lax.fori_loop(0, blocks, place, 0, unroll=8)
    for j in range(cols):
        out_ref[j, slots * rows :, :] = jnp.broadcast_to(
            meta_ref[j : j + 1, :], (16, 128)
        ).astype(jnp.bfloat16)


def dispatch(block_rows, owners, block_slot, cores, cols, slots, cl_dev):
    blocks, rows, _ = cores.shape
    return pl.pallas_call(
        functools.partial(dispatch_kernel, cols, slots, cl_dev),
        in_specs=[whole(SMEM), whole(SMEM), whole(SMEM), whole()],
        out_specs=whole(),
        out_shape=jax.ShapeDtypeStruct((cols, slots * rows + 16, 128), jnp.bfloat16),
        scratch_shapes=[SMEM((cols,), jnp.int32), VMEM((cols, 128), jnp.float32)],
        compiler_params=pltpu.CompilerParams(vmem_limit_bytes=16 * MIB),
        cost_estimate=pl.CostEstimate(flops=4 * MIB, bytes_accessed=3 * MIB, transcendentals=0),
        name="dispatch",
    )(block_rows, owners, block_slot, cores)


UNROLL = 32
X_ROWS = 4


def far_kernel(slots, rows, comp_ref, sent_ref, *refs):
    outs, (acc_ref, meta_ref, smem_ref, list_ref, sem) = (refs[:5], refs[5:10]), refs[10:]
    sources = sent_ref.shape[0]
    group_rows = acc_ref.shape[0]
    part = group_rows // 4
    row_part = part // 4
    me = lax.axis_index("ccol")
    here_x, here_z = me // 4, me % 4

    meta = sent_ref[:, slots * rows : slots * rows + 16, :].astype(jnp.float32)
    meta = jnp.max(meta, axis=1).astype(jnp.int32)
    lane = lax.broadcasted_iota(jnp.int32, meta.shape, 1)
    row = pltpu.roll(meta, 128 - slots, axis=1) & (group_rows - 1)
    to_x = (row // part - here_x) & 3
    to_z = (row // row_part - here_z) & 3
    rest = row & (row_part - 1)
    z_rows = row_part - X_ROWS
    x_place = (to_x * 4 + to_z) * X_ROWS + rest
    z_place = 16 * X_ROWS + (to_z * 4 + to_x) * z_rows + rest - X_ROWS
    filed = jnp.where(rest < X_ROWS, x_place, z_place)
    place = lax.broadcasted_iota(jnp.int32, meta.shape, 0) * slots + lane
    words = (place << 14) + (meta << 7) + filed
    meta_ref[...] = jnp.where(lane < slots, words, meta)
    copy = pltpu.make_async_copy(meta_ref, smem_ref, sem)
    copy.start()
    acc_ref[...] = jnp.zeros_like(acc_ref)
    copy.wait()

    total = 0
    for i in range(sources):
        for p in range(slots):
            list_ref[total + p] = smem_ref[i, p]
        total = total + smem_ref[i, 2 * slots]
    for i in range(UNROLL):
        list_ref[total + i] = 0

    def group(g, carry):
        for i in range(UNROLL):
            at = g * UNROLL + i
            entry = list_ref[at]
            place = entry >> 14
            core = sent_ref[place // slots, pl.ds(pl.multiple_of((place % slots) * rows, rows), rows), :]
            core = jnp.where(at < total, core, jnp.zeros_like(core))
            half = core.shape[1] // 2
            core = jnp.concatenate([core[:, :half], core[:, half:]], axis=0)
            comp = comp_ref[(entry >> 7) & 127]
            acc_ref[entry & 127] += jnp.dot(core, comp, preferred_element_type=jnp.float32)
        return carry

    lax.fori_loop(0, (total + UNROLL - 1) // UNROLL, group, 0)
    begin = 0
    for up_ref, down_ref, next_ref, last_ref, own_ref in outs:
        part = own_ref.shape[0]
        half = part // 2
        own, following, far, last, begin = (begin + i * part for i in range(5))
        own_ref[...] = acc_ref[own : own + part]
        next_ref[...] = acc_ref[following : following + half]
        up_ref[half:] = acc_ref[following + half : following + part].astype(jnp.bfloat16)
        up_ref[:half] = acc_ref[far : far + half].astype(jnp.bfloat16)
        down_ref[half:] = acc_ref[far + half : far + part].astype(jnp.bfloat16)
        down_ref[:half] = acc_ref[last : last + half].astype(jnp.bfloat16)
        last_ref[...] = acc_ref[last + half : last + part]


def far_field(comp, sent, slots, rows, group_rows):
    _, rank, cols = comp.shape
    sources = sent.shape[0]
    x_part = X_ROWS * 4
    kinds = [
        (n, kind)
        for part in (x_part, group_rows // 4 - x_part)
        for n, kind in (
            (part, jnp.bfloat16),
            (part, jnp.bfloat16),
            (part // 2, jnp.float32),
            (part // 2, jnp.float32),
            (part, jnp.float32),
        )
    ]
    parts = pl.pallas_call(
        functools.partial(far_kernel, slots, rows),
        in_specs=[whole()] * 2,
        out_specs=[whole()] * len(kinds),
        out_shape=[jax.ShapeDtypeStruct((n, rank, cols), kind) for n, kind in kinds],
        scratch_shapes=[
            VMEM((group_rows, rank, cols), jnp.float32),
            VMEM((sources, 128), jnp.int32),
            SMEM((sources, 128), jnp.int32),
            SMEM((sources * slots + UNROLL + slots,), jnp.int32),
            pltpu.SemaphoreType.DMA,
        ],
        compiler_params=pltpu.CompilerParams(vmem_limit_bytes=40 * MIB),
        cost_estimate=pl.CostEstimate(
            flops=2 * 128 * rank * rank * cols * 8, bytes_accessed=24 * MIB, transcendentals=0
        ),
        name="far_field",
    )(comp, sent)
    return parts[:5], parts[5:]


def ring(axis_is_x, step):
    def to(i):
        x, z = i // 4, i % 4
        return ((x + step) % 4) * 4 + z if axis_is_x else x * 4 + (z + step) % 4

    return [(i, to(i)) for i in range(16)]


def f32(value):
    return value.astype(jnp.float32)


def both_ways(up, down, along_x):
    return lax.ppermute(up, "ccol", ring(along_x, 1)), lax.ppermute(down, "ccol", ring(along_x, -1))


SMALL = pl.CostEstimate(flops=0, bytes_accessed=0, transcendentals=0)


def pass_kernel(following_ref, last_ref, up_ref, down_ref, up_out_ref, down_out_ref):
    half = following_ref.shape[0]
    up_out_ref[...] = (following_ref[...] + f32(up_ref[:half])).astype(jnp.bfloat16)
    down_out_ref[...] = (last_ref[...] + f32(down_ref[half:])).astype(jnp.bfloat16)


def passed_on(following, last, up, down):
    shape = jax.ShapeDtypeStruct(following.shape, jnp.bfloat16)
    return pl.pallas_call(
        pass_kernel,
        in_specs=[whole()] * 4,
        out_specs=[whole()] * 2,
        out_shape=[shape] * 2,
        compiler_params=pltpu.CompilerParams(vmem_limit_bytes=24 * MIB),
        cost_estimate=SMALL,
        name="passed_on",
    )(following, last, up, down)


def turn_kernel(own_ref, up_in_ref, down_in_ref, up_rest_ref, down_rest_ref, up_ref, down_ref, next_ref, last_ref, here_ref):
    part, _, width = next_ref.shape
    half = up_rest_ref.shape[0]

    def total(kind):
        at = kind * part
        rows = pl.ds(at, part)
        if at < half:
            return own_ref[rows] + f32(down_in_ref[rows]) + f32(up_rest_ref[rows])
        return own_ref[rows] + f32(up_in_ref[rows]) + f32(down_rest_ref[pl.ds(at - half, part)])

    here_ref[...] = total(0)
    following, far, last = total(1), total(2), total(3)
    next_ref[...] = following[:, :, :width]
    up_ref[part:] = following[:, :, width:].astype(jnp.bfloat16)
    up_ref[:part] = far[:, :, :width].astype(jnp.bfloat16)
    down_ref[part:] = far[:, :, width:].astype(jnp.bfloat16)
    down_ref[:part] = last[:, :, :width].astype(jnp.bfloat16)
    last_ref[...] = last[:, :, width:]


def turn(own, up, down, up_rest, down_rest):
    rows, rank, cols = own.shape
    part, width = rows // 4, cols // 2
    kinds = [
        (2 * part, width, jnp.bfloat16),
        (2 * part, width, jnp.bfloat16),
        (part, width, jnp.float32),
        (part, width, jnp.float32),
        (part, cols, jnp.float32),
    ]
    return pl.pallas_call(
        turn_kernel,
        in_specs=[whole()] * 5,
        out_specs=[whole()] * 5,
        out_shape=[jax.ShapeDtypeStruct((n, rank, w), kind) for n, w, kind in kinds],
        compiler_params=pltpu.CompilerParams(vmem_limit_bytes=24 * MIB),
        cost_estimate=SMALL,
        name="turn",
    )(own, up, down, up_rest, down_rest)


def near_kernel(near_ref, before_ref, modes_ref, after_ref, basis_ref, out_ref, turned_ref, ext_ref):
    r = pl.program_id(0)
    halo, panels = before_ref.shape[0], modes_ref.shape[0]
    rank = basis_ref.shape[0]

    @pl.when(r == 0)
    def _():
        ext_ref[:halo] = before_ref[...]
        ext_ref[halo : halo + panels] = modes_ref[...]
        ext_ref[halo + panels :] = after_ref[...]

    window = ext_ref[pl.ds(pl.multiple_of(r * CS, CS), NEAR * CS), :]
    out_ref[...] = jnp.dot(near_ref[...], window, preferred_element_type=jnp.float32)
    have = lax.broadcasted_iota(jnp.int32, (rank, rank), 0)
    want = lax.broadcasted_iota(jnp.int32, (rank, rank), 1)
    order = jnp.where(want < rank // 2, 2 * want, 2 * want - rank + 1)
    select = jnp.where(order == have, 1.0, 0.0).astype(jnp.bfloat16)
    turned_ref[...] = lax.dot_general(
        basis_ref[...], select, (((0,), (0,)), ((), ())), preferred_element_type=jnp.float32
    ).astype(jnp.bfloat16)


def near_field(near_blocks, before, modes, after, row_basis):
    panels, band = near_blocks.shape
    cols = modes.shape[1]
    halo = before.shape[0]
    rank = row_basis.shape[0]
    return pl.pallas_call(
        near_kernel,
        grid=(panels // CS,),
        in_specs=[pl.BlockSpec((CS, band), lambda r: (r, 0))]
        + [whole()] * 3
        + [pl.BlockSpec((rank, CS), lambda r: (0, r))],
        out_specs=[
            pl.BlockSpec((CS, cols), lambda r: (r, 0)),
            pl.BlockSpec((CS, rank), lambda r: (r, 0)),
        ],
        out_shape=[
            jax.ShapeDtypeStruct((panels, cols), jnp.float32),
            jax.ShapeDtypeStruct((panels, rank), jnp.bfloat16),
        ],
        scratch_shapes=[VMEM((panels + 2 * halo, cols), jnp.bfloat16)],
        compiler_params=pltpu.CompilerParams(vmem_limit_bytes=32 * MIB),
        cost_estimate=pl.CostEstimate(
            flops=2 * panels * band * cols, bytes_accessed=2 * MIB, transcendentals=0
        ),
        name="near_field",
    )(near_blocks, before, modes, after, row_basis)


EXPAND = 2


def expand_kernel(near_ref, basis_ref, *refs):
    sides, out_ref = (refs[:5], refs[5:10]), refs[10]
    places = [(side, at) for side in sides for at in range(side[0].shape[0])]
    width = sides[0][3].shape[2]
    step = pl.program_id(0)
    for group in range(len(places) // EXPAND):

        @pl.when(step == group)
        def _():
            for i in range(EXPAND):
                rows = pl.ds(i * CS, CS)
                (own_ref, up_ref, down_ref, up_rest_ref, down_rest_ref), at = places[group * EXPAND + i]
                part = own_ref.shape[0]
                own = own_ref[at]
                first = own[:, :width] + f32(down_ref[at]) + f32(up_rest_ref[at])
                second = own[:, width:] + f32(up_ref[part + at]) + f32(down_rest_ref[at])
                for far, cols in ((first, pl.ds(0, width)), (second, pl.ds(width, width))):
                    value = jnp.dot(basis_ref[rows, :], far.astype(jnp.bfloat16), preferred_element_type=jnp.float32)
                    out_ref[rows, cols] = (near_ref[rows, cols] + value).astype(jnp.bfloat16)


def expand(near, basis, left, right):
    panels, cols = near.shape
    rank = basis.shape[1]
    return pl.pallas_call(
        expand_kernel,
        grid=(panels // CS // EXPAND,),
        in_specs=[
            pl.BlockSpec((EXPAND * CS, cols), lambda r: (r, 0)),
            pl.BlockSpec((EXPAND * CS, rank), lambda r: (r, 0)),
        ]
        + [pl.BlockSpec(v.shape, lambda r: (0, 0, 0)) for v in (*left, *right)],
        out_specs=pl.BlockSpec((EXPAND * CS, cols), lambda r: (r, 0)),
        out_shape=jax.ShapeDtypeStruct((panels, cols), jnp.bfloat16),
        compiler_params=pltpu.CompilerParams(vmem_limit_bytes=24 * MIB),
        cost_estimate=pl.CostEstimate(
            flops=2 * panels * rank * cols, bytes_accessed=7 * MIB, transcendentals=0
        ),
        name="expand",
    )(near, basis, *left, *right)


def per_device(modes, col_basis, row_basis, near_blocks, block_rows, block_owner, block_slot, cores):
    row_devices, col_devices = lax.axis_size("crow"), lax.axis_size("ccol")
    devices = row_devices * col_devices
    cluster_count = modes.shape[0] // CS
    rank = col_basis.shape[0]
    blocks = cores.shape[0]
    slots = CAP * row_devices

    compressed, low, high = compress(col_basis, modes)
    gathered = lax.all_gather(compressed, "crow", axis=0, tiled=True)

    lines = rank * rank // 128
    sent = dispatch(
        block_rows, block_owner[:, 0], block_slot, cores.reshape(blocks, lines, 128),
        col_devices, slots, cluster_count,
    )
    sent = lax.all_to_all(sent, "ccol", split_axis=0, concat_axis=0, tiled=True)

    up = [(i, i + 1) for i in range(devices - 1)]
    down = [(j, i) for i, j in up]
    before = lax.ppermute(high, ("crow", "ccol"), up)
    after = lax.ppermute(low, ("crow", "ccol"), down)
    left, right = far_field(gathered, sent, slots, lines, col_devices * cluster_count)
    for along_x in (True, False):
        left_up, left_down = both_ways(left[0], left[1], along_x)
        right_up, right_down = both_ways(right[0], right[1], not along_x)
        if along_x:
            (before, after), _ = lax.optimization_barrier(((before, after), left[0]))
            near, basis = near_field(near_blocks, before, modes, after, row_basis)
            (left_up, left_down), _ = lax.optimization_barrier(((left_up, left_down), near))
        left_rest = passed_on(left[2], left[3], left_up, left_down)
        right_rest = passed_on(right[2], right[3], right_up, right_down)
        left_rest = both_ways(*left_rest, along_x)
        right_rest = both_ways(*right_rest, not along_x)
        left = (left[4], left_up, left_down, *left_rest)
        right = (right[4], right_up, right_down, *right_rest)
        if along_x:
            left, right = turn(*left), turn(*right)
    return expand(near, basis, left, right)


def solution(mesh):
    both = ("crow", "ccol")
    in_specs = (
        P(both, None),
        P(None, both),
        P(None, both),
        P(both, None),
        P(both),
        P(both, None),
        P(both),
        P(both, None),
    )
    return jax.shard_map(
        per_device, mesh=mesh, in_specs=in_specs, out_specs=P(both, None), check_vma=False
    )
```

```python
import functools

import jax
import jax.numpy as jnp
from jax import lax
from jax.experimental import pallas as pl
from jax.experimental.pallas import tpu as pltpu
from jax.sharding import PartitionSpec as P

CS = 256
NH = 4
NEAR = 9
CAP = 2
MIB = 1 << 20
VMEM = pltpu.VMEM
SMEM = pltpu.SMEM


def whole(space=VMEM):
    return pl.BlockSpec(memory_space=space)


COMPRESS = 4


def compress_kernel(basis_ref, modes_ref, out_ref, low_ref, high_ref):
    step = pl.program_id(0)

    @pl.when(step == 0)
    def _():
        low_ref[...] = modes_ref[: NH * CS, :]

    @pl.when(step == pl.num_programs(0) - 1)
    def _():
        high_ref[...] = modes_ref[(COMPRESS - NH) * CS :, :]

    for i in range(COMPRESS):
        out_ref[i] = jnp.dot(
            basis_ref[:, i * CS : (i + 1) * CS],
            modes_ref[i * CS : (i + 1) * CS, :],
            preferred_element_type=jnp.float32,
        ).astype(jnp.bfloat16)


def compress(col_basis, modes):
    rank, panels = col_basis.shape
    cols = modes.shape[1]
    count = panels // CS
    return pl.pallas_call(
        compress_kernel,
        grid=(count // COMPRESS,),
        in_specs=[
            pl.BlockSpec((rank, COMPRESS * CS), lambda r: (0, r)),
            pl.BlockSpec((COMPRESS * CS, cols), lambda r: (r, 0)),
        ],
        out_specs=[
            pl.BlockSpec((COMPRESS, rank, cols), lambda r: (r, 0, 0)),
            pl.BlockSpec((NH * CS, cols), lambda r: (0, 0)),
            pl.BlockSpec((NH * CS, cols), lambda r: (0, 0)),
        ],
        out_shape=[
            jax.ShapeDtypeStruct((count, rank, cols), jnp.bfloat16),
            jax.ShapeDtypeStruct((NH * CS, cols), jnp.bfloat16),
            jax.ShapeDtypeStruct((NH * CS, cols), jnp.bfloat16),
        ],
        compiler_params=pltpu.CompilerParams(vmem_limit_bytes=58 * MIB),
        cost_estimate=pl.CostEstimate(
            flops=2 * rank * panels * cols, bytes_accessed=3 * MIB, transcendentals=0
        ),
        name="compress",
    )(col_basis, modes)


def dispatch_kernel(
    cols, slots, cl_dev, rows_ref, owners_ref, slot_ref, cores_ref, out_ref, count_ref, meta_ref
):
    blocks, rows, _ = cores_ref.shape
    out_ref[...] = jnp.zeros_like(out_ref)
    meta_ref[...] = jnp.zeros_like(meta_ref)
    lane = lax.broadcasted_iota(jnp.int32, (1, 128), 1)
    for j in range(cols):
        count_ref[j] = 0

    def place(b, carry):
        owner = owners_ref[b]
        column = owner & (cols - 1)
        at = count_ref[column]
        count_ref[column] = at + 1
        out_ref[column, pl.ds(pl.multiple_of(at * rows, rows), rows), :] = cores_ref[b]
        cluster = (owner >> (cols.bit_length() - 1)) * cl_dev + slot_ref[b]
        entry = (
            jnp.where(lane == at, cluster, 0)
            + jnp.where(lane == slots + at, rows_ref[b], 0)
            + jnp.where(lane == 2 * slots, 1, 0)
        )
        meta_ref[pl.ds(column, 1), :] += entry.astype(jnp.float32)
        return carry

    lax.fori_loop(0, blocks, place, 0, unroll=8)
    for j in range(cols):
        out_ref[j, slots * rows :, :] = jnp.broadcast_to(
            meta_ref[j : j + 1, :], (16, 128)
        ).astype(jnp.bfloat16)


def dispatch(block_rows, owners, block_slot, cores, cols, slots, cl_dev):
    blocks, rows, _ = cores.shape
    return pl.pallas_call(
        functools.partial(dispatch_kernel, cols, slots, cl_dev),
        in_specs=[whole(SMEM), whole(SMEM), whole(SMEM), whole()],
        out_specs=whole(),
        out_shape=jax.ShapeDtypeStruct((cols, slots * rows + 16, 128), jnp.bfloat16),
        scratch_shapes=[SMEM((cols,), jnp.int32), VMEM((cols, 128), jnp.float32)],
        compiler_params=pltpu.CompilerParams(vmem_limit_bytes=16 * MIB),
        cost_estimate=pl.CostEstimate(flops=4 * MIB, bytes_accessed=3 * MIB, transcendentals=0),
        name="dispatch",
    )(block_rows, owners, block_slot, cores)


UNROLL = 32
X_ROWS = 4


def far_kernel(slots, rows, comp_ref, sent_ref, *refs):
    outs, (acc_ref, meta_ref, smem_ref, list_ref, sem) = (refs[:5], refs[5:10]), refs[10:]
    sources = sent_ref.shape[0]
    group_rows = acc_ref.shape[0]
    part = group_rows // 4
    row_part = part // 4
    me = lax.axis_index("ccol")
    here_x, here_z = me // 4, me % 4

    meta = sent_ref[:, slots * rows : slots * rows + 16, :].astype(jnp.float32)
    meta = jnp.max(meta, axis=1).astype(jnp.int32)
    lane = lax.broadcasted_iota(jnp.int32, meta.shape, 1)
    row = pltpu.roll(meta, 128 - slots, axis=1) & (group_rows - 1)
    to_x = (row // part - here_x) & 3
    to_z = (row // row_part - here_z) & 3
    rest = row & (row_part - 1)
    z_rows = row_part - X_ROWS
    x_place = (to_x * 4 + to_z) * X_ROWS + rest
    z_place = 16 * X_ROWS + (to_z * 4 + to_x) * z_rows + rest - X_ROWS
    filed = jnp.where(rest < X_ROWS, x_place, z_place)
    place = lax.broadcasted_iota(jnp.int32, meta.shape, 0) * slots + lane
    words = (place << 14) + (meta << 7) + filed
    meta_ref[...] = jnp.where(lane < slots, words, meta)
    copy = pltpu.make_async_copy(meta_ref, smem_ref, sem)
    copy.start()
    acc_ref[...] = jnp.zeros_like(acc_ref)
    copy.wait()

    total = 0
    for i in range(sources):
        for p in range(slots):
            list_ref[total + p] = smem_ref[i, p]
        total = total + smem_ref[i, 2 * slots]
    for i in range(UNROLL):
        list_ref[total + i] = 0

    def group(g, carry):
        for i in range(UNROLL):
            at = g * UNROLL + i
            entry = list_ref[at]
            place = entry >> 14
            core = sent_ref[place // slots, pl.ds(pl.multiple_of((place % slots) * rows, rows), rows), :]
            core = jnp.where(at < total, core, jnp.zeros_like(core))
            half = core.shape[1] // 2
            core = jnp.concatenate([core[:, :half], core[:, half:]], axis=0)
            comp = comp_ref[(entry >> 7) & 127]
            acc_ref[entry & 127] += jnp.dot(core, comp, preferred_element_type=jnp.float32)
        return carry

    lax.fori_loop(0, (total + UNROLL - 1) // UNROLL, group, 0)
    begin = 0
    for up_ref, down_ref, next_ref, last_ref, own_ref in outs:
        part = own_ref.shape[0]
        half = part // 2
        own, following, far, last, begin = (begin + i * part for i in range(5))
        own_ref[...] = acc_ref[own : own + part]
        next_ref[...] = acc_ref[following : following + half]
        up_ref[half:] = acc_ref[following + half : following + part].astype(jnp.bfloat16)
        up_ref[:half] = acc_ref[far : far + half].astype(jnp.bfloat16)
        down_ref[half:] = acc_ref[far + half : far + part].astype(jnp.bfloat16)
        down_ref[:half] = acc_ref[last : last + half].astype(jnp.bfloat16)
        last_ref[...] = acc_ref[last + half : last + part]


def far_field(comp, sent, slots, rows, group_rows):
    _, rank, cols = comp.shape
    sources = sent.shape[0]
    x_part = X_ROWS * 4
    kinds = [
        (n, kind)
        for part in (x_part, group_rows // 4 - x_part)
        for n, kind in (
            (part, jnp.bfloat16),
            (part, jnp.bfloat16),
            (part // 2, jnp.float32),
            (part // 2, jnp.float32),
            (part, jnp.float32),
        )
    ]
    parts = pl.pallas_call(
        functools.partial(far_kernel, slots, rows),
        in_specs=[whole()] * 2,
        out_specs=[whole()] * len(kinds),
        out_shape=[jax.ShapeDtypeStruct((n, rank, cols), kind) for n, kind in kinds],
        scratch_shapes=[
            VMEM((group_rows, rank, cols), jnp.float32),
            VMEM((sources, 128), jnp.int32),
            SMEM((sources, 128), jnp.int32),
            SMEM((sources * slots + UNROLL + slots,), jnp.int32),
            pltpu.SemaphoreType.DMA,
        ],
        compiler_params=pltpu.CompilerParams(vmem_limit_bytes=40 * MIB),
        cost_estimate=pl.CostEstimate(
            flops=2 * 128 * rank * rank * cols * 8, bytes_accessed=24 * MIB, transcendentals=0
        ),
        name="far_field",
    )(comp, sent)
    return parts[:5], parts[5:]


def ring(axis_is_x, step):
    def to(i):
        x, z = i // 4, i % 4
        return ((x + step) % 4) * 4 + z if axis_is_x else x * 4 + (z + step) % 4

    return [(i, to(i)) for i in range(16)]


def f32(value):
    return value.astype(jnp.float32)


def both_ways(up, down, along_x):
    return lax.ppermute(up, "ccol", ring(along_x, 1)), lax.ppermute(down, "ccol", ring(along_x, -1))


SMALL = pl.CostEstimate(flops=0, bytes_accessed=0, transcendentals=0)


def pass_kernel(following_ref, last_ref, up_ref, down_ref, up_out_ref, down_out_ref):
    half = following_ref.shape[0]
    up_out_ref[...] = (following_ref[...] + f32(up_ref[:half])).astype(jnp.bfloat16)
    down_out_ref[...] = (last_ref[...] + f32(down_ref[half:])).astype(jnp.bfloat16)


def passed_on(following, last, up, down):
    shape = jax.ShapeDtypeStruct(following.shape, jnp.bfloat16)
    return pl.pallas_call(
        pass_kernel,
        in_specs=[whole()] * 4,
        out_specs=[whole()] * 2,
        out_shape=[shape] * 2,
        compiler_params=pltpu.CompilerParams(vmem_limit_bytes=24 * MIB),
        cost_estimate=SMALL,
        name="passed_on",
    )(following, last, up, down)


def turn_kernel(own_ref, up_in_ref, down_in_ref, up_rest_ref, down_rest_ref, up_ref, down_ref, next_ref, last_ref, here_ref):
    part, _, width = next_ref.shape
    half = up_rest_ref.shape[0]

    def total(kind):
        at = kind * part
        rows = pl.ds(at, part)
        if at < half:
            return own_ref[rows] + f32(down_in_ref[rows]) + f32(up_rest_ref[rows])
        return own_ref[rows] + f32(up_in_ref[rows]) + f32(down_rest_ref[pl.ds(at - half, part)])

    here_ref[...] = total(0)
    following, far, last = total(1), total(2), total(3)
    next_ref[...] = following[:, :, :width]
    up_ref[part:] = following[:, :, width:].astype(jnp.bfloat16)
    up_ref[:part] = far[:, :, :width].astype(jnp.bfloat16)
    down_ref[part:] = far[:, :, width:].astype(jnp.bfloat16)
    down_ref[:part] = last[:, :, :width].astype(jnp.bfloat16)
    last_ref[...] = last[:, :, width:]


def turn(own, up, down, up_rest, down_rest):
    rows, rank, cols = own.shape
    part, width = rows // 4, cols // 2
    kinds = [
        (2 * part, width, jnp.bfloat16),
        (2 * part, width, jnp.bfloat16),
        (part, width, jnp.float32),
        (part, width, jnp.float32),
        (part, cols, jnp.float32),
    ]
    return pl.pallas_call(
        turn_kernel,
        in_specs=[whole()] * 5,
        out_specs=[whole()] * 5,
        out_shape=[jax.ShapeDtypeStruct((n, rank, w), kind) for n, w, kind in kinds],
        compiler_params=pltpu.CompilerParams(vmem_limit_bytes=24 * MIB),
        cost_estimate=SMALL,
        name="turn",
    )(own, up, down, up_rest, down_rest)


def near_kernel(near_ref, before_ref, modes_ref, after_ref, basis_ref, out_ref, turned_ref, ext_ref):
    r = pl.program_id(0)
    halo, panels = before_ref.shape[0], modes_ref.shape[0]
    rank = basis_ref.shape[0]

    @pl.when(r == 0)
    def _():
        ext_ref[:halo] = before_ref[...]
        ext_ref[halo : halo + panels] = modes_ref[...]
        ext_ref[halo + panels :] = after_ref[...]

    window = ext_ref[pl.ds(pl.multiple_of(r * CS, CS), NEAR * CS), :]
    out_ref[...] = jnp.dot(near_ref[...], window, preferred_element_type=jnp.float32)
    have = lax.broadcasted_iota(jnp.int32, (rank, rank), 0)
    want = lax.broadcasted_iota(jnp.int32, (rank, rank), 1)
    order = jnp.where(want < rank // 2, 2 * want, 2 * want - rank + 1)
    select = jnp.where(order == have, 1.0, 0.0).astype(jnp.bfloat16)
    turned_ref[...] = lax.dot_general(
        basis_ref[...], select, (((0,), (0,)), ((), ())), preferred_element_type=jnp.float32
    ).astype(jnp.bfloat16)


def near_field(near_blocks, before, modes, after, row_basis):
    panels, band = near_blocks.shape
    cols = modes.shape[1]
    halo = before.shape[0]
    rank = row_basis.shape[0]
    return pl.pallas_call(
        near_kernel,
        grid=(panels // CS,),
        in_specs=[pl.BlockSpec((CS, band), lambda r: (r, 0))]
        + [whole()] * 3
        + [pl.BlockSpec((rank, CS), lambda r: (0, r))],
        out_specs=[
            pl.BlockSpec((CS, cols), lambda r: (r, 0)),
            pl.BlockSpec((CS, rank), lambda r: (r, 0)),
        ],
        out_shape=[
            jax.ShapeDtypeStruct((panels, cols), jnp.float32),
            jax.ShapeDtypeStruct((panels, rank), jnp.bfloat16),
        ],
        scratch_shapes=[VMEM((panels + 2 * halo, cols), jnp.bfloat16)],
        compiler_params=pltpu.CompilerParams(vmem_limit_bytes=26 * MIB),
        cost_estimate=pl.CostEstimate(
            flops=2 * panels * band * cols, bytes_accessed=2 * MIB, transcendentals=0
        ),
        name="near_field",
    )(near_blocks, before, modes, after, row_basis)


EXPAND = 2


def expand_kernel(near_ref, basis_ref, *refs):
    sides, out_ref = (refs[:5], refs[5:10]), refs[10]
    places = [(side, at) for side in sides for at in range(side[0].shape[0])]
    width = sides[0][3].shape[2]
    step = pl.program_id(0)
    for group in range(len(places) // EXPAND):

        @pl.when(step == group)
        def _():
            for i in range(EXPAND):
                rows = pl.ds(i * CS, CS)
                (own_ref, up_ref, down_ref, up_rest_ref, down_rest_ref), at = places[group * EXPAND + i]
                part = own_ref.shape[0]
                own = own_ref[at]
                first = own[:, :width] + f32(down_ref[at]) + f32(up_rest_ref[at])
                second = own[:, width:] + f32(up_ref[part + at]) + f32(down_rest_ref[at])
                for far, cols in ((first, pl.ds(0, width)), (second, pl.ds(width, width))):
                    value = jnp.dot(basis_ref[rows, :], far.astype(jnp.bfloat16), preferred_element_type=jnp.float32)
                    out_ref[rows, cols] = (near_ref[rows, cols] + value).astype(jnp.bfloat16)


def expand(near, basis, left, right):
    panels, cols = near.shape
    rank = basis.shape[1]
    return pl.pallas_call(
        expand_kernel,
        grid=(panels // CS // EXPAND,),
        in_specs=[
            pl.BlockSpec((EXPAND * CS, cols), lambda r: (r, 0)),
            pl.BlockSpec((EXPAND * CS, rank), lambda r: (r, 0)),
        ]
        + [pl.BlockSpec(v.shape, lambda r: (0, 0, 0)) for v in (*left, *right)],
        out_specs=pl.BlockSpec((EXPAND * CS, cols), lambda r: (r, 0)),
        out_shape=jax.ShapeDtypeStruct((panels, cols), jnp.bfloat16),
        compiler_params=pltpu.CompilerParams(vmem_limit_bytes=24 * MIB),
        cost_estimate=pl.CostEstimate(
            flops=2 * panels * rank * cols, bytes_accessed=7 * MIB, transcendentals=0
        ),
        name="expand",
    )(near, basis, *left, *right)


def per_device(modes, col_basis, row_basis, near_blocks, block_rows, block_owner, block_slot, cores):
    row_devices, col_devices = lax.axis_size("crow"), lax.axis_size("ccol")
    devices = row_devices * col_devices
    cluster_count = modes.shape[0] // CS
    rank = col_basis.shape[0]
    blocks = cores.shape[0]
    slots = CAP * row_devices

    compressed, low, high = compress(col_basis, modes)
    gathered = lax.all_gather(compressed, "crow", axis=0, tiled=True)

    lines = rank * rank // 128
    sent = dispatch(
        block_rows, block_owner[:, 0], block_slot, cores.reshape(blocks, lines, 128),
        col_devices, slots, cluster_count,
    )
    sent = lax.all_to_all(sent, "ccol", split_axis=0, concat_axis=0, tiled=True)

    up = [(i, i + 1) for i in range(devices - 1)]
    down = [(j, i) for i, j in up]
    before = lax.ppermute(high, ("crow", "ccol"), up)
    after = lax.ppermute(low, ("crow", "ccol"), down)
    left, right = far_field(gathered, sent, slots, lines, col_devices * cluster_count)
    for along_x in (True, False):
        left_up, left_down = both_ways(left[0], left[1], along_x)
        right_up, right_down = both_ways(right[0], right[1], not along_x)
        if along_x:
            (before, after), _ = lax.optimization_barrier(((before, after), left[0]))
            near, basis = near_field(near_blocks, before, modes, after, row_basis)
            (left_up, left_down), _ = lax.optimization_barrier(((left_up, left_down), near))
        left_rest = passed_on(left[2], left[3], left_up, left_down)
        right_rest = passed_on(right[2], right[3], right_up, right_down)
        left_rest = both_ways(*left_rest, along_x)
        right_rest = both_ways(*right_rest, not along_x)
        left = (left[4], left_up, left_down, *left_rest)
        right = (right[4], right_up, right_down, *right_rest)
        if along_x:
            left, right = turn(*left), turn(*right)
    return expand(near, basis, left, right)


def solution(mesh):
    both = ("crow", "ccol")
    in_specs = (
        P(both, None),
        P(None, both),
        P(None, both),
        P(both, None),
        P(both),
        P(both, None),
        P(both),
        P(both, None),
    )
    return jax.shard_map(
        per_device, mesh=mesh, in_specs=in_specs, out_specs=P(both, None), check_vma=False
    )
```

```python
import functools

import jax
import jax.numpy as jnp
from jax import lax
from jax.experimental import pallas as pl
from jax.experimental.pallas import tpu as pltpu
from jax.sharding import PartitionSpec as P

CS = 256
NH = 4
NEAR = 9
CAP = 2
MIB = 1 << 20
VMEM = pltpu.VMEM
SMEM = pltpu.SMEM


def whole(space=VMEM):
    return pl.BlockSpec(memory_space=space)


COMPRESS = 4


def compress_kernel(basis_ref, modes_ref, out_ref, low_ref, high_ref):
    step = pl.program_id(0)

    @pl.when(step == 0)
    def _():
        low_ref[...] = modes_ref[: NH * CS, :]

    @pl.when(step == pl.num_programs(0) - 1)
    def _():
        high_ref[...] = modes_ref[(COMPRESS - NH) * CS :, :]

    for i in range(COMPRESS):
        out_ref[i] = jnp.dot(
            basis_ref[:, i * CS : (i + 1) * CS],
            modes_ref[i * CS : (i + 1) * CS, :],
            preferred_element_type=jnp.float32,
        ).astype(jnp.bfloat16)


def compress(col_basis, modes):
    rank, panels = col_basis.shape
    cols = modes.shape[1]
    count = panels // CS
    return pl.pallas_call(
        compress_kernel,
        grid=(count // COMPRESS,),
        in_specs=[
            pl.BlockSpec((rank, COMPRESS * CS), lambda r: (0, r)),
            pl.BlockSpec((COMPRESS * CS, cols), lambda r: (r, 0)),
        ],
        out_specs=[
            pl.BlockSpec((COMPRESS, rank, cols), lambda r: (r, 0, 0)),
            pl.BlockSpec((NH * CS, cols), lambda r: (0, 0)),
            pl.BlockSpec((NH * CS, cols), lambda r: (0, 0)),
        ],
        out_shape=[
            jax.ShapeDtypeStruct((count, rank, cols), jnp.bfloat16),
            jax.ShapeDtypeStruct((NH * CS, cols), jnp.bfloat16),
            jax.ShapeDtypeStruct((NH * CS, cols), jnp.bfloat16),
        ],
        compiler_params=pltpu.CompilerParams(vmem_limit_bytes=58 * MIB),
        cost_estimate=pl.CostEstimate(
            flops=2 * rank * panels * cols, bytes_accessed=3 * MIB, transcendentals=0
        ),
        name="compress",
    )(col_basis, modes)


def dispatch_kernel(
    cols, slots, cl_dev, rows_ref, owners_ref, slot_ref, cores_ref, out_ref, count_ref, meta_ref
):
    blocks, rows, _ = cores_ref.shape
    out_ref[...] = jnp.zeros_like(out_ref)
    meta_ref[...] = jnp.zeros_like(meta_ref)
    lane = lax.broadcasted_iota(jnp.int32, (1, 128), 1)
    for j in range(cols):
        count_ref[j] = 0

    def place(b, carry):
        owner = owners_ref[b]
        column = owner & (cols - 1)
        at = count_ref[column]
        count_ref[column] = at + 1
        out_ref[column, pl.ds(pl.multiple_of(at * rows, rows), rows), :] = cores_ref[b]
        cluster = (owner >> (cols.bit_length() - 1)) * cl_dev + slot_ref[b]
        entry = (
            jnp.where(lane == at, cluster, 0)
            + jnp.where(lane == slots + at, rows_ref[b], 0)
            + jnp.where(lane == 2 * slots, 1, 0)
        )
        meta_ref[pl.ds(column, 1), :] += entry.astype(jnp.float32)
        return carry

    lax.fori_loop(0, blocks, place, 0, unroll=8)
    for j in range(cols):
        out_ref[j, slots * rows :, :] = jnp.broadcast_to(
            meta_ref[j : j + 1, :], (16, 128)
        ).astype(jnp.bfloat16)


def dispatch(block_rows, owners, block_slot, cores, cols, slots, cl_dev):
    blocks, rows, _ = cores.shape
    return pl.pallas_call(
        functools.partial(dispatch_kernel, cols, slots, cl_dev),
        in_specs=[whole(SMEM), whole(SMEM), whole(SMEM), whole()],
        out_specs=whole(),
        out_shape=jax.ShapeDtypeStruct((cols, slots * rows + 16, 128), jnp.bfloat16),
        scratch_shapes=[SMEM((cols,), jnp.int32), VMEM((cols, 128), jnp.float32)],
        compiler_params=pltpu.CompilerParams(vmem_limit_bytes=16 * MIB),
        cost_estimate=pl.CostEstimate(flops=4 * MIB, bytes_accessed=3 * MIB, transcendentals=0),
        name="dispatch",
    )(block_rows, owners, block_slot, cores)


UNROLL = 32
X_ROWS = 4


def far_kernel(slots, rows, gathered_ref, sent_ref, *refs):
    outs, (comp_ref, acc_ref, meta_ref, smem_ref, list_ref, sem, comp_sem) = (refs[:5], refs[5:10]), refs[10:]
    comp_copy = pltpu.make_async_copy(gathered_ref, comp_ref, comp_sem)
    comp_copy.start()
    sources = sent_ref.shape[0]
    group_rows = acc_ref.shape[0]
    part = group_rows // 4
    row_part = part // 4
    me = lax.axis_index("ccol")
    here_x, here_z = me // 4, me % 4

    meta = sent_ref[:, slots * rows : slots * rows + 16, :].astype(jnp.float32)
    meta = jnp.max(meta, axis=1).astype(jnp.int32)
    lane = lax.broadcasted_iota(jnp.int32, meta.shape, 1)
    row = pltpu.roll(meta, 128 - slots, axis=1) & (group_rows - 1)
    to_x = (row // part - here_x) & 3
    to_z = (row // row_part - here_z) & 3
    rest = row & (row_part - 1)
    z_rows = row_part - X_ROWS
    x_place = (to_x * 4 + to_z) * X_ROWS + rest
    z_place = 16 * X_ROWS + (to_z * 4 + to_x) * z_rows + rest - X_ROWS
    filed = jnp.where(rest < X_ROWS, x_place, z_place)
    place = lax.broadcasted_iota(jnp.int32, meta.shape, 0) * slots + lane
    words = (place << 14) + (meta << 7) + filed
    meta_ref[...] = jnp.where(lane < slots, words, meta)
    copy = pltpu.make_async_copy(meta_ref, smem_ref, sem)
    copy.start()
    acc_ref[...] = jnp.zeros_like(acc_ref)
    copy.wait()

    total = 0
    for i in range(sources):
        for p in range(slots):
            list_ref[total + p] = smem_ref[i, p]
        total = total + smem_ref[i, 2 * slots]
    for i in range(UNROLL):
        list_ref[total + i] = 0

    comp_copy.wait()

    def group(g, carry):
        for i in range(UNROLL):
            at = g * UNROLL + i
            entry = list_ref[at]
            place = entry >> 14
            core = sent_ref[place // slots, pl.ds(pl.multiple_of((place % slots) * rows, rows), rows), :]
            core = jnp.where(at < total, core, jnp.zeros_like(core))
            half = core.shape[1] // 2
            core = jnp.concatenate([core[:, :half], core[:, half:]], axis=0)
            comp = comp_ref[(entry >> 7) & 127]
            acc_ref[entry & 127] += jnp.dot(core, comp, preferred_element_type=jnp.float32)
        return carry

    lax.fori_loop(0, (total + UNROLL - 1) // UNROLL, group, 0)
    begin = 0
    for up_ref, down_ref, next_ref, last_ref, own_ref in outs:
        part = own_ref.shape[0]
        half = part // 2
        own, following, far, last, begin = (begin + i * part for i in range(5))
        own_ref[...] = acc_ref[own : own + part]
        next_ref[...] = acc_ref[following : following + half]
        up_ref[half:] = acc_ref[following + half : following + part].astype(jnp.bfloat16)
        up_ref[:half] = acc_ref[far : far + half].astype(jnp.bfloat16)
        down_ref[half:] = acc_ref[far + half : far + part].astype(jnp.bfloat16)
        down_ref[:half] = acc_ref[last : last + half].astype(jnp.bfloat16)
        last_ref[...] = acc_ref[last + half : last + part]


def far_field(comp, sent, slots, rows, group_rows):
    _, rank, cols = comp.shape
    sources = sent.shape[0]
    x_part = X_ROWS * 4
    kinds = [
        (n, kind)
        for part in (x_part, group_rows // 4 - x_part)
        for n, kind in (
            (part, jnp.bfloat16),
            (part, jnp.bfloat16),
            (part // 2, jnp.float32),
            (part // 2, jnp.float32),
            (part, jnp.float32),
        )
    ]
    parts = pl.pallas_call(
        functools.partial(far_kernel, slots, rows),
        in_specs=[whole(pl.ANY), whole()],
        out_specs=[whole()] * len(kinds),
        out_shape=[jax.ShapeDtypeStruct((n, rank, cols), kind) for n, kind in kinds],
        scratch_shapes=[
            VMEM(comp.shape, comp.dtype),
            VMEM((group_rows, rank, cols), jnp.float32),
            VMEM((sources, 128), jnp.int32),
            SMEM((sources, 128), jnp.int32),
            SMEM((sources * slots + UNROLL + slots,), jnp.int32),
            pltpu.SemaphoreType.DMA,
            pltpu.SemaphoreType.DMA,
        ],
        compiler_params=pltpu.CompilerParams(vmem_limit_bytes=40 * MIB),
        cost_estimate=pl.CostEstimate(
            flops=2 * 128 * rank * rank * cols * 8, bytes_accessed=24 * MIB, transcendentals=0
        ),
        name="far_field",
    )(comp, sent)
    return parts[:5], parts[5:]


def ring(axis_is_x, step):
    def to(i):
        x, z = i // 4, i % 4
        return ((x + step) % 4) * 4 + z if axis_is_x else x * 4 + (z + step) % 4

    return [(i, to(i)) for i in range(16)]


def f32(value):
    return value.astype(jnp.float32)


def both_ways(up, down, along_x):
    return lax.ppermute(up, "ccol", ring(along_x, 1)), lax.ppermute(down, "ccol", ring(along_x, -1))


SMALL = pl.CostEstimate(flops=0, bytes_accessed=0, transcendentals=0)


def pass_kernel(following_ref, last_ref, up_ref, down_ref, up_out_ref, down_out_ref):
    half = following_ref.shape[0]
    up_out_ref[...] = (following_ref[...] + f32(up_ref[:half])).astype(jnp.bfloat16)
    down_out_ref[...] = (last_ref[...] + f32(down_ref[half:])).astype(jnp.bfloat16)


def passed_on(following, last, up, down):
    shape = jax.ShapeDtypeStruct(following.shape, jnp.bfloat16)
    return pl.pallas_call(
        pass_kernel,
        in_specs=[whole()] * 4,
        out_specs=[whole()] * 2,
        out_shape=[shape] * 2,
        compiler_params=pltpu.CompilerParams(vmem_limit_bytes=24 * MIB),
        cost_estimate=SMALL,
        name="passed_on",
    )(following, last, up, down)


def turn_kernel(own_ref, up_in_ref, down_in_ref, up_rest_ref, down_rest_ref, up_ref, down_ref, next_ref, last_ref, here_ref):
    part, _, width = next_ref.shape
    half = up_rest_ref.shape[0]

    def total(kind):
        at = kind * part
        rows = pl.ds(at, part)
        if at < half:
            return own_ref[rows] + f32(down_in_ref[rows]) + f32(up_rest_ref[rows])
        return own_ref[rows] + f32(up_in_ref[rows]) + f32(down_rest_ref[pl.ds(at - half, part)])

    here_ref[...] = total(0)
    following, far, last = total(1), total(2), total(3)
    next_ref[...] = following[:, :, :width]
    up_ref[part:] = following[:, :, width:].astype(jnp.bfloat16)
    up_ref[:part] = far[:, :, :width].astype(jnp.bfloat16)
    down_ref[part:] = far[:, :, width:].astype(jnp.bfloat16)
    down_ref[:part] = last[:, :, :width].astype(jnp.bfloat16)
    last_ref[...] = last[:, :, width:]


def turn(own, up, down, up_rest, down_rest):
    rows, rank, cols = own.shape
    part, width = rows // 4, cols // 2
    kinds = [
        (2 * part, width, jnp.bfloat16),
        (2 * part, width, jnp.bfloat16),
        (part, width, jnp.float32),
        (part, width, jnp.float32),
        (part, cols, jnp.float32),
    ]
    return pl.pallas_call(
        turn_kernel,
        in_specs=[whole()] * 5,
        out_specs=[whole()] * 5,
        out_shape=[jax.ShapeDtypeStruct((n, rank, w), kind) for n, w, kind in kinds],
        compiler_params=pltpu.CompilerParams(vmem_limit_bytes=24 * MIB),
        cost_estimate=SMALL,
        name="turn",
    )(own, up, down, up_rest, down_rest)


def near_kernel(near_ref, before_ref, modes_ref, after_ref, basis_ref, out_ref, turned_ref, ext_ref):
    r = pl.program_id(0)
    halo, panels = before_ref.shape[0], modes_ref.shape[0]
    rank = basis_ref.shape[0]

    @pl.when(r == 0)
    def _():
        ext_ref[:halo] = before_ref[...]
        ext_ref[halo : halo + panels] = modes_ref[...]
        ext_ref[halo + panels :] = after_ref[...]

    window = ext_ref[pl.ds(pl.multiple_of(r * CS, CS), NEAR * CS), :]
    out_ref[...] = jnp.dot(near_ref[...], window, preferred_element_type=jnp.float32)
    have = lax.broadcasted_iota(jnp.int32, (rank, rank), 0)
    want = lax.broadcasted_iota(jnp.int32, (rank, rank), 1)
    order = jnp.where(want < rank // 2, 2 * want, 2 * want - rank + 1)
    select = jnp.where(order == have, 1.0, 0.0).astype(jnp.bfloat16)
    turned_ref[...] = lax.dot_general(
        basis_ref[...], select, (((0,), (0,)), ((), ())), preferred_element_type=jnp.float32
    ).astype(jnp.bfloat16)


def near_field(near_blocks, before, modes, after, row_basis):
    panels, band = near_blocks.shape
    cols = modes.shape[1]
    halo = before.shape[0]
    rank = row_basis.shape[0]
    return pl.pallas_call(
        near_kernel,
        grid=(panels // CS,),
        in_specs=[pl.BlockSpec((CS, band), lambda r: (r, 0))]
        + [whole()] * 3
        + [pl.BlockSpec((rank, CS), lambda r: (0, r))],
        out_specs=[
            pl.BlockSpec((CS, cols), lambda r: (r, 0)),
            pl.BlockSpec((CS, rank), lambda r: (r, 0)),
        ],
        out_shape=[
            jax.ShapeDtypeStruct((panels, cols), jnp.float32),
            jax.ShapeDtypeStruct((panels, rank), jnp.bfloat16),
        ],
        scratch_shapes=[VMEM((panels + 2 * halo, cols), jnp.bfloat16)],
        compiler_params=pltpu.CompilerParams(vmem_limit_bytes=26 * MIB),
        cost_estimate=pl.CostEstimate(
            flops=2 * panels * band * cols, bytes_accessed=2 * MIB, transcendentals=0
        ),
        name="near_field",
    )(near_blocks, before, modes, after, row_basis)


EXPAND = 2


def expand_kernel(near_ref, basis_ref, *refs):
    sides, out_ref = (refs[:5], refs[5:10]), refs[10]
    places = [(side, at) for side in sides for at in range(side[0].shape[0])]
    width = sides[0][3].shape[2]
    step = pl.program_id(0)
    for group in range(len(places) // EXPAND):

        @pl.when(step == group)
        def _():
            for i in range(EXPAND):
                rows = pl.ds(i * CS, CS)
                (own_ref, up_ref, down_ref, up_rest_ref, down_rest_ref), at = places[group * EXPAND + i]
                part = own_ref.shape[0]
                own = own_ref[at]
                first = own[:, :width] + f32(down_ref[at]) + f32(up_rest_ref[at])
                second = own[:, width:] + f32(up_ref[part + at]) + f32(down_rest_ref[at])
                for far, cols in ((first, pl.ds(0, width)), (second, pl.ds(width, width))):
                    value = jnp.dot(basis_ref[rows, :], far.astype(jnp.bfloat16), preferred_element_type=jnp.float32)
                    out_ref[rows, cols] = (near_ref[rows, cols] + value).astype(jnp.bfloat16)


def expand(near, basis, left, right):
    panels, cols = near.shape
    rank = basis.shape[1]
    return pl.pallas_call(
        expand_kernel,
        grid=(panels // CS // EXPAND,),
        in_specs=[
            pl.BlockSpec((EXPAND * CS, cols), lambda r: (r, 0)),
            pl.BlockSpec((EXPAND * CS, rank), lambda r: (r, 0)),
        ]
        + [pl.BlockSpec(v.shape, lambda r: (0, 0, 0)) for v in (*left, *right)],
        out_specs=pl.BlockSpec((EXPAND * CS, cols), lambda r: (r, 0)),
        out_shape=jax.ShapeDtypeStruct((panels, cols), jnp.bfloat16),
        compiler_params=pltpu.CompilerParams(vmem_limit_bytes=24 * MIB),
        cost_estimate=pl.CostEstimate(
            flops=2 * panels * rank * cols, bytes_accessed=7 * MIB, transcendentals=0
        ),
        name="expand",
    )(near, basis, *left, *right)


def per_device(modes, col_basis, row_basis, near_blocks, block_rows, block_owner, block_slot, cores):
    row_devices, col_devices = lax.axis_size("crow"), lax.axis_size("ccol")
    devices = row_devices * col_devices
    cluster_count = modes.shape[0] // CS
    rank = col_basis.shape[0]
    blocks = cores.shape[0]
    slots = CAP * row_devices

    compressed, low, high = compress(col_basis, modes)
    gathered = lax.all_gather(compressed, "crow", axis=0, tiled=True)

    lines = rank * rank // 128
    sent = dispatch(
        block_rows, block_owner[:, 0], block_slot, cores.reshape(blocks, lines, 128),
        col_devices, slots, cluster_count,
    )
    sent = lax.all_to_all(sent, "ccol", split_axis=0, concat_axis=0, tiled=True)

    up = [(i, i + 1) for i in range(devices - 1)]
    down = [(j, i) for i, j in up]
    before = lax.ppermute(high, ("crow", "ccol"), up)
    after = lax.ppermute(low, ("crow", "ccol"), down)
    left, right = far_field(gathered, sent, slots, lines, col_devices * cluster_count)
    for along_x in (True, False):
        left_up, left_down = both_ways(left[0], left[1], along_x)
        right_up, right_down = both_ways(right[0], right[1], not along_x)
        if along_x:
            (before, after), _ = lax.optimization_barrier(((before, after), left[0]))
            near, basis = near_field(near_blocks, before, modes, after, row_basis)
            (left_up, left_down), _ = lax.optimization_barrier(((left_up, left_down), near))
        left_rest = passed_on(left[2], left[3], left_up, left_down)
        right_rest = passed_on(right[2], right[3], right_up, right_down)
        left_rest = both_ways(*left_rest, along_x)
        right_rest = both_ways(*right_rest, not along_x)
        left = (left[4], left_up, left_down, *left_rest)
        right = (right[4], right_up, right_down, *right_rest)
        if along_x:
            left, right = turn(*left), turn(*right)
    return expand(near, basis, left, right)


def solution(mesh):
    both = ("crow", "ccol")
    in_specs = (
        P(both, None),
        P(None, both),
        P(None, both),
        P(both, None),
        P(both),
        P(both, None),
        P(both),
        P(both, None),
    )
    return jax.shard_map(
        per_device, mesh=mesh, in_specs=in_specs, out_specs=P(both, None), check_vma=False
    )
```
